512 devices in a mesh: gx: 32 (over z_lo, x), gy: 16 (over y, z_hi, core).
Axes of the slice: x: 4, y: 4, z: 16 (z_hi: 2, z_lo: 8; z = z_hi * 8 + z_lo), core: 2. Of those that a mesh axis runs over, the one named last changes fastest.
Arguments:
- volts_start: float32 [8, 512, 16384], P(None, 'gx', 'gy'), may hold values from 0.55 to 1, as said below
- seg_cond: float32 [8, 512, 16384], P(None, 'gx', 'gy'), may hold values from 0.5 to 2
- via_cond: float32 [7, 512, 16384], P(None, 'gx', 'gy'), may hold values from 1 to 4
- via_mask: int32 [7, 512, 16384], P(None, 'gx', 'gy'), may hold values 0 or 1
- pad_mask: int32 [512, 16384], P('gx', 'gy'), may hold values 0 or 1
- load_current: float32 [512, 16384], P('gx', 'gy'), may hold values from 0 to 2.7, as said below
- stress_start: float32 [8, 512, 16384], P(None, 'gx', 'gy'), may hold values from -6 to 6
- mobility: float32 [8, 512, 16384], P(None, 'gx', 'gy'), may hold values from 0.1 to 0.45
- blocked: int32 [8, 512, 16384], P(None, 'gx', 'gy'), may hold values 0 or 1
- layer_dirs: int32 [8], replicated, may hold values from 0 to 1, as said below
Outputs:
- volts_final: float32 [8, 512, 16384], P(None, 'gx', 'gy')
- stress_final: float32 [8, 512, 16384], P(None, 'gx', 'gy')
- resid_rms: float32 [], replicated
The draws below stay inside these ranges and needn't reach their ends.
Inputs may be any that keep to these rules, and one draw needn't show every extreme that they name: `volts_start`: node voltages near the supply level, one sign. `load_current`: positive load currents. `layer_dirs`: exactly 4 layers run along x and the others along y.
All inputs are finite; a program needn't handle non-finite values. No bound on the sum of `via_mask` or of `pad_mask` or of `blocked` on one device may be relied on, other than what follows from the above.
Results may differ from the reference program's by a relative error of at most 0.00002.
Values sent between devices are 32-bit elements; how exact they have to be, the bound alone decides.
No kernel may reach another device: no remote copies, remote signals or barrier semaphores. Data moves between devices by JAX's collectives and lax.ppermute only.
A program may use at most 64 MiB of HBM per device.

```python
import math
import jax
import jax.numpy as jnp

L = 8
SWEEPS = 3
STEPS = 3
NX = 512
NY = 16384


def ramp_pair(strong):
    span_x = jnp.arange(NX, dtype=jnp.float32) / max(NX - 1, 1)
    span_y = jnp.arange(NY, dtype=jnp.float32) / max(NY - 1, 1)
    return (1.0 + strong * span_x)[:, None] * (1.0 + 2.0 * span_y)[None, :]


def draw_volts_start(key, part):
    noise = jax.random.uniform(jax.random.fold_in(key, 11), (L, NX, NY), jnp.float32)
    scale = 0.05 * ramp_pair(2.0)
    return 1.0 - scale[None] * noise


def draw_load_current(key, part):
    noise = jax.random.uniform(jax.random.fold_in(key, 13), (NX, NY), jnp.float32, 0.5, 1.5)
    return 0.1 * ramp_pair(2.0) * noise


def draw_layer_dirs(key, part):
    order = jax.random.permutation(jax.random.fold_in(key, 7), L)
    return (order % 2).astype(jnp.int32)


def with_ends(result, own_key, least, high):
    index_at = [jax.random.randint(jax.random.fold_in(own_key, axis), (), 0, length) for axis, length in enumerate(result.shape)]
    main_axis = result.shape.index(max(result.shape))
    beside = index_at[:main_axis] + [(index_at[main_axis] + 1) % result.shape[main_axis]] + index_at[main_axis + 1:]
    return result.at[tuple(index_at)].set(least).at[tuple(beside)].set(high)


def levels(rng, dims, shards, low, top_value):
    factor_of = 1.0
    for dim, blocks in shards:
        draws = jax.random.uniform(jax.random.fold_in(jax.random.fold_in(rng, 6), dim), (blocks,), jnp.float32, low / len(shards), top_value / len(shards))
        factor_of = factor_of * jnp.repeat(jnp.exp(draws), dims[dim] // blocks).reshape((-1,) + (1,) * (len(dims) - 1 - dim))
    return factor_of


def bell_draw(rng, dims, scale, bound, cuts=(), kind=jnp.bfloat16):
    array = scale * jax.random.normal(rng, dims, jnp.float32)
    if cuts:
        array = array * levels(rng, dims, cuts, -0.22, 0.18)
    return jnp.clip(array, -bound, bound).astype(kind)


def setup_inputs(seed: int = 0) -> dict:
    keys = jax.random.split(jax.random.key(seed), 11)
    return {
        "volts_start": draw_volts_start(jax.random.fold_in(keys[10], 71), 0),
        "seg_cond": jnp.clip(jnp.exp(math.log(2.0) - 1.3862944 * jax.random.uniform(keys[1], (L, NX, NY), jnp.float32) ** levels(keys[1], (L, NX, NY), ((1, 32), (2, 16)), -0.2, 0.2)), 0.5, 2.0),
        "via_cond": jnp.clip(jnp.exp(math.log(4.0) - 1.3862944 * jax.random.uniform(keys[2], (L - 1, NX, NY), jnp.float32) ** levels(keys[2], (L - 1, NX, NY), ((1, 32), (2, 16)), -0.2, 0.2)), 1.0, 4.0),
        "via_mask": with_ends((jax.random.randint(keys[3], (L - 1, NX, NY), 0, 4) < 3).astype(jnp.int32), jax.random.fold_in(keys[3], 1), 0, 1),
        "pad_mask": with_ends((jax.random.randint(keys[4], (NX, NY), 0, 8) < 1).astype(jnp.int32), jax.random.fold_in(keys[4], 1), 0, 1),
        "load_current": draw_load_current(jax.random.fold_in(keys[10], 71), 0),
        "stress_start": bell_draw(keys[6], (L, NX, NY), 1.0, 6.0, ((1, 32), (2, 16)), jnp.float32),
        "mobility": jnp.clip(jnp.exp(math.log(0.45) - 1.50407736 * jax.random.uniform(keys[7], (L, NX, NY), jnp.float32) ** levels(keys[7], (L, NX, NY), ((1, 32), (2, 16)), -0.2, 0.2)), 0.1, 0.45),
        "blocked": with_ends((jax.random.randint(keys[8], (L, NX, NY), 0, 4) < 1).astype(jnp.int32), jax.random.fold_in(keys[8], 1), 0, 1),
        "layer_dirs": draw_layer_dirs(jax.random.fold_in(keys[10], 71), 0),
    }


damping = 0.8
pad_conductance = 4.0
supply_volts = 1.0
wind_factor = 4.0

def prior_x(field):
    return jnp.pad(field, ((0, 0), (1, 0), (0, 0)))[:, :-1, :]

def prior_y(field):
    return jnp.pad(field, ((0, 0), (0, 0), (1, 0)))[:, :, :-1]

def layer_pair(field):
    zero = jnp.zeros_like(field[:1])
    return (jnp.concatenate([zero, field[:-1]], 0), jnp.concatenate([field[1:], zero], 0))

def inflow(volts, cond_xr, cond_yr, via_below, via_above, sources):
    padded = jnp.pad(volts, ((0, 0), (1, 1), (1, 1)))
    below, above = layer_pair(volts)
    total = prior_x(cond_xr) * padded[:, :-2, 1:-1] + cond_xr * padded[:, 2:, 1:-1]
    total = total + prior_y(cond_yr) * padded[:, 1:-1, :-2] + cond_yr * padded[:, 1:-1, 2:]
    return total + via_below * below + via_above * above + sources

def reference(volts_start, seg_cond, via_cond, via_mask, pad_mask, load_current, stress_start, mobility, blocked, layer_dirs):
    layers = seg_cond.shape[0]
    along_y = layer_dirs.astype(jnp.float32)[:, None, None]
    along_x = 1.0 - along_y
    inner_x = (jnp.arange(NX) < NX - 1).astype(jnp.float32)[None, :, None]
    inner_y = (jnp.arange(NY) < NY - 1).astype(jnp.float32)[None, None, :]
    cond_xr = seg_cond * along_x * inner_x
    cond_yr = seg_cond * along_y * inner_y
    via_both = via_cond * via_mask.astype(jnp.float32)
    zero = jnp.zeros((1, NX, NY), jnp.float32)
    via_below = jnp.concatenate([zero, via_both], 0)
    via_above = jnp.concatenate([via_both, zero], 0)
    pads = pad_conductance * pad_mask.astype(jnp.float32)
    level = jnp.arange(layers)[:, None, None]
    top_cond = jnp.where(level == layers - 1, pads[None], jnp.float32(0.0))
    sources = top_cond * supply_volts - jnp.where(level == 0, load_current[None], jnp.float32(0.0))
    diagonal = prior_x(cond_xr) + cond_xr + prior_y(cond_yr) + cond_yr + via_below + via_above + top_cond
    volts = volts_start
    for sweep in range(SWEEPS):
        volts = (1.0 - damping) * volts + damping * inflow(volts, cond_xr, cond_yr, via_below, via_above, sources) / diagonal
    resid = inflow(volts, cond_xr, cond_yr, via_below, via_above, sources) - diagonal * volts
    resid_rms = jnp.sqrt(jnp.sum(resid * resid) / (layers * NX * NY))
    padded = jnp.pad(volts, ((0, 0), (1, 1), (1, 1)))
    current_x = cond_xr * (volts - padded[:, 2:, 1:-1])
    current_y = cond_yr * (volts - padded[:, 1:-1, 2:])
    open_seg = 1.0 - blocked.astype(jnp.float32)
    mobile_x = mobility * open_seg * along_x * inner_x
    mobile_y = mobility * open_seg * along_y * inner_y
    wind_x = mobile_x * wind_factor * current_x
    wind_y = mobile_y * wind_factor * current_y
    drift = wind_x - prior_x(wind_x) + wind_y - prior_y(wind_y)
    mobile_xl = prior_x(mobile_x)
    mobile_yl = prior_y(mobile_y)
    stress = stress_start
    for step in range(STEPS):
        padded = jnp.pad(stress, ((0, 0), (1, 1), (1, 1)))
        stress = stress + mobile_x * (padded[:, 2:, 1:-1] - stress) - mobile_xl * (stress - padded[:, :-2, 1:-1]) + mobile_y * (padded[:, 1:-1, 2:] - stress) - mobile_yl * (stress - padded[:, 1:-1, :-2]) + drift
    return (volts, stress, resid_rms)
```

```python
import jax
import jax.numpy as jnp
from jax import lax
from jax.sharding import PartitionSpec as P

SWEEPS = 3
STEPS = 3


X = ("z_lo", "x")
Y = ("y", "z_hi", "core")


def sum_all(value):
    for axes in (("z_hi", "z_lo"), ("x", "y", "core")):
        count = lax.axis_size(axes)
        held = jnp.broadcast_to(value, (count, 8, 128))
        value = jnp.sum(lax.all_to_all(held, axes, 0, 0)[:, 0, 0])
    return value


damping = 0.8
pad_conductance = 4.0
supply_volts = 1.0
wind_factor = 4.0


def from_behind(value, axis, steps):
    count = lax.axis_size(axis)
    initial, last = (max(0, -steps), min(count, count - steps))
    return lax.ppermute(value, axis, [(source, source + steps) for source in range(initial, last)])


def with_halo(cells, sides, width):
    for axis, dim in sides:
        count = lax.axis_size(axis)
        ends = count - 1
        head = lax.slice_in_dim(cells, 0, width, axis=dim)
        tail = lax.slice_in_dim(cells, cells.shape[dim] - width, cells.shape[dim], axis=dim)
        cells = jnp.concatenate(
            [
                lax.ppermute(tail, axis, [(i, (i + 1) % count) for i in range(ends)]),
                cells,
                lax.ppermute(head, axis, [((i + 1) % count, i) for i in range(ends)]),
            ],
            axis=dim,
        )
    return cells


def layer_pair(field):
    zero = jnp.zeros_like(field[:1])
    return (jnp.concatenate([zero, field[:-1]], 0), jnp.concatenate([field[1:], zero], 0))


def lateral_both(padded, cond_xl, cond_xr, cond_yl, cond_yr):
    total = cond_xl * padded[:, :-2, 1:-1] + cond_xr * padded[:, 2:, 1:-1]
    return total + cond_yl * padded[:, 1:-1, :-2] + cond_yr * padded[:, 1:-1, 2:]


def finish(lateral, volts, via_below, via_above, sources):
    below, above = layer_pair(volts)
    return lateral + via_below * below + via_above * above + sources


def body(
    volts_start,
    seg_cond,
    via_cond,
    via_mask,
    pad_mask,
    load_current,
    stress_start,
    mobility,
    blocked,
    layer_dirs,
):
    layers, rows_x, rows_y = seg_cond.shape
    total_x = rows_x * lax.axis_size(X)
    total_y = rows_y * lax.axis_size(Y)
    index_x = lax.axis_index(X) * rows_x + jnp.arange(rows_x, dtype=jnp.int32)
    index_y = lax.axis_index(Y) * rows_y + jnp.arange(rows_y, dtype=jnp.int32)
    inner_x = (index_x < total_x - 1).astype(jnp.float32)[None, :, None]
    inner_y = (index_y < total_y - 1).astype(jnp.float32)[None, None, :]
    along_y = layer_dirs.astype(jnp.float32)[:, None, None]
    along_x = 1.0 - along_y
    cond_xr = seg_cond * along_x * inner_x
    cond_yr = seg_cond * along_y * inner_y
    via_both = via_cond * via_mask.astype(jnp.float32)
    zero = jnp.zeros((1, rows_x, rows_y), jnp.float32)
    via_below = jnp.concatenate([zero, via_both], 0)
    via_above = jnp.concatenate([via_both, zero], 0)
    pads = pad_conductance * pad_mask.astype(jnp.float32)
    level = jnp.arange(layers)[:, None, None]
    top_cond = jnp.where(level == layers - 1, pads[None], jnp.float32(0.0))
    sources = top_cond * supply_volts - jnp.where(level == 0, load_current[None], jnp.float32(0.0))
    open_seg = 1.0 - blocked.astype(jnp.float32)
    mobile_x = mobility * open_seg * along_x * inner_x
    mobile_y = mobility * open_seg * along_y * inner_y
    edge_x = from_behind(jnp.stack([cond_xr[:, -1:, :], mobile_x[:, -1:, :]]), X, 1)
    edge_y = from_behind(jnp.stack([cond_yr[:, :, -1:], mobile_y[:, :, -1:]]), Y, 1)
    cond_xl = jnp.concatenate([edge_x[0], cond_xr[:, :-1, :]], 1)
    mobile_xl = jnp.concatenate([edge_x[1], mobile_x[:, :-1, :]], 1)
    cond_yl = jnp.concatenate([edge_y[0], cond_yr[:, :, :-1]], 2)
    mobile_yl = jnp.concatenate([edge_y[1], mobile_y[:, :, :-1]], 2)
    diagonal = cond_xl + cond_xr + cond_yl + cond_yr + via_below + via_above + top_cond
    volts = volts_start
    for sweep in range(SWEEPS):
        padded = with_halo(volts, ((X, 1), (Y, 2)), 1)
        lateral = lateral_both(padded, cond_xl, cond_xr, cond_yl, cond_yr)
        volts = (1.0 - damping) * volts + damping * finish(
            lateral, volts, via_below, via_above, sources
        ) / diagonal
    padded = with_halo(volts, ((X, 1), (Y, 2)), 1)
    lateral = lateral_both(padded, cond_xl, cond_xr, cond_yl, cond_yr)
    current_x = cond_xr * (volts - padded[:, 2:, 1:-1])
    current_y = cond_yr * (volts - padded[:, 1:-1, 2:])
    current_xl = cond_xl * (padded[:, :-2, 1:-1] - volts)
    current_yl = cond_yl * (padded[:, 1:-1, :-2] - volts)
    resid = finish(lateral, volts, via_below, via_above, sources) - diagonal * volts
    squared = sum_all(jnp.sum(resid * resid))
    resid_rms = jnp.sqrt(squared / (layers * total_x * total_y))
    wind_x = mobile_x * wind_factor * current_x
    wind_y = mobile_y * wind_factor * current_y
    wind_xl = mobile_xl * wind_factor * current_xl
    wind_yl = mobile_yl * wind_factor * current_yl
    drift = wind_x - wind_xl + wind_y - wind_yl
    stress = stress_start
    for step in range(STEPS):
        side = with_halo(stress, ((X, 1), (Y, 2)), 1)
        stress = (
            stress
            + mobile_x * (side[:, 2:, 1:-1] - stress)
            - mobile_xl * (stress - side[:, :-2, 1:-1])
            + mobile_y * (side[:, 1:-1, 2:] - stress)
            - mobile_yl * (stress - side[:, 1:-1, :-2])
            + drift
        )
    return (volts, stress, resid_rms)


def solution(mesh):
    in_specs = (
        P(None, X, Y),
        P(None, X, Y),
        P(None, X, Y),
        P(None, X, Y),
        P(X, Y),
        P(X, Y),
        P(None, X, Y),
        P(None, X, Y),
        P(None, X, Y),
        P(),
    )
    out_specs = (P(None, X, Y), P(None, X, Y), P())
    fine = jax.sharding.Mesh(mesh.devices.reshape(8, 4, 4, 2, 2), X + Y)
    return jax.shard_map(body, mesh=fine, in_specs=in_specs, out_specs=out_specs, check_vma=False)
```

```python
import functools

import jax
import jax.numpy as jnp
from jax import lax
from jax.experimental import pallas as pl
from jax.experimental.pallas import tpu as pltpu
from jax.sharding import PartitionSpec as P

SWEEPS = 3
STEPS = 3
LAYERS = 8
ROWS = 16
LANES = 128
REACH = 8
OWN = 16
STRIP = REACH + OWN
SLOTS = 4
EDGE = 12
FIELDS = 6

damping = 0.8
pad_conductance = 4.0
supply_volts = 1.0
wind_factor = 4.0

X = ("z_lo", "x")
Y = ("y", "z_hi", "core")


def iota(shape, dim):
    return lax.broadcasted_iota(jnp.int32, shape, dim)


def lane_dirs(dirs, shape):
    layer = iota(shape, len(shape) - 1) // ROWS
    found = jnp.zeros(shape, jnp.int32)
    for l in range(LAYERS):
        found = jnp.where(layer == l, dirs[l], found)
    return found == 1


def slots_of(dirs):
    slot, count = [], jnp.int32(0)
    for l in range(LAYERS):
        slot.append(count)
        count = count + (1 - dirs[l])
    return slot


def pack_columns(total_x, total_y, width, dirs, pos, *refs):
    ins, (own_ref, a_ref, b_ref) = refs[:18], refs[18:]
    gx, gy = pos[0], pos[1]
    col = iota((1, 1, LANES), 2)

    def pick(i):
        first, last = ins[2 * i][...], ins[2 * i + 1][...]
        return jnp.where(col.reshape((1,) * (first.ndim - 1) + (LANES,)) < LANES // 2, first, last)

    volts, seg, via_cond, via_mask, pad, load, stress, mob, blk = (pick(i) for i in range(9))
    none = jnp.zeros((1, ROWS, LANES), jnp.float32)
    via = jnp.concatenate([via_cond * via_mask.astype(jnp.float32), none], 0)
    ends = jnp.concatenate(
        [load[None]] + [none] * (LAYERS - 2) + [pad_conductance * pad.astype(jnp.float32)[None]], 0
    )
    mobile = mob * (1.0 - blk.astype(jnp.float32))
    shape = (OWN, LANES)
    along_y = lane_dirs(dirs, shape)
    x = gx * ROWS + iota(shape, 1) % ROWS
    even = gy % 2 == 0
    for f, field in enumerate((volts, seg, via, ends, stress, mobile)):
        turned = field.reshape(LANES, LANES).T
        pieces = []
        for side, start in enumerate((0, LANES - OWN)):
            piece = turned[start : start + OWN]
            if f in (1, 5):
                y = gy * width + (0 if side == 0 else width - OWN) + iota(shape, 0)
                inner = jnp.where(along_y, y, x) < jnp.where(along_y, total_y - 1, total_x - 1)
                piece = jnp.where(inner, piece, 0.0)
            own_ref[side, f] = piece
            pieces.append(piece)
        left, right = pieces[0][:REACH], pieces[1][OWN - REACH :]
        a_ref[f] = jnp.where(even, right, left)
        b_ref[f] = jnp.where(even, left, right)


def inner_x(gx, total_x, shape):
    return (gx * ROWS + iota(shape, 0) < total_x - 1).astype(jnp.float32)


def inner_y(gy, total_y, shape):
    return (gy * shape[1] + iota(shape, 1) < total_y - 1).astype(jnp.float32)


def pack_rows(total_x, dirs, pos, volts, seg, via_cond, via_mask, pad, load, stress, mob, blk, a_ref, b_ref):
    gx = pos[0]
    even = gx % 2 == 0
    width = volts.shape[2]
    inner = inner_x(gx, total_x, (ROWS, width))
    slot = slots_of(dirs)
    for l in range(LAYERS):

        @pl.when(dirs[l] == 0)
        def _(l=l):
            cond = seg[l] * inner
            mobile = mob[l] * (1.0 - blk[l].astype(jnp.float32)) * inner
            held, s = volts[l], stress[l]
            out = []
            for edge in (ROWS - 1, 0):
                here = slice(edge, edge + 1)
                num = jnp.zeros((1, width), jnp.float32)
                diag = cond[here]
                if edge:
                    num = cond[edge - 1 : edge] * held[edge - 1 : edge]
                    diag = diag + cond[edge - 1 : edge]
                else:
                    num = cond[here] * held[1:2]
                if l > 0:
                    below = via_cond[l - 1, here] * via_mask[l - 1, here].astype(jnp.float32)
                    num, diag = num + below * volts[l - 1, here], diag + below
                if l < LAYERS - 1:
                    above = via_cond[l, here] * via_mask[l, here].astype(jnp.float32)
                    num, diag = num + above * volts[l + 1, here], diag + above
                if l == LAYERS - 1:
                    top = pad_conductance * pad[here].astype(jnp.float32)
                    num, diag = num + top * supply_volts, diag + top
                if l == 0:
                    num = num - load[here]
                three = slice(ROWS - 3, ROWS) if edge else slice(0, 3)
                out.append([cond[three], mobile[three], s[three], held[here], num, diag])
            base = slot[l] * EDGE
            at = 0
            for right, left in zip(*out):
                for i in range(right.shape[0]):
                    row = slice(i, i + 1)
                    a_ref[pl.ds(base + at, 1), :] = jnp.where(even, right[row], left[row])
                    b_ref[pl.ds(base + at, 1), :] = jnp.where(even, left[row], right[row])
                    at += 1


def guarded(diag):
    return jnp.where(diag == 0.0, 1.0, diag)


def blocks(width, along_y):
    if along_y:
        return [(slice(r, r + 8), slice(0, width)) for r in range(0, ROWS, 8)]
    step = min(512, width)
    return [(slice(0, ROWS), slice(c, c + step)) for c in range(0, width, step)]


def rest_of(l, at, v, via, pad, load):
    total = None
    if l > 0:
        total = via[(l - 1, *at)] * v[(l - 1, *at)]
    if l < LAYERS - 1:
        above = via[(l, *at)] * v[(l + 1, *at)]
        total = above if total is None else total + above
    if l == LAYERS - 1:
        total = total + pad_conductance * supply_volts * pad[at].astype(jnp.float32)
    if l == 0:
        total = total - load[at]
    return total


def shifted(value, dim, before, after):
    n = value.shape[dim]
    prior, later = pltpu.roll(value, 1, dim), pltpu.roll(value, n - 1, dim)
    if dim == 0:
        row = iota(value.shape, 0)
        if before is not None:
            prior = jnp.where(row == 0, before, prior)
            later = jnp.where(row == n - 1, after, later)
    return prior, later


def strip_pair(recv_a, recv_b, even, own, f):
    from_right = jnp.where(even, recv_a[f], recv_b[f])
    from_left = jnp.where(even, recv_b[f], recv_a[f])
    return (
        jnp.concatenate([from_left, own[0, f]], 0),
        jnp.concatenate([own[1, f], from_right], 0),
    )


def early_sweeps(
    total_x, total_y, dirs, pos, volts, seg, via_cond, via_mask, pad, load, gxa, gxb, own, gya, gyb,
    cond_o, prior_o, via_o, diag_o, volts_o, edges_o, a_ref, b_ref, rate, one, two, halo, to_right, to_left,
):
    gx, gy = pos[0], pos[1]
    even = gx % 2 == 0
    width = volts.shape[2]
    slot = slots_of(dirs)

    def near(right, row, lanes=slice(None)):
        a, b = gxa[pl.ds(row, 1), lanes], gxb[pl.ds(row, 1), lanes]
        return jnp.where(even, a, b) if right else jnp.where(even, b, a)

    for l in range(LAYERS):
        if l < LAYERS - 1:
            via_o[l] = via_cond[l] * via_mask[l].astype(jnp.float32)

        @pl.when(dirs[l] == 0)
        def _(l=l):
            cond = seg[l] * inner_x(gx, total_x, (ROWS, width))
            cond_o[l] = cond
            prior_o[l] = shifted(cond, 0, near(False, slot[l] * EDGE + 2), 0.0)[0]

        @pl.when(dirs[l] == 1)
        def _(l=l):
            cond = seg[l] * inner_y(gy, total_y, (ROWS, width))
            cond_o[l] = cond
            prior_o[l] = pltpu.roll(cond, 1, 1)

    for l in range(LAYERS):
        diag = cond_o[l] + prior_o[l]
        if l > 0:
            diag = diag + via_o[l - 1]
        if l < LAYERS - 1:
            diag = diag + via_o[l]
        else:
            diag = diag + pad_conductance * pad[...].astype(jnp.float32)
        diag_o[l] = diag
        rate[l] = damping / guarded(diag)

    for sweep, (old, new) in enumerate(((volts, one), (one, two), (two, volts_o))):
        for l in range(LAYERS):

            @pl.when(dirs[l] == 0)
            def _(l=l):
                base = slot[l] * EDGE
                for at in blocks(width, False):
                    lanes = at[1]
                    v = old[(l, *at)]
                    if sweep == 0:
                        before, after = near(False, base + 9, lanes), near(True, base + 9, lanes)
                        cond_left = near(False, base + 2, lanes)
                        last = cond_o[l, ROWS - 1 :, lanes]
                        halo[0, pl.ds(slot[l], 1), lanes] = (1.0 - damping) * before + damping * (
                            near(False, base + 10, lanes) + cond_left * v[:1]
                        ) / guarded(near(False, base + 11, lanes))
                        halo[1, pl.ds(slot[l], 1), lanes] = (1.0 - damping) * after + damping * (
                            near(True, base + 10, lanes) + last * v[ROWS - 1 :]
                        ) / guarded(near(True, base + 11, lanes) + last)
                    elif sweep == 1:
                        before, after = halo[0, pl.ds(slot[l], 1), lanes], halo[1, pl.ds(slot[l], 1), lanes]
                    else:
                        before = after = 0.0
                    prior, later = shifted(v, 0, before, after)
                    num = prior_o[(l, *at)] * prior + cond_o[(l, *at)] * later + rest_of(l, at, old, via_o, pad, load)
                    result = (1.0 - damping) * v + rate[(l, *at)] * num
                    new[(l, *at)] = result
                    if sweep == 2:
                        edges_o[0, l : l + 1, lanes] = v[:1]
                        edges_o[1, l : l + 1, lanes] = v[ROWS - 1 :]
                        send = slot[l] * 4
                        for ref, e, d in ((to_right, ROWS - 1, -1), (to_left, 0, 1)):
                            ref[pl.ds(send, 1), lanes] = v[e : e + 1]
                            ref[pl.ds(send + 1, 1), lanes] = num[e : e + 1]
                            ref[pl.ds(send + 2, 1), lanes] = result[e + d : e + d + 1]
                            ref[pl.ds(send + 3, 1), lanes] = result[e + 2 * d : e + 2 * d + 1]

            @pl.when(dirs[l] == 1)
            def _(l=l):
                for at in blocks(width, True):
                    v = old[(l, *at)]
                    prior, later = shifted(v, 1, None, None)
                    num = prior_o[(l, *at)] * prior + cond_o[(l, *at)] * later + rest_of(l, at, old, via_o, pad, load)
                    new[(l, *at)] = (1.0 - damping) * v + rate[(l, *at)] * num
                    if sweep == 2:
                        edges_o[:, l : l + 1, :] = jnp.zeros((2, 1, width), jnp.float32)

    x = iota((STRIP, LANES), 1) % ROWS
    for f in range(FIELDS):
        left, right = strip_pair(gya, gyb, gy % 2 == 0, own, f)
        right_going = jnp.where(x >= 8, left, pltpu.roll(right, LANES - 8, 1))
        left_going = jnp.where(x < 8, left, pltpu.roll(right, 8, 1))
        a_ref[f * STRIP : (f + 1) * STRIP] = jnp.where(even, right_going, left_going)
        b_ref[f * STRIP : (f + 1) * STRIP] = jnp.where(even, left_going, right_going)
    for j in range(width // LANES):
        start = FIELDS * STRIP + j * ROWS
        lanes = slice(j * LANES, (j + 1) * LANES)
        a_ref[start : start + ROWS] = jnp.where(even, to_right[:, lanes], to_left[:, lanes])
        b_ref[start : start + ROWS] = jnp.where(even, to_left[:, lanes], to_right[:, lanes])


def strips(dirs, even_y, even_x, own, gya, gyb, ma, mb):
    tall = (2 * STRIP, LANES)
    x = iota((STRIP, LANES), 1) % ROWS
    own_f, far_f = [], []
    for f in range(FIELDS):
        left, right = strip_pair(gya, gyb, even_y, own, f)
        a, b = ma[f * STRIP : (f + 1) * STRIP], mb[f * STRIP : (f + 1) * STRIP]
        from_right, from_left = jnp.where(even_x, a, b), jnp.where(even_x, b, a)
        far_left = jnp.where(x >= 8, from_left, from_right)
        far_right = jnp.where(x >= 8, pltpu.roll(from_left, 8, 1), pltpu.roll(from_right, LANES - 8, 1))
        own_f.append(jnp.concatenate([left, right], 0))
        far_f.append(jnp.concatenate([far_left, far_right], 0))
    fields = list(zip(own_f, far_f))
    along_y = lane_dirs(dirs, tall)
    layer, x = iota(tall, 1) // ROWS, iota(tall, 1) % ROWS

    def later(pair):
        o, h = pair
        out = []
        for this, other in ((o, h), (h, o)):
            across = jnp.where(x == ROWS - 1, pltpu.roll(other, ROWS - 1, 1), pltpu.roll(this, LANES - 1, 1))
            out.append(jnp.where(along_y, pltpu.roll(this, tall[0] - 1, 0), across))
        return out

    def prior(pair):
        o, h = pair
        out = []
        for this, other in ((o, h), (h, o)):
            across = jnp.where(x == 0, pltpu.roll(other, LANES - ROWS + 1, 1), pltpu.roll(this, 1, 1))
            out.append(jnp.where(along_y, pltpu.roll(this, 1, 0), across))
        return out

    volts, cond, via, ends, stress, mobile = fields
    via_below = [pltpu.roll(a, ROWS, 1) for a in via]
    top = [jnp.where(layer == LAYERS - 1, a, 0.0) for a in ends]
    load = [jnp.where(layer == 0, a, 0.0) for a in ends]
    cond_prior = prior(cond)
    diag = [guarded(p + c + vb + va + t) for p, c, vb, va, t in zip(cond_prior, cond, via_below, via, top)]
    rate = [damping / d for d in diag]

    def inflow(v):
        before, after = prior(v), later(v)
        return [
            cond_prior[i] * before[i]
            + cond[i] * after[i]
            + via_below[i] * pltpu.roll(v[i], ROWS, 1)
            + via[i] * pltpu.roll(v[i], LANES - ROWS, 1)
            + top[i] * supply_volts
            - load[i]
            for i in range(2)
        ]

    for _ in range(SWEEPS):
        num = inflow(volts)
        volts = [(1.0 - damping) * v + r * n for v, r, n in zip(volts, rate, num)]
    resid = inflow(volts)[0] - diag[0] * volts[0]
    sub = iota(tall, 0)
    inside = ((sub >= REACH) & (sub < 2 * REACH)) | ((sub >= STRIP + REACH) & (sub < STRIP + 2 * REACH))
    squares = jnp.where(inside, resid * resid, 0.0)
    after = later(volts)
    wind = [mobile[i] * wind_factor * (cond[i] * (volts[i] - after[i])) for i in range(2)]
    for _ in range(STEPS):
        after = later(stress)
        flux = [mobile[i] * (after[i] - stress[i]) + wind[i] for i in range(2)]
        back = prior(flux)
        stress = [stress[i] + flux[i] - back[i] for i in range(2)]

    def turned(value):
        middle = jnp.zeros((LANES - 2 * OWN, LANES), jnp.float32)
        whole = jnp.concatenate([value[REACH:STRIP], middle, value[STRIP : STRIP + OWN]], 0)
        return whole.T.reshape(LAYERS, ROWS, LANES)

    return turned(volts[0]), turned(stress[0]), squares


def finish(
    total_x, total_y, dirs, pos, cond, prior, via, diag, pad, load, early, edges, stress, mob, blk, gxa, gxb, own,
    gya, gyb, ma, mb, volts_o, stress_o, sum_o, sums, near_left, near_right, ext_c, ext_m, ext_v, ext_s,
):
    gx, gy = pos[0], pos[1]
    even = gx % 2 == 0
    width = early.shape[2]
    slot = slots_of(dirs)

    def near(right, row, lanes=slice(None)):
        a, b = gxa[pl.ds(row, 1), lanes], gxb[pl.ds(row, 1), lanes]
        return jnp.where(even, a, b) if right else jnp.where(even, b, a)

    for j in range(width // LANES):
        start = FIELDS * STRIP + j * ROWS
        lanes = slice(j * LANES, (j + 1) * LANES)
        a, b = ma[start : start + ROWS], mb[start : start + ROWS]
        near_right[:, lanes] = jnp.where(even, a, b)
        near_left[:, lanes] = jnp.where(even, b, a)
    for ref in (ext_c, ext_m, ext_v, ext_s):
        ref[0:8] = jnp.zeros((8, width), jnp.float32)
        ref[24:32] = jnp.zeros((8, width), jnp.float32)
    sums[...] = jnp.zeros_like(sums)

    for l in range(LAYERS):

        @pl.when(dirs[l] == 0)
        def _(l=l):
            v = early[l]
            row = iota(v.shape, 0)
            v2_left, v2_right = near_left[pl.ds(slot[l] * 4, 1), :], near_right[pl.ds(slot[l] * 4, 1), :]
            extra = jnp.where(row == 0, prior[l] * v2_left, jnp.where(row == ROWS - 1, cond[l] * v2_right, 0.0))
            volts_o[l] = v + damping * extra / guarded(diag[l])

        @pl.when(dirs[l] == 1)
        def _(l=l):
            volts_o[l] = early[l]

    for l in range(LAYERS):

        def add(at, before, after, dim, l=l):
            v = volts_o[(l, *at)]
            first, second = shifted(v, dim, before, after)
            resid = (
                prior[(l, *at)] * first
                + cond[(l, *at)] * second
                + rest_of(l, at, volts_o, via, pad, load)
                - diag[(l, *at)] * v
            )
            col = at[1].start + iota(v.shape, 1)
            squares = jnp.where((col >= REACH) & (col < width - REACH), resid * resid, 0.0)
            total = jnp.zeros((8, LANES), jnp.float32)
            for r in range(0, v.shape[0], 8):
                for c in range(0, v.shape[1], LANES):
                    total = total + squares[r : r + 8, c : c + LANES]
            sums[...] += total

        @pl.when(dirs[l] == 0)
        def _(l=l):
            base, low = slot[l] * EDGE, slot[l] * 4
            last = cond[l, ROWS - 1 :, :]
            v_before = (1.0 - damping) * near_left[pl.ds(low, 1), :] + damping * (
                near_left[pl.ds(low + 1, 1), :] + near(False, base + 2) * edges[0, l : l + 1, :]
            ) / guarded(near(False, base + 11))
            v_after = (1.0 - damping) * near_right[pl.ds(low, 1), :] + damping * (
                near_right[pl.ds(low + 1, 1), :] + last * edges[1, l : l + 1, :]
            ) / guarded(near(True, base + 11) + last)
            ext_v[7:8] = v_before
            ext_v[6:7] = near_left[pl.ds(low + 2, 1), :]
            ext_v[5:6] = near_left[pl.ds(low + 3, 1), :]
            ext_v[24:25] = v_after
            ext_v[25:26] = near_right[pl.ds(low + 2, 1), :]
            ext_v[26:27] = near_right[pl.ds(low + 3, 1), :]
            ext_v[8:24] = volts_o[l]
            for at in blocks(width, False):
                add(at, ext_v[7:8, at[1]], ext_v[24:25, at[1]], 0)
            for ref, first in ((ext_c, 0), (ext_m, 3), (ext_s, 6)):
                for i in range(3):
                    ref[5 + i : 6 + i] = near(False, base + first + i)
                    ref[24 + i : 25 + i] = near(True, base + first + i)
            ext_c[8:24] = cond[l]
            ext_m[8:24] = mob[l] * (1.0 - blk[l].astype(jnp.float32)) * inner_x(gx, total_x, (ROWS, width))
            ext_s[8:24] = stress[l]
            n = 32
            step = min(256, width)
            for start in range(0, width, step):
                lanes = slice(start, start + step)
                v, m, s = ext_v[:, lanes], ext_m[:, lanes], ext_s[:, lanes]
                wind = m * wind_factor * (ext_c[:, lanes] * (v - pltpu.roll(v, n - 1, 0)))
                for _ in range(STEPS):
                    flux = m * (pltpu.roll(s, n - 1, 0) - s) + wind
                    s = s + flux - pltpu.roll(flux, 1, 0)
                stress_o[l, :, lanes] = s[8:24]

        @pl.when(dirs[l] == 1)
        def _(l=l):
            for at in blocks(width, True):
                add(at, None, None, 1)
                v, s = volts_o[(l, *at)], stress[(l, *at)]
                inner = inner_y(gy, total_y, (8, width))
                m = mob[(l, *at)] * (1.0 - blk[(l, *at)].astype(jnp.float32)) * inner
                wind = m * wind_factor * (cond[(l, *at)] * (v - pltpu.roll(v, width - 1, 1)))
                for _ in range(STEPS):
                    flux = m * (pltpu.roll(s, width - 1, 1) - s) + wind
                    s = s + flux - pltpu.roll(flux, 1, 1)
                stress_o[(l, *at)] = s

    strip_v, strip_s, squares = strips(dirs, gy % 2 == 0, even, own, gya, gyb, ma, mb)
    lane = iota((1, 1, LANES), 2)
    for ref, strip in ((volts_o, strip_v), (stress_o, strip_s)):
        ref[:, :, :LANES] = jnp.where(lane < REACH, strip, ref[:, :, :LANES])
        ref[:, :, width - LANES :] = jnp.where(lane >= LANES - REACH, strip, ref[:, :, width - LANES :])
    total = jnp.sum(sums[...]) + jnp.sum(squares)
    sum_o[...] = jnp.full(sum_o.shape, total, jnp.float32)


def call(kernel, ins, outs, scratch=(), scalars=2, in_specs=None, grid=None):
    smem = pl.BlockSpec(memory_space=pltpu.SMEM)
    if in_specs is None:
        in_specs = [pl.BlockSpec(memory_space=pltpu.VMEM)] * (len(ins) - scalars)
    out_specs = [pl.BlockSpec(memory_space=pltpu.VMEM)] * len(outs)
    return pl.pallas_call(
        kernel,
        out_shape=[jax.ShapeDtypeStruct(s, jnp.float32) for s in outs],
        in_specs=[smem] * scalars + in_specs,
        out_specs=out_specs,
        scratch_shapes=[pltpu.VMEM(s, jnp.float32) for s in scratch],
        compiler_params=pltpu.CompilerParams(vmem_limit_bytes=48 * 2**20),
        **({"grid": grid} if grid else {}),
    )(*ins)


def swap(value, axes, first):
    count = lax.axis_size(axes)
    pairs = [(i, i + 1) for i in range(first, count - 1, 2)]
    return lax.ppermute(value, axes, pairs + [(b, a) for a, b in pairs])


def sum_all(held):
    for axes, then in ((("z_hi", "z_lo"), ("x", "y", "core")), (("x", "y", "core"), ())):
        total = jnp.sum(lax.all_to_all(held, axes, 0, 0), 0)
        held = jnp.broadcast_to(total, (lax.axis_size(then), 8, LANES)) if then else total
    return held[0, 0]


def body(volts_start, seg_cond, via_cond, via_mask, pad_mask, load_current, stress_start, mobility, blocked, layer_dirs):
    layers, rows, width = seg_cond.shape
    total_x, total_y = rows * lax.axis_size(X), width * lax.axis_size(Y)
    pos = jnp.stack([lax.axis_index(X), lax.axis_index(Y)]).astype(jnp.int32)
    shape = (layers, rows, width)
    fields = (volts_start, seg_cond, via_cond, via_mask, pad_mask, load_current, stress_start, mobility, blocked)
    ends, specs = [], []
    for a in fields:
        for at in (0, width // LANES - 1):
            ends.append(a)
            index = (0,) * (a.ndim - 1) + (at,)
            specs.append(pl.BlockSpec(a.shape[:-1] + (LANES,), lambda i, index=index: index))
    column = (FIELDS, REACH, LANES)
    own, gya, gyb = call(
        functools.partial(pack_columns, total_x, total_y, width),
        (layer_dirs, pos, *ends),
        [(2, FIELDS, OWN, LANES), column, column],
        in_specs=specs,
        grid=(1,),
    )
    gyb = swap(gyb, Y, 1)
    gya = swap(gya, Y, 0)
    gxa, gxb = call(functools.partial(pack_rows, total_x), (layer_dirs, pos, *fields), [(SLOTS * EDGE, width)] * 2)
    gxa, gxb = swap(gxa, X, 0), swap(gxb, X, 1)
    message = (FIELDS * STRIP + ROWS * (width // LANES), LANES)
    cond, prior, via, diag, early, edges, ma, mb = call(
        functools.partial(early_sweeps, total_x, total_y),
        (layer_dirs, pos, *fields[:6], gxa, gxb, own, gya, gyb),
        [shape, shape, (layers - 1, rows, width), shape, shape, (2, layers, width), message, message],
        scratch=[shape, shape, shape, (2, SLOTS, width), (ROWS, width), (ROWS, width)],
    )
    ma, mb = swap(ma, X, 0), swap(mb, X, 1)
    volts, stress, held = call(
        functools.partial(finish, total_x, total_y),
        (layer_dirs, pos, cond, prior, via, diag, pad_mask, load_current, early, edges, *fields[6:], gxa, gxb, own,
         gya, gyb, ma, mb),
        [shape, shape, (lax.axis_size(("z_hi", "z_lo")), 8, LANES)],
        scratch=[(8, LANES), (ROWS, width), (ROWS, width)] + [(32, width)] * 4,
    )
    resid_rms = jnp.sqrt(sum_all(held) / (layers * total_x * total_y))
    return volts, stress, resid_rms


def solution(mesh):
    gx, gy = mesh.shape["gx"], mesh.shape["gy"]
    fine = jax.sharding.Mesh(mesh.devices.reshape(gx // 4, 4, gy // 4, 2, 2), X + Y)
    cells, plane = P(None, X, Y), P(X, Y)
    in_specs = (cells, cells, cells, cells, plane, plane, cells, cells, cells, P())
    return jax.shard_map(body, mesh=fine, in_specs=in_specs, out_specs=(cells, cells, P()), check_vma=False)
```

```python
import functools

import jax
import jax.numpy as jnp
from jax import lax
from jax.experimental import pallas as pl
from jax.experimental.pallas import tpu as pltpu
from jax.sharding import PartitionSpec as P

SWEEPS = 3
STEPS = 3
LAYERS = 8
ROWS = 16
LANES = 128
REACH = 8
OWN = 16
STRIP = REACH + OWN
SLOTS = 4
EDGE = 12
FIELDS = 6

COST_ROWS = 2**20
COST_STRIPS = 4000 * 2**20
COST_EARLY = 1024

damping = 0.8
pad_conductance = 4.0
supply_volts = 1.0
wind_factor = 4.0

X = ("z_lo", "x")
Y = ("y", "z_hi", "core")


def iota(shape, dim):
    return lax.broadcasted_iota(jnp.int32, shape, dim)


def lane_dirs(dirs, shape):
    layer = iota(shape, len(shape) - 1) // ROWS
    found = jnp.zeros(shape, jnp.int32)
    for l in range(LAYERS):
        found = jnp.where(layer == l, dirs[l], found)
    return found == 1


def slots_of(dirs):
    slot, count = [], jnp.int32(0)
    for l in range(LAYERS):
        slot.append(count)
        count = count + (1 - dirs[l])
    return slot


def fetch(sources, targets, sems):
    copies = [pltpu.make_async_copy(a, b, sems.at[i]) for i, (a, b) in enumerate(zip(sources, targets))]
    for copy in copies:
        copy.start()
    for copy in copies:
        copy.wait()


def pack_columns(total_x, total_y, width, dirs, pos, *refs):
    given, (own_ref, a_ref, b_ref), ins, sems = refs[:9], refs[9:12], refs[12:30], refs[30]
    parts = []
    for ref in given:
        for lanes in (slice(0, LANES), slice(width - LANES, width)):
            parts.append(ref.at[(slice(None),) * (len(ref.shape) - 1) + (lanes,)])
    fetch(parts, ins, sems)
    gx, gy = pos[0], pos[1]
    col = iota((1, 1, LANES), 2)

    def pick(i):
        first, last = ins[2 * i][...], ins[2 * i + 1][...]
        return jnp.where(col.reshape((1,) * (first.ndim - 1) + (LANES,)) < LANES // 2, first, last)

    volts, seg, via_cond, via_mask, pad, load, stress, mob, blk = (pick(i) for i in range(9))
    none = jnp.zeros((1, ROWS, LANES), jnp.float32)
    via = jnp.concatenate([via_cond * via_mask.astype(jnp.float32), none], 0)
    ends = jnp.concatenate(
        [load[None]] + [none] * (LAYERS - 2) + [pad_conductance * pad.astype(jnp.float32)[None]], 0
    )
    mobile = mob * (1.0 - blk.astype(jnp.float32))
    shape = (OWN, LANES)
    along_y = lane_dirs(dirs, shape)
    x = gx * ROWS + iota(shape, 1) % ROWS
    even = gy % 2 == 0
    for f, field in enumerate((volts, seg, via, ends, stress, mobile)):
        turned = field.reshape(LANES, LANES).T
        pieces = []
        for side, start in enumerate((0, LANES - OWN)):
            piece = turned[start : start + OWN]
            if f in (1, 5):
                y = gy * width + (0 if side == 0 else width - OWN) + iota(shape, 0)
                inner = jnp.where(along_y, y, x) < jnp.where(along_y, total_y - 1, total_x - 1)
                piece = jnp.where(inner, piece, 0.0)
            own_ref[side, f] = piece
            pieces.append(piece)
        left, right = pieces[0][:REACH], pieces[1][OWN - REACH :]
        a_ref[f] = jnp.where(even, right, left)
        b_ref[f] = jnp.where(even, left, right)


def inner_x(gx, total_x, shape):
    return (gx * ROWS + iota(shape, 0) < total_x - 1).astype(jnp.float32)


def inner_y(gy, total_y, shape):
    return (gy * shape[1] + iota(shape, 1) < total_y - 1).astype(jnp.float32)


def pack_rows(total_x, dirs, pos, after, *refs):
    given, (a_ref, b_ref), held_refs, sems = refs[:9], refs[9:11], refs[11:20], refs[20]
    fetch(given, held_refs, sems)
    volts, seg, via_cond, via_mask, pad, load, stress, mob, blk = held_refs
    gx = pos[0]
    even = gx % 2 == 0
    width = volts.shape[2]
    inner = inner_x(gx, total_x, (ROWS, width))
    slot = slots_of(dirs)
    for l in range(LAYERS):

        @pl.when(dirs[l] == 0)
        def _(l=l):
            cond = seg[l] * inner
            mobile = mob[l] * (1.0 - blk[l].astype(jnp.float32)) * inner
            held, s = volts[l], stress[l]
            out = []
            for edge in (ROWS - 1, 0):
                here = slice(edge, edge + 1)
                num = jnp.zeros((1, width), jnp.float32)
                diag = cond[here]
                if edge:
                    num = cond[edge - 1 : edge] * held[edge - 1 : edge]
                    diag = diag + cond[edge - 1 : edge]
                else:
                    num = cond[here] * held[1:2]
                if l > 0:
                    below = via_cond[l - 1, here] * via_mask[l - 1, here].astype(jnp.float32)
                    num, diag = num + below * volts[l - 1, here], diag + below
                if l < LAYERS - 1:
                    above = via_cond[l, here] * via_mask[l, here].astype(jnp.float32)
                    num, diag = num + above * volts[l + 1, here], diag + above
                if l == LAYERS - 1:
                    top = pad_conductance * pad[here].astype(jnp.float32)
                    num, diag = num + top * supply_volts, diag + top
                if l == 0:
                    num = num - load[here]
                three = slice(ROWS - 3, ROWS) if edge else slice(0, 3)
                out.append([cond[three], mobile[three], s[three], held[here], num, diag])
            base = slot[l] * EDGE
            at = 0
            for right, left in zip(*out):
                for i in range(right.shape[0]):
                    row = slice(i, i + 1)
                    a_ref[pl.ds(base + at, 1), :] = jnp.where(even, right[row], left[row])
                    b_ref[pl.ds(base + at, 1), :] = jnp.where(even, left[row], right[row])
                    at += 1


def guarded(diag):
    return jnp.where(diag == 0.0, 1.0, diag)


def blocks(width, along_y):
    if along_y:
        return [(slice(r, r + 8), slice(0, width)) for r in range(0, ROWS, 8)]
    step = min(512, width)
    return [(slice(0, ROWS), slice(c, c + step)) for c in range(0, width, step)]


def rest_of(l, at, v, via, pad, load):
    total = None
    if l > 0:
        total = via[(l - 1, *at)] * v[(l - 1, *at)]
    if l < LAYERS - 1:
        above = via[(l, *at)] * v[(l + 1, *at)]
        total = above if total is None else total + above
    if l == LAYERS - 1:
        total = total + pad_conductance * supply_volts * pad[at].astype(jnp.float32)
    if l == 0:
        total = total - load[at]
    return total


def shifted(value, dim, before, after):
    n = value.shape[dim]
    prior, later = pltpu.roll(value, 1, dim), pltpu.roll(value, n - 1, dim)
    if dim == 0:
        row = iota(value.shape, 0)
        if before is not None:
            prior = jnp.where(row == 0, before, prior)
            later = jnp.where(row == n - 1, after, later)
    return prior, later


def strip_pair(recv_a, recv_b, even, own, f):
    from_right = jnp.where(even, recv_a[f], recv_b[f])
    from_left = jnp.where(even, recv_b[f], recv_a[f])
    return (
        jnp.concatenate([from_left, own[0, f]], 0),
        jnp.concatenate([own[1, f], from_right], 0),
    )


def early_sweeps(
    total_x, total_y, dirs, pos, volts, seg, via_cond, via_mask, pad, load, gxa, gxb, strips_a, strips_b,
    cond_o, prior_o, via_o, diag_o, volts_o, edges_o, a_ref, b_ref, rate, one, two, halo, to_right, to_left,
):
    gx, gy = pos[0], pos[1]
    even = gx % 2 == 0
    width = volts.shape[2]
    slot = slots_of(dirs)

    def near(right, row, lanes=slice(None)):
        a, b = gxa[pl.ds(row, 1), lanes], gxb[pl.ds(row, 1), lanes]
        return jnp.where(even, a, b) if right else jnp.where(even, b, a)

    for l in range(LAYERS):
        if l < LAYERS - 1:
            via_o[l] = via_cond[l] * via_mask[l].astype(jnp.float32)

        @pl.when(dirs[l] == 0)
        def _(l=l):
            cond = seg[l] * inner_x(gx, total_x, (ROWS, width))
            cond_o[l] = cond
            prior_o[l] = shifted(cond, 0, near(False, slot[l] * EDGE + 2), 0.0)[0]

        @pl.when(dirs[l] == 1)
        def _(l=l):
            cond = seg[l] * inner_y(gy, total_y, (ROWS, width))
            cond_o[l] = cond
            prior_o[l] = pltpu.roll(cond, 1, 1)

    for l in range(LAYERS):
        diag = cond_o[l] + prior_o[l]
        if l > 0:
            diag = diag + via_o[l - 1]
        if l < LAYERS - 1:
            diag = diag + via_o[l]
        else:
            diag = diag + pad_conductance * pad[...].astype(jnp.float32)
        diag_o[l] = diag
        rate[l] = damping / guarded(diag)

    for sweep, (old, new) in enumerate(((volts, one), (one, two), (two, volts_o))):
        for l in range(LAYERS):

            @pl.when(dirs[l] == 0)
            def _(l=l):
                base = slot[l] * EDGE
                for at in blocks(width, False):
                    lanes = at[1]
                    v = old[(l, *at)]
                    if sweep == 0:
                        before, after = near(False, base + 9, lanes), near(True, base + 9, lanes)
                        cond_left = near(False, base + 2, lanes)
                        last = cond_o[l, ROWS - 1 :, lanes]
                        halo[0, pl.ds(slot[l], 1), lanes] = (1.0 - damping) * before + damping * (
                            near(False, base + 10, lanes) + cond_left * v[:1]
                        ) / guarded(near(False, base + 11, lanes))
                        halo[1, pl.ds(slot[l], 1), lanes] = (1.0 - damping) * after + damping * (
                            near(True, base + 10, lanes) + last * v[ROWS - 1 :]
                        ) / guarded(near(True, base + 11, lanes) + last)
                    elif sweep == 1:
                        before, after = halo[0, pl.ds(slot[l], 1), lanes], halo[1, pl.ds(slot[l], 1), lanes]
                    else:
                        before = after = 0.0
                    prior, later = shifted(v, 0, before, after)
                    num = prior_o[(l, *at)] * prior + cond_o[(l, *at)] * later + rest_of(l, at, old, via_o, pad, load)
                    result = (1.0 - damping) * v + rate[(l, *at)] * num
                    new[(l, *at)] = result
                    if sweep == 2:
                        edges_o[0, l : l + 1, lanes] = v[:1]
                        edges_o[1, l : l + 1, lanes] = v[ROWS - 1 :]
                        send = slot[l] * 4
                        for ref, e, d in ((to_right, ROWS - 1, -1), (to_left, 0, 1)):
                            ref[pl.ds(send, 1), lanes] = v[e : e + 1]
                            ref[pl.ds(send + 1, 1), lanes] = num[e : e + 1]
                            ref[pl.ds(send + 2, 1), lanes] = result[e + d : e + d + 1]
                            ref[pl.ds(send + 3, 1), lanes] = result[e + 2 * d : e + 2 * d + 1]

            @pl.when(dirs[l] == 1)
            def _(l=l):
                for at in blocks(width, True):
                    v = old[(l, *at)]
                    prior, later = shifted(v, 1, None, None)
                    num = prior_o[(l, *at)] * prior + cond_o[(l, *at)] * later + rest_of(l, at, old, via_o, pad, load)
                    new[(l, *at)] = (1.0 - damping) * v + rate[(l, *at)] * num
                    if sweep == 2:
                        edges_o[:, l : l + 1, :] = jnp.zeros((2, 1, width), jnp.float32)

    a_ref[: FIELDS * STRIP] = strips_a[...]
    b_ref[: FIELDS * STRIP] = strips_b[...]
    for j in range(width // LANES):
        start = FIELDS * STRIP + j * ROWS
        lanes = slice(j * LANES, (j + 1) * LANES)
        a_ref[start : start + ROWS] = jnp.where(even, to_right[:, lanes], to_left[:, lanes])
        b_ref[start : start + ROWS] = jnp.where(even, to_left[:, lanes], to_right[:, lanes])


def pack_strips(pos, own, gyb, gya, a_ref, b_ref):
    gx, gy = pos[0], pos[1]
    even = gx % 2 == 0
    x = iota((STRIP, LANES), 1) % ROWS
    for f in range(FIELDS):
        left, right = strip_pair(gya, gyb, gy % 2 == 0, own, f)
        right_going = jnp.where(x >= 8, left, pltpu.roll(right, LANES - 8, 1))
        left_going = jnp.where(x < 8, left, pltpu.roll(right, 8, 1))
        a_ref[f * STRIP : (f + 1) * STRIP] = jnp.where(even, right_going, left_going)
        b_ref[f * STRIP : (f + 1) * STRIP] = jnp.where(even, left_going, right_going)


def strip_field(f, even_y, even_x, own, gya, gyb, ma, mb):
    x = iota((STRIP, LANES), 1) % ROWS
    left, right = strip_pair(gya, gyb, even_y, own, f)
    a, b = ma[f * STRIP : (f + 1) * STRIP], mb[f * STRIP : (f + 1) * STRIP]
    from_right, from_left = jnp.where(even_x, a, b), jnp.where(even_x, b, a)
    far_left = jnp.where(x >= 8, from_left, from_right)
    far_right = jnp.where(x >= 8, pltpu.roll(from_left, 8, 1), pltpu.roll(from_right, LANES - 8, 1))
    return jnp.concatenate([left, right], 0), jnp.concatenate([far_left, far_right], 0)


def strip_shifts(dirs):
    tall = (2 * STRIP, LANES)
    along_y = lane_dirs(dirs, tall)
    x = iota(tall, 1) % ROWS

    def later(pair):
        o, h = pair
        out = []
        for this, other in ((o, h), (h, o)):
            across = jnp.where(x == ROWS - 1, pltpu.roll(other, ROWS - 1, 1), pltpu.roll(this, LANES - 1, 1))
            out.append(jnp.where(along_y, pltpu.roll(this, tall[0] - 1, 0), across))
        return out

    def prior(pair):
        o, h = pair
        out = []
        for this, other in ((o, h), (h, o)):
            across = jnp.where(x == 0, pltpu.roll(other, LANES - ROWS + 1, 1), pltpu.roll(this, 1, 1))
            out.append(jnp.where(along_y, pltpu.roll(this, 1, 0), across))
        return out

    return prior, later


def strips(dirs, even_y, even_x, own, gya, gyb, ma, mb):
    tall = (2 * STRIP, LANES)
    layer = iota(tall, 1) // ROWS
    prior, later = strip_shifts(dirs)
    volts, cond, via, ends, mobile = (
        strip_field(f, even_y, even_x, own, gya, gyb, ma, mb) for f in (0, 1, 2, 3, 5)
    )
    via_below = [pltpu.roll(a, ROWS, 1) for a in via]
    top = [jnp.where(layer == LAYERS - 1, a, 0.0) for a in ends]
    load = [jnp.where(layer == 0, a, 0.0) for a in ends]
    cond_prior = prior(cond)
    diag = [guarded(p + c + vb + va + t) for p, c, vb, va, t in zip(cond_prior, cond, via_below, via, top)]
    rate = [damping / d for d in diag]

    def inflow(v):
        before, after = prior(v), later(v)
        return [
            cond_prior[i] * before[i]
            + cond[i] * after[i]
            + via_below[i] * pltpu.roll(v[i], ROWS, 1)
            + via[i] * pltpu.roll(v[i], LANES - ROWS, 1)
            + top[i] * supply_volts
            - load[i]
            for i in range(2)
        ]

    for _ in range(SWEEPS):
        num = inflow(volts)
        volts = [(1.0 - damping) * v + r * n for v, r, n in zip(volts, rate, num)]
    resid = inflow(volts)[0] - diag[0] * volts[0]
    sub = iota(tall, 0)
    inside = ((sub >= REACH) & (sub < 2 * REACH)) | ((sub >= STRIP + REACH) & (sub < STRIP + 2 * REACH))
    squares = jnp.where(inside, resid * resid, 0.0)
    after = later(volts)
    wind = [mobile[i] * wind_factor * (cond[i] * (volts[i] - after[i])) for i in range(2)]
    return turned(volts[0]), wind, squares


def strip_stress(dirs, even_y, even_x, own, gya, gyb, ma, mb, wind):
    stress, mobile = (strip_field(f, even_y, even_x, own, gya, gyb, ma, mb) for f in (4, 5))
    prior, later = strip_shifts(dirs)
    for _ in range(STEPS):
        after = later(stress)
        flux = [mobile[i] * (after[i] - stress[i]) + wind[i] for i in range(2)]
        back = prior(flux)
        stress = [stress[i] + flux[i] - back[i] for i in range(2)]
    return turned(stress[0])


def turned(value):
    middle = jnp.zeros((LANES - 2 * OWN, LANES), jnp.float32)
    whole = jnp.concatenate([value[REACH:STRIP], middle, value[STRIP : STRIP + OWN]], 0)
    return whole.T.reshape(LAYERS, ROWS, LANES)


def last_sweep(
    dirs, pos, cond, prior, via, diag, pad, load, early, edges, gxa, gxb, own, gya, gyb, ma, mb,
    volts_o, sum_o, sides_o, wind_o, sums, near_left, near_right,
):
    gx, gy = pos[0], pos[1]
    even = gx % 2 == 0
    width = early.shape[2]
    slot = slots_of(dirs)

    def near(right, row):
        a, b = gxa[pl.ds(row, 1), :], gxb[pl.ds(row, 1), :]
        return jnp.where(even, a, b) if right else jnp.where(even, b, a)

    for j in range(width // LANES):
        start = FIELDS * STRIP + j * ROWS
        lanes = slice(j * LANES, (j + 1) * LANES)
        a, b = ma[start : start + ROWS], mb[start : start + ROWS]
        near_right[:, lanes] = jnp.where(even, a, b)
        near_left[:, lanes] = jnp.where(even, b, a)
    sums[...] = jnp.zeros_like(sums)

    for l in range(LAYERS):

        @pl.when(dirs[l] == 0)
        def _(l=l):
            v = early[l]
            row = iota(v.shape, 0)
            base, low = slot[l] * EDGE, slot[l] * 4
            v2_left, v2_right = near_left[pl.ds(low, 1), :], near_right[pl.ds(low, 1), :]
            extra = jnp.where(row == 0, prior[l] * v2_left, jnp.where(row == ROWS - 1, cond[l] * v2_right, 0.0))
            volts_o[l] = v + damping * extra / guarded(diag[l])
            last = cond[l, ROWS - 1 :, :]
            sides_o[0, pl.ds(low, 1), :] = (1.0 - damping) * v2_left + damping * (
                near_left[pl.ds(low + 1, 1), :] + near(False, base + 2) * edges[0, l : l + 1, :]
            ) / guarded(near(False, base + 11))
            sides_o[1, pl.ds(low, 1), :] = (1.0 - damping) * v2_right + damping * (
                near_right[pl.ds(low + 1, 1), :] + last * edges[1, l : l + 1, :]
            ) / guarded(near(True, base + 11) + last)
            for side, ref in enumerate((near_left, near_right)):
                sides_o[side, pl.ds(low + 1, 1), :] = ref[pl.ds(low + 2, 1), :]
                sides_o[side, pl.ds(low + 2, 1), :] = ref[pl.ds(low + 3, 1), :]

        @pl.when(dirs[l] == 1)
        def _(l=l):
            volts_o[l] = early[l]

    for l in range(LAYERS):

        def add(at, before, after, dim, l=l):
            v = volts_o[(l, *at)]
            first, second = shifted(v, dim, before, after)
            resid = (
                prior[(l, *at)] * first
                + cond[(l, *at)] * second
                + rest_of(l, at, volts_o, via, pad, load)
                - diag[(l, *at)] * v
            )
            col = at[1].start + iota(v.shape, 1)
            squares = jnp.where((col >= REACH) & (col < width - REACH), resid * resid, 0.0)
            total = jnp.zeros((8, LANES), jnp.float32)
            for r in range(0, v.shape[0], 8):
                for c in range(0, v.shape[1], LANES):
                    total = total + squares[r : r + 8, c : c + LANES]
            sums[...] += total

        @pl.when(dirs[l] == 0)
        def _(l=l):
            for at in blocks(width, False):
                low = pl.ds(slot[l] * 4, 1)
                add(at, sides_o[0, low, at[1]], sides_o[1, low, at[1]], 0)

        @pl.when(dirs[l] == 1)
        def _(l=l):
            for at in blocks(width, True):
                add(at, None, None, 1)

    strip_v, wind, squares = strips(dirs, gy % 2 == 0, even, own, gya, gyb, ma, mb)
    for i in range(2):
        wind_o[i] = wind[i]
    place(volts_o, strip_v)
    total = jnp.sum(sums[...]) + jnp.sum(squares)
    sum_o[...] = jnp.full(sum_o.shape, total, jnp.float32)


def place(ref, strip):
    width = ref.shape[2]
    lane = iota((1, 1, LANES), 2)
    ref[:, :, :LANES] = jnp.where(lane < REACH, strip, ref[:, :, :LANES])
    ref[:, :, width - LANES :] = jnp.where(lane >= LANES - REACH, strip, ref[:, :, width - LANES :])


def stress_steps(
    total_x, total_y, dirs, pos, cond, volts, sides, stress, mob, blk, gxa, gxb, own, gya, gyb, ma, mb, wind_strip,
    stress_o, ext_c, ext_m, ext_v, ext_s,
):
    gx, gy = pos[0], pos[1]
    even = gx % 2 == 0
    width = volts.shape[2]
    slot = slots_of(dirs)

    def near(right, row):
        a, b = gxa[pl.ds(row, 1), :], gxb[pl.ds(row, 1), :]
        return jnp.where(even, a, b) if right else jnp.where(even, b, a)

    for ref in (ext_c, ext_m, ext_v, ext_s):
        ref[0:8] = jnp.zeros((8, width), jnp.float32)
        ref[24:32] = jnp.zeros((8, width), jnp.float32)

    for l in range(LAYERS):

        @pl.when(dirs[l] == 0)
        def _(l=l):
            base, low = slot[l] * EDGE, slot[l] * 4
            for i in range(3):
                ext_v[7 - i : 8 - i] = sides[0, pl.ds(low + i, 1), :]
                ext_v[24 + i : 25 + i] = sides[1, pl.ds(low + i, 1), :]
                for ref, first in ((ext_c, 0), (ext_m, 3), (ext_s, 6)):
                    ref[5 + i : 6 + i] = near(False, base + first + i)
                    ref[24 + i : 25 + i] = near(True, base + first + i)
            ext_v[8:24] = volts[l]
            ext_c[8:24] = cond[l]
            ext_m[8:24] = mob[l] * (1.0 - blk[l].astype(jnp.float32)) * inner_x(gx, total_x, (ROWS, width))
            ext_s[8:24] = stress[l]
            n = 32
            step = min(256, width)
            for start in range(0, width, step):
                lanes = slice(start, start + step)
                v, m, s = ext_v[:, lanes], ext_m[:, lanes], ext_s[:, lanes]
                wind = m * wind_factor * (ext_c[:, lanes] * (v - pltpu.roll(v, n - 1, 0)))
                for _ in range(STEPS):
                    flux = m * (pltpu.roll(s, n - 1, 0) - s) + wind
                    s = s + flux - pltpu.roll(flux, 1, 0)
                stress_o[l, :, lanes] = s[8:24]

        @pl.when(dirs[l] == 1)
        def _(l=l):
            for at in blocks(width, True):
                v, s = volts[(l, *at)], stress[(l, *at)]
                inner = inner_y(gy, total_y, (8, width))
                m = mob[(l, *at)] * (1.0 - blk[(l, *at)].astype(jnp.float32)) * inner
                wind = m * wind_factor * (cond[(l, *at)] * (v - pltpu.roll(v, width - 1, 1)))
                for _ in range(STEPS):
                    flux = m * (pltpu.roll(s, width - 1, 1) - s) + wind
                    s = s + flux - pltpu.roll(flux, 1, 1)
                stress_o[(l, *at)] = s

    wind = [wind_strip[0], wind_strip[1]]
    place(stress_o, strip_stress(dirs, gy % 2 == 0, even, own, gya, gyb, ma, mb, wind))


def call(kernel, ins, outs, scratch=(), scalars=2, copies=0, cost=0):
    smem, vmem = pl.BlockSpec(memory_space=pltpu.SMEM), pl.BlockSpec(memory_space=pltpu.VMEM)
    held = pl.BlockSpec(memory_space=pltpu.HBM) if copies else vmem
    scratch = [pltpu.VMEM(*(s if isinstance(s[0], tuple) else (s, jnp.float32))) for s in scratch]
    return pl.pallas_call(
        kernel,
        out_shape=[jax.ShapeDtypeStruct(s, jnp.float32) for s in outs],
        in_specs=[smem] * scalars + [held] * (len(ins) - scalars),
        out_specs=[vmem] * len(outs),
        scratch_shapes=scratch + ([pltpu.SemaphoreType.DMA((copies,))] if copies else []),
        compiler_params=pltpu.CompilerParams(vmem_limit_bytes=(62 if copies else 16) * 2**20),
        cost_estimate=pl.CostEstimate(flops=cost, bytes_accessed=cost, transcendentals=0),
    )(*ins)


def swap(value, axes, first):
    count = lax.axis_size(axes)
    pairs = [(i, i + 1) for i in range(first, count - 1, 2)]
    return lax.ppermute(value, axes, pairs + [(b, a) for a, b in pairs])


def sum_all(held):
    for axes, then in ((("z_hi", "z_lo"), ("x", "y", "core")), (("x", "y", "core"), ())):
        total = jnp.sum(lax.all_to_all(held, axes, 0, 0), 0)
        held = jnp.broadcast_to(total, (lax.axis_size(then), 8, LANES)) if then else total
    return held[0, 0]


def body(volts_start, seg_cond, via_cond, via_mask, pad_mask, load_current, stress_start, mobility, blocked, layer_dirs):
    layers, rows, width = seg_cond.shape
    total_x, total_y = rows * lax.axis_size(X), width * lax.axis_size(Y)
    pos = jnp.stack([lax.axis_index(X), lax.axis_index(Y)]).astype(jnp.int32)
    shape = (layers, rows, width)
    fields = (volts_start, seg_cond, via_cond, via_mask, pad_mask, load_current, stress_start, mobility, blocked)
    column = (FIELDS, REACH, LANES)
    own, gya, gyb = call(
        functools.partial(pack_columns, total_x, total_y, width),
        (layer_dirs, pos, *fields),
        [(2, FIELDS, OWN, LANES), column, column],
        scratch=[(a.shape[:-1] + (LANES,), a.dtype) for a in fields for _ in range(2)],
        copies=18,
    )
    gyb, gya = swap(gyb, Y, 1), swap(gya, Y, 0)
    gxa, gxb = call(
        functools.partial(pack_rows, total_x),
        (layer_dirs, pos, own, *fields),
        [(SLOTS * EDGE, width)] * 2,
        scratch=[(a.shape, a.dtype) for a in fields],
        copies=9,
        cost=COST_ROWS,
    )
    gxa, gxb = swap(gxa, X, 0), swap(gxb, X, 1)
    side = (FIELDS * STRIP, LANES)
    sa, sb = call(pack_strips, (pos, own, gyb, gya), [side, side], scalars=1, cost=COST_STRIPS)
    message = (FIELDS * STRIP + ROWS * (width // LANES), LANES)
    cond, prior, via, diag, early, edges, ma, mb = call(
        functools.partial(early_sweeps, total_x, total_y),
        (layer_dirs, pos, *fields[:6], gxa, gxb, sa, sb),
        [shape, shape, (layers - 1, rows, width), shape, shape, (2, layers, width), message, message],
        scratch=[shape, shape, shape, (2, SLOTS, width), (ROWS, width), (ROWS, width)],
        cost=COST_EARLY,
    )
    ma, mb = swap(ma, X, 0), swap(mb, X, 1)
    volts, held, sides, wind = call(
        last_sweep,
        (layer_dirs, pos, cond, prior, via, diag, pad_mask, load_current, early, edges, gxa, gxb, own, gya, gyb, ma, mb),
        [shape, (lax.axis_size(("z_hi", "z_lo")), 8, LANES), (2, ROWS, width), (2, 2 * STRIP, LANES)],
        scratch=[(8, LANES), (ROWS, width), (ROWS, width)],
    )
    (stress,) = call(
        functools.partial(stress_steps, total_x, total_y),
        (layer_dirs, pos, cond, volts, sides, *fields[6:], gxa, gxb, own, gya, gyb, ma, mb, wind),
        [shape],
        scratch=[(32, width)] * 4,
        cost=12 * 2**20,
    )
    resid_rms = jnp.sqrt(sum_all(held) / (layers * total_x * total_y))
    return volts, stress, resid_rms


def solution(mesh):
    gx, gy = mesh.shape["gx"], mesh.shape["gy"]
    fine = jax.sharding.Mesh(mesh.devices.reshape(gx // 4, 4, gy // 4, 2, 2), X + Y)
    cells, plane = P(None, X, Y), P(X, Y)
    in_specs = (cells, cells, cells, cells, plane, plane, cells, cells, cells, P())
    return jax.shard_map(body, mesh=fine, in_specs=in_specs, out_specs=(cells, cells, P()), check_vma=False)
```

```python
import functools

import jax
import jax.numpy as jnp
from jax import lax
from jax.experimental import pallas as pl
from jax.experimental.pallas import tpu as pltpu
from jax.sharding import PartitionSpec as P

SWEEPS = 3
STEPS = 3
LAYERS = 8
ROWS = 16
LANES = 128
REACH = 8
OWN = 16
STRIP = REACH + OWN
SLOTS = 4
EDGE = 12
FIELDS = 6

COST_ROWS = 2**20
COST_STRIPS = 4000 * 2**20
COST_EARLY = 1024
COST_SETUP = 4 * 2**20

damping = 0.8
pad_conductance = 4.0
supply_volts = 1.0
wind_factor = 4.0

X = ("z_lo", "x")
Y = ("y", "z_hi", "core")
NEAR = ("x", "y", "core")
FAR = ("z_hi", "z_lo")


def position():
    out = []
    for axes in (X, Y):
        at = lax.axis_index(axes[0])
        for a in axes[1:]:
            at = at * lax.axis_size(a) + lax.axis_index(a)
        out.append(at)
    return out


def iota(shape, dim):
    return lax.broadcasted_iota(jnp.int32, shape, dim)


def lane_dirs(dirs, shape):
    layer = iota(shape, len(shape) - 1) // ROWS
    found = jnp.zeros(shape, jnp.int32)
    for l in range(LAYERS):
        found = jnp.where(layer == l, dirs[l], found)
    return found == 1


def slots_of(dirs):
    slot, count = [], jnp.int32(0)
    for l in range(LAYERS):
        slot.append(count)
        count = count + (1 - dirs[l])
    return slot


def fetch(sources, targets, sems):
    copies = [pltpu.make_async_copy(a, b, sems.at[i]) for i, (a, b) in enumerate(zip(sources, targets))]
    for copy in copies:
        copy.start()
    return copies


def pack_columns(total_x, total_y, width, dirs, *refs):
    given, (own_ref, a_ref, b_ref), ins, sems = refs[:9], refs[9:12], refs[12:30], refs[30]
    parts = []
    for ref in given:
        for lanes in (slice(0, LANES), slice(width - LANES, width)):
            parts.append(ref.at[(slice(None),) * (len(ref.shape) - 1) + (lanes,)])
    copies = fetch(parts, ins, sems)
    gx, gy = position()
    col = iota((1, 1, LANES), 2)

    def pick(i):
        for copy in copies[2 * i : 2 * i + 2]:
            copy.wait()
        first, last = ins[2 * i][...], ins[2 * i + 1][...]
        return jnp.where(col.reshape((1,) * (first.ndim - 1) + (LANES,)) < LANES // 2, first, last)

    def field(f):
        if f < 2:
            return pick(f)
        if f == 2:
            return jnp.concatenate([pick(2) * pick(3).astype(jnp.float32), none], 0)
        if f == 3:
            top, load = pad_conductance * pick(4).astype(jnp.float32), pick(5)
            return jnp.concatenate([load[None]] + [none] * (LAYERS - 2) + [top[None]], 0)
        if f == 4:
            return pick(6)
        return pick(7) * (1.0 - pick(8).astype(jnp.float32))

    none = jnp.zeros((1, ROWS, LANES), jnp.float32)
    shape = (OWN, LANES)
    along_y = lane_dirs(dirs, shape)
    x = gx * ROWS + iota(shape, 1) % ROWS
    even = gy % 2 == 0
    for f in range(FIELDS):
        turned = field(f).reshape(LANES, LANES).T
        pieces = []
        for side, start in enumerate((0, LANES - OWN)):
            piece = turned[start : start + OWN]
            if f in (1, 5):
                y = gy * width + (0 if side == 0 else width - OWN) + iota(shape, 0)
                inner = jnp.where(along_y, y, x) < jnp.where(along_y, total_y - 1, total_x - 1)
                piece = jnp.where(inner, piece, 0.0)
            own_ref[side, f] = piece
            pieces.append(piece)
        left, right = pieces[0][:REACH], pieces[1][OWN - REACH :]
        a_ref[f] = jnp.where(even, right, left)
        b_ref[f] = jnp.where(even, left, right)


def inner_x(gx, total_x, shape):
    return (gx * ROWS + iota(shape, 0) < total_x - 1).astype(jnp.float32)


def inner_y(gy, total_y, shape):
    return (gy * shape[1] + iota(shape, 1) < total_y - 1).astype(jnp.float32)


def pack_rows(total_x, dirs, volts, seg, via_cond, via_mask, pad, load, stress, mob, blk, a_ref, b_ref):
    gx, _ = position()
    even = gx % 2 == 0
    width = volts.shape[2]
    inner = inner_x(gx, total_x, (ROWS, width))
    slot = slots_of(dirs)
    for l in range(LAYERS):

        @pl.when(dirs[l] == 0)
        def _(l=l):
            cond = seg[l] * inner
            mobile = mob[l] * (1.0 - blk[l].astype(jnp.float32)) * inner
            held, s = volts[l], stress[l]
            out = []
            for edge in (ROWS - 1, 0):
                here = slice(edge, edge + 1)
                num = jnp.zeros((1, width), jnp.float32)
                diag = cond[here]
                if edge:
                    num = cond[edge - 1 : edge] * held[edge - 1 : edge]
                    diag = diag + cond[edge - 1 : edge]
                else:
                    num = cond[here] * held[1:2]
                if l > 0:
                    below = via_cond[l - 1, here] * via_mask[l - 1, here].astype(jnp.float32)
                    num, diag = num + below * volts[l - 1, here], diag + below
                if l < LAYERS - 1:
                    above = via_cond[l, here] * via_mask[l, here].astype(jnp.float32)
                    num, diag = num + above * volts[l + 1, here], diag + above
                if l == LAYERS - 1:
                    top = pad_conductance * pad[here].astype(jnp.float32)
                    num, diag = num + top * supply_volts, diag + top
                if l == 0:
                    num = num - load[here]
                three = slice(ROWS - 3, ROWS) if edge else slice(0, 3)
                out.append([cond[three], mobile[three], s[three], held[here], num, diag])
            base = slot[l] * EDGE
            at = 0
            for right, left in zip(*out):
                for i in range(right.shape[0]):
                    row = slice(i, i + 1)
                    a_ref[pl.ds(base + at, 1), :] = jnp.where(even, right[row], left[row])
                    b_ref[pl.ds(base + at, 1), :] = jnp.where(even, left[row], right[row])
                    at += 1


def guarded(diag):
    return jnp.where(diag == 0.0, 1.0, diag)


def blocks(width, along_y):
    if along_y:
        return [(slice(r, r + 8), slice(0, width)) for r in range(0, ROWS, 8)]
    step = min(512, width)
    return [(slice(0, ROWS), slice(c, c + step)) for c in range(0, width, step)]


def rest_of(l, at, v, via, pad, load):
    total = None
    if l > 0:
        total = via[(l - 1, *at)] * v[(l - 1, *at)]
    if l < LAYERS - 1:
        above = via[(l, *at)] * v[(l + 1, *at)]
        total = above if total is None else total + above
    if l == LAYERS - 1:
        total = total + pad_conductance * supply_volts * pad[at].astype(jnp.float32)
    if l == 0:
        total = total - load[at]
    return total


def shifted(value, dim, before, after):
    n = value.shape[dim]
    prior, later = pltpu.roll(value, 1, dim), pltpu.roll(value, n - 1, dim)
    if dim == 0:
        row = iota(value.shape, 0)
        if before is not None:
            prior = jnp.where(row == 0, before, prior)
            later = jnp.where(row == n - 1, after, later)
    return prior, later


def strip_pair(recv_a, recv_b, even, own, f):
    from_right = jnp.where(even, recv_a[f], recv_b[f])
    from_left = jnp.where(even, recv_b[f], recv_a[f])
    return (
        jnp.concatenate([from_left, own[0, f]], 0),
        jnp.concatenate([own[1, f], from_right], 0),
    )


def conductances(
    total_x, total_y, dirs, after_a, after_b, seg, via_cond, via_mask, pad, cond_o, prior_o, via_o, diag_o, rate_o,
):
    gx, gy = position()
    width = seg.shape[2]
    for l in range(LAYERS):
        if l < LAYERS - 1:
            via_o[l] = via_cond[l] * via_mask[l].astype(jnp.float32)

        @pl.when(dirs[l] == 0)
        def _(l=l):
            cond = seg[l] * inner_x(gx, total_x, (ROWS, width))
            cond_o[l] = cond
            prior_o[l] = shifted(cond, 0, 0.0, 0.0)[0]

        @pl.when(dirs[l] == 1)
        def _(l=l):
            cond = seg[l] * inner_y(gy, total_y, (ROWS, width))
            cond_o[l] = cond
            prior_o[l] = pltpu.roll(cond, 1, 1)

    for l in range(LAYERS):
        diag = cond_o[l] + prior_o[l]
        if l > 0:
            diag = diag + via_o[l - 1]
        if l < LAYERS - 1:
            diag = diag + via_o[l]
        else:
            diag = diag + pad_conductance * pad[...].astype(jnp.float32)
        diag_o[l] = diag
        rate_o[l] = damping / guarded(diag)


def early_sweeps(
    dirs, cond_o, prior_i, via_o, diag_i, rate_i, volts, pad, load, gxa, gxb, strips_a, strips_b,
    prior_o, diag_o, rate_o, volts_o, edges_o, a_ref, b_ref, one, two, halo, to_right, to_left,
):
    gx, gy = position()
    even = gx % 2 == 0
    width = volts.shape[2]
    slot = slots_of(dirs)

    def near(right, row, lanes=slice(None)):
        a, b = gxa[pl.ds(row, 1), lanes], gxb[pl.ds(row, 1), lanes]
        return jnp.where(even, a, b) if right else jnp.where(even, b, a)

    for l in range(LAYERS):

        @pl.when(dirs[l] == 0)
        def _(l=l):
            first = near(False, slot[l] * EDGE + 2)
            prior_o[l, :1] = first
            diag_o[l, :1] = diag_i[l, :1] + first
            rate_o[l, :1] = damping / guarded(diag_o[l, :1])

    for sweep, (old, new) in enumerate(((volts, one), (one, two), (two, volts_o))):
        for l in range(LAYERS):

            @pl.when(dirs[l] == 0)
            def _(l=l):
                base = slot[l] * EDGE
                for at in blocks(width, False):
                    lanes = at[1]
                    v = old[(l, *at)]
                    if sweep == 0:
                        before, after = near(False, base + 9, lanes), near(True, base + 9, lanes)
                        cond_left = near(False, base + 2, lanes)
                        last = cond_o[l, ROWS - 1 :, lanes]
                        halo[0, pl.ds(slot[l], 1), lanes] = (1.0 - damping) * before + damping * (
                            near(False, base + 10, lanes) + cond_left * v[:1]
                        ) / guarded(near(False, base + 11, lanes))
                        halo[1, pl.ds(slot[l], 1), lanes] = (1.0 - damping) * after + damping * (
                            near(True, base + 10, lanes) + last * v[ROWS - 1 :]
                        ) / guarded(near(True, base + 11, lanes) + last)
                    elif sweep == 1:
                        before, after = halo[0, pl.ds(slot[l], 1), lanes], halo[1, pl.ds(slot[l], 1), lanes]
                    else:
                        before = after = 0.0
                    prior, later = shifted(v, 0, before, after)
                    num = prior_o[(l, *at)] * prior + cond_o[(l, *at)] * later + rest_of(l, at, old, via_o, pad, load)
                    result = (1.0 - damping) * v + rate_o[(l, *at)] * num
                    new[(l, *at)] = result
                    if sweep == 2:
                        edges_o[0, l : l + 1, lanes] = v[:1]
                        edges_o[1, l : l + 1, lanes] = v[ROWS - 1 :]
                        send = slot[l] * 4
                        for ref, e, d in ((to_right, ROWS - 1, -1), (to_left, 0, 1)):
                            ref[pl.ds(send, 1), lanes] = v[e : e + 1]
                            ref[pl.ds(send + 1, 1), lanes] = num[e : e + 1]
                            ref[pl.ds(send + 2, 1), lanes] = result[e + d : e + d + 1]
                            ref[pl.ds(send + 3, 1), lanes] = result[e + 2 * d : e + 2 * d + 1]

            @pl.when(dirs[l] == 1)
            def _(l=l):
                for at in blocks(width, True):
                    v = old[(l, *at)]
                    prior, later = shifted(v, 1, None, None)
                    num = prior_o[(l, *at)] * prior + cond_o[(l, *at)] * later + rest_of(l, at, old, via_o, pad, load)
                    new[(l, *at)] = (1.0 - damping) * v + rate_o[(l, *at)] * num
                    if sweep == 2:
                        edges_o[:, l : l + 1, :] = jnp.zeros((2, 1, width), jnp.float32)

    a_ref[: FIELDS * STRIP] = strips_a[...]
    b_ref[: FIELDS * STRIP] = strips_b[...]
    for j in range(width // LANES):
        start = FIELDS * STRIP + j * ROWS
        lanes = slice(j * LANES, (j + 1) * LANES)
        a_ref[start : start + ROWS] = jnp.where(even, to_right[:, lanes], to_left[:, lanes])
        b_ref[start : start + ROWS] = jnp.where(even, to_left[:, lanes], to_right[:, lanes])


def pack_strips(own, gyb, gya, a_ref, b_ref):
    gx, gy = position()
    even = gx % 2 == 0
    x = iota((STRIP, LANES), 1) % ROWS
    for f in range(FIELDS):
        left, right = strip_pair(gya, gyb, gy % 2 == 0, own, f)
        right_going = jnp.where(x >= 8, left, pltpu.roll(right, LANES - 8, 1))
        left_going = jnp.where(x < 8, left, pltpu.roll(right, 8, 1))
        a_ref[f * STRIP : (f + 1) * STRIP] = jnp.where(even, right_going, left_going)
        b_ref[f * STRIP : (f + 1) * STRIP] = jnp.where(even, left_going, right_going)


def strip_field(f, even_y, even_x, own, gya, gyb, ma, mb):
    x = iota((STRIP, LANES), 1) % ROWS
    left, right = strip_pair(gya, gyb, even_y, own, f)
    a, b = ma[f * STRIP : (f + 1) * STRIP], mb[f * STRIP : (f + 1) * STRIP]
    from_right, from_left = jnp.where(even_x, a, b), jnp.where(even_x, b, a)
    far_left = jnp.where(x >= 8, from_left, from_right)
    far_right = jnp.where(x >= 8, pltpu.roll(from_left, 8, 1), pltpu.roll(from_right, LANES - 8, 1))
    return jnp.concatenate([left, right], 0), jnp.concatenate([far_left, far_right], 0)


def strip_shifts(dirs):
    tall = (2 * STRIP, LANES)
    along_y = lane_dirs(dirs, tall)
    x = iota(tall, 1) % ROWS

    def later(pair):
        o, h = pair
        out = []
        for this, other in ((o, h), (h, o)):
            across = jnp.where(x == ROWS - 1, pltpu.roll(other, ROWS - 1, 1), pltpu.roll(this, LANES - 1, 1))
            out.append(jnp.where(along_y, pltpu.roll(this, tall[0] - 1, 0), across))
        return out

    def prior(pair):
        o, h = pair
        out = []
        for this, other in ((o, h), (h, o)):
            across = jnp.where(x == 0, pltpu.roll(other, LANES - ROWS + 1, 1), pltpu.roll(this, 1, 1))
            out.append(jnp.where(along_y, pltpu.roll(this, 1, 0), across))
        return out

    return prior, later


def strips(dirs, even_y, even_x, own, gya, gyb, ma, mb):
    tall = (2 * STRIP, LANES)
    layer = iota(tall, 1) // ROWS
    prior, later = strip_shifts(dirs)
    volts, cond, via, ends, mobile = (
        strip_field(f, even_y, even_x, own, gya, gyb, ma, mb) for f in (0, 1, 2, 3, 5)
    )
    via_below = [pltpu.roll(a, ROWS, 1) for a in via]
    top = [jnp.where(layer == LAYERS - 1, a, 0.0) for a in ends]
    load = [jnp.where(layer == 0, a, 0.0) for a in ends]
    cond_prior = prior(cond)
    diag = [guarded(p + c + vb + va + t) for p, c, vb, va, t in zip(cond_prior, cond, via_below, via, top)]
    rate = [damping / d for d in diag]

    def inflow(v):
        before, after = prior(v), later(v)
        return [
            cond_prior[i] * before[i]
            + cond[i] * after[i]
            + via_below[i] * pltpu.roll(v[i], ROWS, 1)
            + via[i] * pltpu.roll(v[i], LANES - ROWS, 1)
            + top[i] * supply_volts
            - load[i]
            for i in range(2)
        ]

    for _ in range(SWEEPS):
        num = inflow(volts)
        volts = [(1.0 - damping) * v + r * n for v, r, n in zip(volts, rate, num)]
    resid = inflow(volts)[0] - diag[0] * volts[0]
    sub = iota(tall, 0)
    inside = ((sub >= REACH) & (sub < 2 * REACH)) | ((sub >= STRIP + REACH) & (sub < STRIP + 2 * REACH))
    squares = jnp.where(inside, resid * resid, 0.0)
    after = later(volts)
    wind = [mobile[i] * wind_factor * (cond[i] * (volts[i] - after[i])) for i in range(2)]
    return turned(volts[0]), wind, squares


def strip_stress(dirs, even_y, even_x, own, gya, gyb, ma, mb, wind):
    stress, mobile = (strip_field(f, even_y, even_x, own, gya, gyb, ma, mb) for f in (4, 5))
    prior, later = strip_shifts(dirs)
    for _ in range(STEPS):
        after = later(stress)
        flux = [mobile[i] * (after[i] - stress[i]) + wind[i] for i in range(2)]
        back = prior(flux)
        stress = [stress[i] + flux[i] - back[i] for i in range(2)]
    return turned(stress[0])


def turned(value):
    middle = jnp.zeros((LANES - 2 * OWN, LANES), jnp.float32)
    whole = jnp.concatenate([value[REACH:STRIP], middle, value[STRIP : STRIP + OWN]], 0)
    return whole.T.reshape(LAYERS, ROWS, LANES)


def last_sweep(
    dirs, cond, prior, via, diag, pad, load, early, edges, gxa, gxb, own, gya, gyb, ma, mb,
    volts_o, sum_o, sides_o, wind_o, sums, near_left, near_right,
):
    gx, gy = position()
    even = gx % 2 == 0
    width = early.shape[2]
    slot = slots_of(dirs)

    def near(right, row):
        a, b = gxa[pl.ds(row, 1), :], gxb[pl.ds(row, 1), :]
        return jnp.where(even, a, b) if right else jnp.where(even, b, a)

    for j in range(width // LANES):
        start = FIELDS * STRIP + j * ROWS
        lanes = slice(j * LANES, (j + 1) * LANES)
        a, b = ma[start : start + ROWS], mb[start : start + ROWS]
        near_right[:, lanes] = jnp.where(even, a, b)
        near_left[:, lanes] = jnp.where(even, b, a)
    sums[...] = jnp.zeros_like(sums)

    for l in range(LAYERS):

        @pl.when(dirs[l] == 0)
        def _(l=l):
            v = early[l]
            row = iota(v.shape, 0)
            base, low = slot[l] * EDGE, slot[l] * 4
            v2_left, v2_right = near_left[pl.ds(low, 1), :], near_right[pl.ds(low, 1), :]
            extra = jnp.where(row == 0, prior[l] * v2_left, jnp.where(row == ROWS - 1, cond[l] * v2_right, 0.0))
            volts_o[l] = v + damping * extra / guarded(diag[l])
            last = cond[l, ROWS - 1 :, :]
            sides_o[0, pl.ds(low, 1), :] = (1.0 - damping) * v2_left + damping * (
                near_left[pl.ds(low + 1, 1), :] + near(False, base + 2) * edges[0, l : l + 1, :]
            ) / guarded(near(False, base + 11))
            sides_o[1, pl.ds(low, 1), :] = (1.0 - damping) * v2_right + damping * (
                near_right[pl.ds(low + 1, 1), :] + last * edges[1, l : l + 1, :]
            ) / guarded(near(True, base + 11) + last)
            for side, ref in enumerate((near_left, near_right)):
                sides_o[side, pl.ds(low + 1, 1), :] = ref[pl.ds(low + 2, 1), :]
                sides_o[side, pl.ds(low + 2, 1), :] = ref[pl.ds(low + 3, 1), :]

        @pl.when(dirs[l] == 1)
        def _(l=l):
            volts_o[l] = early[l]

    for l in range(LAYERS):

        def add(at, before, after, dim, l=l):
            v = volts_o[(l, *at)]
            first, second = shifted(v, dim, before, after)
            resid = (
                prior[(l, *at)] * first
                + cond[(l, *at)] * second
                + rest_of(l, at, volts_o, via, pad, load)
                - diag[(l, *at)] * v
            )
            col = at[1].start + iota(v.shape, 1)
            squares = jnp.where((col >= REACH) & (col < width - REACH), resid * resid, 0.0)
            total = jnp.zeros((8, LANES), jnp.float32)
            for r in range(0, v.shape[0], 8):
                for c in range(0, v.shape[1], LANES):
                    total = total + squares[r : r + 8, c : c + LANES]
            sums[...] += total

        @pl.when(dirs[l] == 0)
        def _(l=l):
            for at in blocks(width, False):
                low = pl.ds(slot[l] * 4, 1)
                add(at, sides_o[0, low, at[1]], sides_o[1, low, at[1]], 0)

        @pl.when(dirs[l] == 1)
        def _(l=l):
            for at in blocks(width, True):
                add(at, None, None, 1)

    strip_v, wind, squares = strips(dirs, gy % 2 == 0, even, own, gya, gyb, ma, mb)
    for i in range(2):
        wind_o[i] = wind[i]
    place(volts_o, strip_v)
    total = jnp.sum(sums[...]) + jnp.sum(squares)
    sum_o[...] = jnp.full(sum_o.shape, total, jnp.float32)


def place(ref, strip):
    width = ref.shape[2]
    lane = iota((1, 1, LANES), 2)
    ref[:, :, :LANES] = jnp.where(lane < REACH, strip, ref[:, :, :LANES])
    ref[:, :, width - LANES :] = jnp.where(lane >= LANES - REACH, strip, ref[:, :, width - LANES :])


def stress_steps(
    total_x, total_y, dirs, cond, volts, sides, stress, mob, blk, gxa, gxb, own, gya, gyb, ma, mb, wind_strip,
    stress_o, ext_c, ext_m, ext_v, ext_s,
):
    gx, gy = position()
    even = gx % 2 == 0
    width = volts.shape[2]
    slot = slots_of(dirs)

    def near(right, row):
        a, b = gxa[pl.ds(row, 1), :], gxb[pl.ds(row, 1), :]
        return jnp.where(even, a, b) if right else jnp.where(even, b, a)

    for ref in (ext_c, ext_m, ext_v, ext_s):
        ref[0:8] = jnp.zeros((8, width), jnp.float32)
        ref[24:32] = jnp.zeros((8, width), jnp.float32)

    for l in range(LAYERS):

        @pl.when(dirs[l] == 0)
        def _(l=l):
            base, low = slot[l] * EDGE, slot[l] * 4
            for i in range(3):
                ext_v[7 - i : 8 - i] = sides[0, pl.ds(low + i, 1), :]
                ext_v[24 + i : 25 + i] = sides[1, pl.ds(low + i, 1), :]
                for ref, first in ((ext_c, 0), (ext_m, 3), (ext_s, 6)):
                    ref[5 + i : 6 + i] = near(False, base + first + i)
                    ref[24 + i : 25 + i] = near(True, base + first + i)
            ext_v[8:24] = volts[l]
            ext_c[8:24] = cond[l]
            ext_m[8:24] = mob[l] * (1.0 - blk[l].astype(jnp.float32)) * inner_x(gx, total_x, (ROWS, width))
            ext_s[8:24] = stress[l]
            n = 32
            step = min(256, width)
            for start in range(0, width, step):
                lanes = slice(start, start + step)
                v, m, s = ext_v[:, lanes], ext_m[:, lanes], ext_s[:, lanes]
                wind = m * wind_factor * (ext_c[:, lanes] * (v - pltpu.roll(v, n - 1, 0)))
                for _ in range(STEPS):
                    flux = m * (pltpu.roll(s, n - 1, 0) - s) + wind
                    s = s + flux - pltpu.roll(flux, 1, 0)
                stress_o[l, :, lanes] = s[8:24]

        @pl.when(dirs[l] == 1)
        def _(l=l):
            for at in blocks(width, True):
                v, s = volts[(l, *at)], stress[(l, *at)]
                inner = inner_y(gy, total_y, (8, width))
                m = mob[(l, *at)] * (1.0 - blk[(l, *at)].astype(jnp.float32)) * inner
                wind = m * wind_factor * (cond[(l, *at)] * (v - pltpu.roll(v, width - 1, 1)))
                for _ in range(STEPS):
                    flux = m * (pltpu.roll(s, width - 1, 1) - s) + wind
                    s = s + flux - pltpu.roll(flux, 1, 1)
                stress_o[(l, *at)] = s

    wind = [wind_strip[0], wind_strip[1]]
    place(stress_o, strip_stress(dirs, gy % 2 == 0, even, own, gya, gyb, ma, mb, wind))


def call(kernel, ins, outs, scratch=(), scalars=1, copies=0, cost=0, aliases={}):
    smem, vmem = pl.BlockSpec(memory_space=pltpu.SMEM), pl.BlockSpec(memory_space=pltpu.VMEM)
    held = pl.BlockSpec(memory_space=pltpu.HBM) if copies else vmem
    scratch = [pltpu.VMEM(*(s if isinstance(s[0], tuple) else (s, jnp.float32))) for s in scratch]
    return pl.pallas_call(
        kernel,
        out_shape=[jax.ShapeDtypeStruct(s, jnp.float32) for s in outs],
        in_specs=[smem] * scalars + [held] * (len(ins) - scalars),
        out_specs=[vmem] * len(outs),
        input_output_aliases=aliases,
        scratch_shapes=scratch + ([pltpu.SemaphoreType.DMA((copies,))] if copies else []),
        compiler_params=pltpu.CompilerParams(vmem_limit_bytes=(57 if copies else 16) * 2**20),
        cost_estimate=pl.CostEstimate(flops=cost, bytes_accessed=cost, transcendentals=0),
    )(*ins)


def swap(value, axes, first):
    count = lax.axis_size(axes)
    pairs = [(i, i + 1) for i in range(first, count - 1, 2)]
    return lax.ppermute(value, axes, pairs + [(b, a) for a, b in pairs])


def partial_sum(held, out):
    total = held[0]
    for i in range(1, held.shape[0]):
        total = total + held[i]
    for i in range(out.shape[0]):
        out[i] = total


def root_mean(count, held, out):
    total = jnp.sum(held[...][:, :1, :1])
    out[...] = jnp.sqrt(jnp.full((1, LANES), total / count, jnp.float32))


def rms_all(held, count):
    got = lax.all_to_all(held, NEAR, 0, 0)
    (held,) = call(partial_sum, (got,), [(lax.axis_size(FAR), 1, LANES)], scalars=0)
    got = lax.all_to_all(held, FAR, 0, 0)
    (out,) = call(functools.partial(root_mean, count), (got,), [(1, LANES)], scalars=0)
    return out[0, 0]


def body(volts_start, seg_cond, via_cond, via_mask, pad_mask, load_current, stress_start, mobility, blocked, layer_dirs):
    layers, rows, width = seg_cond.shape
    total_x, total_y = rows * lax.axis_size(X), width * lax.axis_size(Y)
    shape = (layers, rows, width)
    fields = (volts_start, seg_cond, via_cond, via_mask, pad_mask, load_current, stress_start, mobility, blocked)
    column = (FIELDS, REACH, LANES)
    own, gya, gyb = call(
        functools.partial(pack_columns, total_x, total_y, width),
        (layer_dirs, *fields),
        [(2, FIELDS, OWN, LANES), column, column],
        scratch=[(a.shape[:-1] + (LANES,), a.dtype) for a in fields for _ in range(2)],
        copies=18,
    )
    gyb, gya = swap(gyb, Y, 1), swap(gya, Y, 0)
    own, fields = lax.optimization_barrier((own, fields))
    gxa, gxb = call(
        functools.partial(pack_rows, total_x),
        (layer_dirs, *fields),
        [(SLOTS * EDGE, width)] * 2,
        cost=COST_ROWS,
    )
    sent_a, sent_b = gxa, gxb
    gxa, gxb = swap(gxa, X, 0), swap(gxb, X, 1)
    side = (FIELDS * STRIP, LANES)
    sa, sb = call(pack_strips, (own, gyb, gya), [side, side], scalars=0, cost=COST_STRIPS)
    message = (FIELDS * STRIP + ROWS * (width // LANES), LANES)
    cond, prior, via, diag, rate = call(
        functools.partial(conductances, total_x, total_y),
        (layer_dirs, sent_a, sent_b, *fields[1:5]),
        [shape, shape, (layers - 1, rows, width), shape, shape],
        cost=COST_SETUP,
    )
    prior, diag, _, early, edges, ma, mb = call(
        early_sweeps,
        (layer_dirs, cond, prior, via, diag, rate, fields[0], *fields[4:6], gxa, gxb, sa, sb),
        [shape, shape, shape, shape, (2, layers, width), message, message],
        scratch=[shape, shape, (2, SLOTS, width), (ROWS, width), (ROWS, width)],
        cost=COST_EARLY,
        aliases={2: 0, 4: 1, 5: 2},
    )
    ma, mb = swap(ma, X, 0), swap(mb, X, 1)
    volts, held, sides, wind = call(
        last_sweep,
        (layer_dirs, cond, prior, via, diag, *fields[4:6], early, edges, gxa, gxb, own, gya, gyb, ma, mb),
        [shape, (lax.axis_size(NEAR), 1, LANES), (2, ROWS, width), (2, 2 * STRIP, LANES)],
        scratch=[(8, LANES), (ROWS, width), (ROWS, width)],
    )
    (stress,) = call(
        functools.partial(stress_steps, total_x, total_y),
        (layer_dirs, cond, volts, sides, *fields[6:], gxa, gxb, own, gya, gyb, ma, mb, wind),
        [shape],
        scratch=[(32, width)] * 4,
        cost=12 * 2**20,
    )
    resid_rms = rms_all(held, layers * total_x * total_y)
    return volts, stress, resid_rms


def solution(mesh):
    gx, gy = mesh.shape["gx"], mesh.shape["gy"]
    fine = jax.sharding.Mesh(mesh.devices.reshape(gx // 4, 4, gy // 4, 2, 2), X + Y)
    cells, plane = P(None, X, Y), P(X, Y)
    in_specs = (cells, cells, cells, cells, plane, plane, cells, cells, cells, P())
    return jax.shard_map(body, mesh=fine, in_specs=in_specs, out_specs=(cells, cells, P()), check_vma=False)
```

```python
import functools

import jax
import jax.numpy as jnp
from jax import lax
from jax.experimental import pallas as pl
from jax.experimental.pallas import tpu as pltpu
from jax.sharding import PartitionSpec as P

SWEEPS = 3
STEPS = 3
LAYERS = 8
ROWS = 16
LANES = 128
REACH = 8
OWN = 16
STRIP = REACH + OWN
SLOTS = 4
EDGE = 12
FIELDS = 6

COST_ROWS = 2**20
COST_STRIPS = 4000 * 2**20
COST_EARLY = 1024
COST_SETUP = 4 * 2**20

damping = 0.8
pad_conductance = 4.0
supply_volts = 1.0
wind_factor = 4.0

X = ("z_lo", "x")
Y = ("y", "z_hi", "core")
NEAR = ("x", "y", "core")
FAR = ("z_hi", "z_lo")


def position():
    out = []
    for axes in (X, Y):
        at = lax.axis_index(axes[0])
        for a in axes[1:]:
            at = at * lax.axis_size(a) + lax.axis_index(a)
        out.append(at)
    return out


def iota(shape, dim):
    return lax.broadcasted_iota(jnp.int32, shape, dim)


def lane_dirs(dirs, shape):
    layer = iota(shape, len(shape) - 1) // ROWS
    found = jnp.zeros(shape, jnp.int32)
    for l in range(LAYERS):
        found = jnp.where(layer == l, dirs[l], found)
    return found == 1


def slots_of(dirs):
    slot, count = [], jnp.int32(0)
    for l in range(LAYERS):
        slot.append(count)
        count = count + (1 - dirs[l])
    return slot


def fetch(sources, targets, sems):
    copies = [pltpu.make_async_copy(a, b, sems.at[i]) for i, (a, b) in enumerate(zip(sources, targets))]
    for copy in copies:
        copy.start()
    return copies


def pack_columns(total_x, total_y, width, dirs, *refs):
    given, (own_ref, a_ref, b_ref), ins, sems = refs[:9], refs[9:12], refs[12:30], refs[30]
    parts = []
    for ref in given:
        for lanes in (slice(0, LANES), slice(width - LANES, width)):
            parts.append(ref.at[(slice(None),) * (len(ref.shape) - 1) + (lanes,)])
    copies = fetch(parts, ins, sems)
    gx, gy = position()
    col = iota((1, 1, LANES), 2)

    def pick(i):
        for copy in copies[2 * i : 2 * i + 2]:
            copy.wait()
        first, last = ins[2 * i][...], ins[2 * i + 1][...]
        return jnp.where(col.reshape((1,) * (first.ndim - 1) + (LANES,)) < LANES // 2, first, last)

    def field(f):
        if f < 2:
            return pick(f)
        if f == 2:
            return jnp.concatenate([pick(2) * pick(3).astype(jnp.float32), none], 0)
        if f == 3:
            top, load = pad_conductance * pick(4).astype(jnp.float32), pick(5)
            return jnp.concatenate([load[None]] + [none] * (LAYERS - 2) + [top[None]], 0)
        if f == 4:
            return pick(6)
        return pick(7) * (1.0 - pick(8).astype(jnp.float32))

    none = jnp.zeros((1, ROWS, LANES), jnp.float32)
    shape = (OWN, LANES)
    along_y = lane_dirs(dirs, shape)
    x = gx * ROWS + iota(shape, 1) % ROWS
    even = gy % 2 == 0
    for f in range(FIELDS):
        turned = field(f).reshape(LANES, LANES).T
        pieces = []
        for side, start in enumerate((0, LANES - OWN)):
            piece = turned[start : start + OWN]
            if f in (1, 5):
                y = gy * width + (0 if side == 0 else width - OWN) + iota(shape, 0)
                inner = jnp.where(along_y, y, x) < jnp.where(along_y, total_y - 1, total_x - 1)
                piece = jnp.where(inner, piece, 0.0)
            own_ref[side, f] = piece
            pieces.append(piece)
        left, right = pieces[0][:REACH], pieces[1][OWN - REACH :]
        a_ref[f] = jnp.where(even, right, left)
        b_ref[f] = jnp.where(even, left, right)


def inner_x(gx, total_x, shape):
    return (gx * ROWS + iota(shape, 0) < total_x - 1).astype(jnp.float32)


def inner_y(gy, total_y, shape):
    return (gy * shape[1] + iota(shape, 1) < total_y - 1).astype(jnp.float32)


def pack_rows(total_x, dirs, volts, seg, via_cond, via_mask, pad, load, stress, mob, blk, a_ref, b_ref):
    gx, _ = position()
    even = gx % 2 == 0
    width = volts.shape[2]
    inner = inner_x(gx, total_x, (ROWS, width))
    slot = slots_of(dirs)
    for l in range(LAYERS):

        @pl.when(dirs[l] == 0)
        def _(l=l):
            cond = seg[l] * inner
            mobile = mob[l] * (1.0 - blk[l].astype(jnp.float32)) * inner
            held, s = volts[l], stress[l]
            out = []
            for edge in (ROWS - 1, 0):
                here = slice(edge, edge + 1)
                num = jnp.zeros((1, width), jnp.float32)
                diag = cond[here]
                if edge:
                    num = cond[edge - 1 : edge] * held[edge - 1 : edge]
                    diag = diag + cond[edge - 1 : edge]
                else:
                    num = cond[here] * held[1:2]
                if l > 0:
                    below = via_cond[l - 1, here] * via_mask[l - 1, here].astype(jnp.float32)
                    num, diag = num + below * volts[l - 1, here], diag + below
                if l < LAYERS - 1:
                    above = via_cond[l, here] * via_mask[l, here].astype(jnp.float32)
                    num, diag = num + above * volts[l + 1, here], diag + above
                if l == LAYERS - 1:
                    top = pad_conductance * pad[here].astype(jnp.float32)
                    num, diag = num + top * supply_volts, diag + top
                if l == 0:
                    num = num - load[here]
                three = slice(ROWS - 3, ROWS) if edge else slice(0, 3)
                out.append([cond[three], mobile[three], s[three], held[here], num, diag])
            base = slot[l] * EDGE
            at = 0
            for right, left in zip(*out):
                for i in range(right.shape[0]):
                    row = slice(i, i + 1)
                    a_ref[pl.ds(base + at, 1), :] = jnp.where(even, right[row], left[row])
                    b_ref[pl.ds(base + at, 1), :] = jnp.where(even, left[row], right[row])
                    at += 1


def guarded(diag):
    return jnp.where(diag == 0.0, 1.0, diag)


def blocks(width, along_y):
    if along_y:
        return [(slice(r, r + 8), slice(0, width)) for r in range(0, ROWS, 8)]
    step = min(512, width)
    return [(slice(0, ROWS), slice(c, c + step)) for c in range(0, width, step)]


def rest_of(l, at, v, via, pad, load):
    total = None
    if l > 0:
        total = via[(l - 1, *at)] * v[(l - 1, *at)]
    if l < LAYERS - 1:
        above = via[(l, *at)] * v[(l + 1, *at)]
        total = above if total is None else total + above
    if l == LAYERS - 1:
        total = total + pad_conductance * supply_volts * pad[at].astype(jnp.float32)
    if l == 0:
        total = total - load[at]
    return total


def shifted(value, dim, before, after):
    n = value.shape[dim]
    prior, later = pltpu.roll(value, 1, dim), pltpu.roll(value, n - 1, dim)
    if dim == 0:
        row = iota(value.shape, 0)
        if before is not None:
            prior = jnp.where(row == 0, before, prior)
            later = jnp.where(row == n - 1, after, later)
    return prior, later


def strip_pair(recv_a, recv_b, even, own, f):
    from_right = jnp.where(even, recv_a[f], recv_b[f])
    from_left = jnp.where(even, recv_b[f], recv_a[f])
    return (
        jnp.concatenate([from_left, own[0, f]], 0),
        jnp.concatenate([own[1, f], from_right], 0),
    )


def conductances(
    total_x, total_y, dirs, after_a, after_b, volts, seg, via_cond, via_mask, pad, load,
    cond_o, prior_o, via_o, diag_o, rate_o, volts_o,
):
    gx, gy = position()
    width = seg.shape[2]
    for l in range(LAYERS):
        if l < LAYERS - 1:
            via_o[l] = via_cond[l] * via_mask[l].astype(jnp.float32)

        @pl.when(dirs[l] == 0)
        def _(l=l):
            cond = seg[l] * inner_x(gx, total_x, (ROWS, width))
            cond_o[l] = cond
            prior_o[l] = shifted(cond, 0, 0.0, 0.0)[0]

        @pl.when(dirs[l] == 1)
        def _(l=l):
            cond = seg[l] * inner_y(gy, total_y, (ROWS, width))
            cond_o[l] = cond
            prior_o[l] = pltpu.roll(cond, 1, 1)

    for l in range(LAYERS):
        diag = cond_o[l] + prior_o[l]
        if l > 0:
            diag = diag + via_o[l - 1]
        if l < LAYERS - 1:
            diag = diag + via_o[l]
        else:
            diag = diag + pad_conductance * pad[...].astype(jnp.float32)
        diag_o[l] = diag
        rate_o[l] = damping / guarded(diag)

    for l in range(LAYERS):
        for along_y in (False, True):

            @pl.when(dirs[l] == int(along_y))
            def _(l=l, along_y=along_y):
                for at in blocks(width, along_y):
                    v = volts[(l, *at)]
                    prior, later = shifted(v, int(along_y), 0.0, 0.0)
                    num = prior_o[(l, *at)] * prior + cond_o[(l, *at)] * later + rest_of(l, at, volts, via_o, pad, load)
                    volts_o[(l, *at)] = (1.0 - damping) * v + rate_o[(l, *at)] * num


def early_sweeps(
    dirs, cond_o, prior_i, via_o, diag_i, rate_i, first_v, volts, pad, load, gxa, gxb, strips_a, strips_b,
    prior_o, diag_o, volts_o, edges_o, a_ref, b_ref, rate_o, one, two, halo, to_right, to_left,
):
    gx, gy = position()
    even = gx % 2 == 0
    width = volts.shape[2]
    slot = slots_of(dirs)

    def near(right, row, lanes=slice(None)):
        a, b = gxa[pl.ds(row, 1), lanes], gxb[pl.ds(row, 1), lanes]
        return jnp.where(even, a, b) if right else jnp.where(even, b, a)

    for l in range(LAYERS):

        one[l] = first_v[l]

        @pl.when(dirs[l] == 0)
        def _(l=l):
            base = slot[l] * EDGE
            before, after, cond_left = near(False, base + 9), near(True, base + 9), near(False, base + 2)
            v, last = volts[l], cond_o[l, ROWS - 1 :]
            prior_o[l], diag_o[l], rate_o[l] = prior_i[l], diag_i[l], rate_i[l]
            prior_o[l, :1] = cond_left
            diag = diag_i[l, :1] + cond_left
            diag_o[l, :1] = diag
            rate = damping / guarded(diag)
            rate_o[l, :1] = rate
            end = (slice(0, 1), slice(None))
            num = cond_left * before + cond_o[l, :1] * v[1:2] + rest_of(l, end, volts, via_o, pad, load)
            one[l, :1] = (1.0 - damping) * v[:1] + rate * num
            one[l, ROWS - 1 :] = first_v[l, ROWS - 1 :] + rate_i[l, ROWS - 1 :] * last * after
            halo[0, pl.ds(slot[l], 1), :] = (1.0 - damping) * before + damping * (
                near(False, base + 10) + cond_left * v[:1]
            ) / guarded(near(False, base + 11))
            halo[1, pl.ds(slot[l], 1), :] = (1.0 - damping) * after + damping * (
                near(True, base + 10) + last * v[ROWS - 1 :]
            ) / guarded(near(True, base + 11) + last)

    for sweep, (old, new) in ((1, (one, two)), (2, (two, volts_o))):
        for l in range(LAYERS):

            @pl.when(dirs[l] == 0)
            def _(l=l):
                for at in blocks(width, False):
                    lanes = at[1]
                    v = old[(l, *at)]
                    if sweep == 1:
                        before, after = halo[0, pl.ds(slot[l], 1), lanes], halo[1, pl.ds(slot[l], 1), lanes]
                    else:
                        before = after = 0.0
                    prior, later = shifted(v, 0, before, after)
                    num = prior_o[(l, *at)] * prior + cond_o[(l, *at)] * later + rest_of(l, at, old, via_o, pad, load)
                    result = (1.0 - damping) * v + rate_o[(l, *at)] * num
                    new[(l, *at)] = result
                    if sweep == 2:
                        edges_o[0, l : l + 1, lanes] = v[:1]
                        edges_o[1, l : l + 1, lanes] = v[ROWS - 1 :]
                        send = slot[l] * 4
                        for ref, e, d in ((to_right, ROWS - 1, -1), (to_left, 0, 1)):
                            ref[pl.ds(send, 1), lanes] = v[e : e + 1]
                            ref[pl.ds(send + 1, 1), lanes] = num[e : e + 1]
                            ref[pl.ds(send + 2, 1), lanes] = result[e + d : e + d + 1]
                            ref[pl.ds(send + 3, 1), lanes] = result[e + 2 * d : e + 2 * d + 1]

            @pl.when(dirs[l] == 1)
            def _(l=l):
                for at in blocks(width, True):
                    v = old[(l, *at)]
                    prior, later = shifted(v, 1, None, None)
                    num = prior_i[(l, *at)] * prior + cond_o[(l, *at)] * later + rest_of(l, at, old, via_o, pad, load)
                    new[(l, *at)] = (1.0 - damping) * v + rate_i[(l, *at)] * num
                    if sweep == 2:
                        edges_o[:, l : l + 1, :] = jnp.zeros((2, 1, width), jnp.float32)

    a_ref[: FIELDS * STRIP] = strips_a[...]
    b_ref[: FIELDS * STRIP] = strips_b[...]
    for j in range(width // LANES):
        start = FIELDS * STRIP + j * ROWS
        lanes = slice(j * LANES, (j + 1) * LANES)
        a_ref[start : start + ROWS] = jnp.where(even, to_right[:, lanes], to_left[:, lanes])
        b_ref[start : start + ROWS] = jnp.where(even, to_left[:, lanes], to_right[:, lanes])


def pack_strips(own, gyb, gya, a_ref, b_ref):
    gx, gy = position()
    even = gx % 2 == 0
    x = iota((STRIP, LANES), 1) % ROWS
    for f in range(FIELDS):
        left, right = strip_pair(gya, gyb, gy % 2 == 0, own, f)
        right_going = jnp.where(x >= 8, left, pltpu.roll(right, LANES - 8, 1))
        left_going = jnp.where(x < 8, left, pltpu.roll(right, 8, 1))
        a_ref[f * STRIP : (f + 1) * STRIP] = jnp.where(even, right_going, left_going)
        b_ref[f * STRIP : (f + 1) * STRIP] = jnp.where(even, left_going, right_going)


def strip_field(f, even_y, even_x, own, gya, gyb, ma, mb):
    x = iota((STRIP, LANES), 1) % ROWS
    left, right = strip_pair(gya, gyb, even_y, own, f)
    a, b = ma[f * STRIP : (f + 1) * STRIP], mb[f * STRIP : (f + 1) * STRIP]
    from_right, from_left = jnp.where(even_x, a, b), jnp.where(even_x, b, a)
    far_left = jnp.where(x >= 8, from_left, from_right)
    far_right = jnp.where(x >= 8, pltpu.roll(from_left, 8, 1), pltpu.roll(from_right, LANES - 8, 1))
    return jnp.concatenate([left, right], 0), jnp.concatenate([far_left, far_right], 0)


def strip_shifts(dirs):
    tall = (2 * STRIP, LANES)
    along_y = lane_dirs(dirs, tall)
    x = iota(tall, 1) % ROWS

    def later(pair):
        o, h = pair
        out = []
        for this, other in ((o, h), (h, o)):
            across = jnp.where(x == ROWS - 1, pltpu.roll(other, ROWS - 1, 1), pltpu.roll(this, LANES - 1, 1))
            out.append(jnp.where(along_y, pltpu.roll(this, tall[0] - 1, 0), across))
        return out

    def prior(pair):
        o, h = pair
        out = []
        for this, other in ((o, h), (h, o)):
            across = jnp.where(x == 0, pltpu.roll(other, LANES - ROWS + 1, 1), pltpu.roll(this, 1, 1))
            out.append(jnp.where(along_y, pltpu.roll(this, 1, 0), across))
        return out

    return prior, later


def strips(dirs, even_y, even_x, own, gya, gyb, ma, mb):
    tall = (2 * STRIP, LANES)
    layer = iota(tall, 1) // ROWS
    prior, later = strip_shifts(dirs)
    volts, cond, via, ends, mobile = (
        strip_field(f, even_y, even_x, own, gya, gyb, ma, mb) for f in (0, 1, 2, 3, 5)
    )
    via_below = [pltpu.roll(a, ROWS, 1) for a in via]
    top = [jnp.where(layer == LAYERS - 1, a, 0.0) for a in ends]
    load = [jnp.where(layer == 0, a, 0.0) for a in ends]
    cond_prior = prior(cond)
    diag = [guarded(p + c + vb + va + t) for p, c, vb, va, t in zip(cond_prior, cond, via_below, via, top)]
    rate = [damping / d for d in diag]

    def inflow(v):
        before, after = prior(v), later(v)
        return [
            cond_prior[i] * before[i]
            + cond[i] * after[i]
            + via_below[i] * pltpu.roll(v[i], ROWS, 1)
            + via[i] * pltpu.roll(v[i], LANES - ROWS, 1)
            + top[i] * supply_volts
            - load[i]
            for i in range(2)
        ]

    for _ in range(SWEEPS):
        num = inflow(volts)
        volts = [(1.0 - damping) * v + r * n for v, r, n in zip(volts, rate, num)]
    resid = inflow(volts)[0] - diag[0] * volts[0]
    sub = iota(tall, 0)
    inside = ((sub >= REACH) & (sub < 2 * REACH)) | ((sub >= STRIP + REACH) & (sub < STRIP + 2 * REACH))
    squares = jnp.where(inside, resid * resid, 0.0)
    after = later(volts)
    wind = [mobile[i] * wind_factor * (cond[i] * (volts[i] - after[i])) for i in range(2)]
    return volts[0], wind, squares


def strip_stress(dirs, even_y, even_x, own, gya, gyb, ma, mb, wind):
    stress, mobile = (strip_field(f, even_y, even_x, own, gya, gyb, ma, mb) for f in (4, 5))
    prior, later = strip_shifts(dirs)
    for _ in range(STEPS):
        after = later(stress)
        flux = [mobile[i] * (after[i] - stress[i]) + wind[i] for i in range(2)]
        back = prior(flux)
        stress = [stress[i] + flux[i] - back[i] for i in range(2)]
    return turned(stress[0])


def turned(value):
    middle = jnp.zeros((LANES - 2 * OWN, LANES), jnp.float32)
    whole = jnp.concatenate([value[REACH:STRIP], middle, value[STRIP : STRIP + OWN]], 0)
    return whole.T.reshape(LAYERS, ROWS, LANES)


def inner_residuals(
    dirs, cond, prior_x, prior_y, via, diag_x, diag_y, pad, load, early, sum_o, ends_o,
):
    width = early.shape[2]
    sum_o[...] = jnp.zeros_like(sum_o)
    for l in range(LAYERS):

        def add(along_y, prior, diag, l=l):
            for at in blocks(width, along_y):
                v = early[(l, *at)]
                first, second = shifted(v, int(along_y), 0.0, 0.0)
                resid = (
                    prior[(l, *at)] * first
                    + cond[(l, *at)] * second
                    + rest_of(l, at, early, via, pad, load)
                    - diag[(l, *at)] * v
                )
                row, col = at[0].start + iota(v.shape, 0), at[1].start + iota(v.shape, 1)
                inside = (col >= REACH) & (col < width - REACH) & (row >= 2) & (row < ROWS - 2)
                squares = jnp.where(inside, resid * resid, 0.0)
                total = jnp.zeros((8, LANES), jnp.float32)
                for r in range(0, v.shape[0], 8):
                    for c in range(0, v.shape[1], LANES):
                        total = total + squares[r : r + 8, c : c + LANES]
                sum_o[...] += total
                for i, r in enumerate((0, 1, ROWS - 2, ROWS - 1)):
                    if at[0].start <= r < at[0].stop:
                        ends_o[i, l : l + 1, at[1]] = resid[r - at[0].start : r - at[0].start + 1]

        here = slice(l, l + 1)
        if l < LAYERS - 1:
            ends_o[10, here], ends_o[11, here] = via[l, :1], via[l, ROWS - 1 :]
        else:
            ends_o[10, here] = ends_o[11, here] = jnp.zeros((1, width), jnp.float32)

        @pl.when(dirs[l] == 0)
        def _(l=l, add=add, here=here):
            add(False, prior_x, diag_x)
            ends_o[4, here], ends_o[5, here] = diag_x[l, :1], diag_x[l, ROWS - 1 :]
            ends_o[6, here], ends_o[7, here] = prior_x[l, :1], cond[l, ROWS - 1 :]
            ends_o[8, here], ends_o[9, here] = cond[l, :1], cond[l, ROWS - 2 : ROWS - 1]

        @pl.when(dirs[l] == 1)
        def _(l=l, add=add, here=here):
            add(True, prior_y, diag_y)
            ends_o[4, here], ends_o[5, here] = diag_y[l, :1], diag_y[l, ROWS - 1 :]
            for i in range(6, 10):
                ends_o[i, here] = jnp.zeros((1, width), jnp.float32)


def last_sweep(
    dirs, inner, ends, edges, gxa, gxb, own, gya, gyb, ma, mb,
    sum_o, sides_o, strip_o, near_left, near_right, second, third,
):
    gx, gy = position()
    even = gx % 2 == 0
    width = ends.shape[2]
    slot = slots_of(dirs)

    def near(right, row):
        a, b = gxa[pl.ds(row, 1), :], gxb[pl.ds(row, 1), :]
        return jnp.where(even, a, b) if right else jnp.where(even, b, a)

    for j in range(width // LANES):
        start = FIELDS * STRIP + j * ROWS
        lanes = slice(j * LANES, (j + 1) * LANES)
        a, b = ma[start : start + ROWS], mb[start : start + ROWS]
        near_right[:, lanes] = jnp.where(even, a, b)
        near_left[:, lanes] = jnp.where(even, b, a)
    second[...] = jnp.zeros_like(second)
    third[...] = jnp.zeros_like(third)
    for l in range(LAYERS):

        @pl.when(dirs[l] == 0)
        def _(l=l):
            base, low = slot[l] * EDGE, slot[l] * 4
            for side, ref in enumerate((near_left, near_right)):
                here = slice(l, l + 1)
                v2 = ref[pl.ds(low, 1), :]
                cond = ends[6 + side, here]
                diag = near(bool(side), base + 11)
                if side:
                    diag = diag + cond
                v3 = (1.0 - damping) * v2 + damping * (
                    ref[pl.ds(low + 1, 1), :] + cond * edges[side, here]
                ) / guarded(diag)
                second[side, here] = v2
                third[side, here] = v3
                sides_o[pl.ds(low + ROWS * side, 1), :] = v3
                sides_o[pl.ds(low + ROWS * side + 1, 1), :] = ref[pl.ds(low + 2, 1), :]
                sides_o[pl.ds(low + ROWS * side + 2, 1), :] = ref[pl.ds(low + 3, 1), :]

    total = inner[...]
    col = iota((LAYERS, width), 1)
    inside = (col >= REACH) & (col < width - REACH)
    for side in range(2):
        diag, cond, via = ends[4 + side], ends[6 + side], ends[10 + side]
        change = damping * cond * second[side] / guarded(diag)
        second[side] = change
        outer = (
            ends[3 * side]
            - diag * change
            + cond * third[side]
            + pltpu.roll(via, 1, 0) * pltpu.roll(change, 1, 0)
            + via * pltpu.roll(change, LAYERS - 1, 0)
        )
        next_in = ends[1 + side] + ends[8 + side] * change
        squares = jnp.where(inside, outer * outer + next_in * next_in, 0.0)
        for c in range(0, width, LANES):
            total = total + squares[:, c : c + LANES]
    for l in range(LAYERS):

        @pl.when(dirs[l] == 0)
        def _(l=l):
            for side in range(2):
                sides_o[pl.ds(slot[l] * 4 + ROWS * side + 3, 1), :] = second[side, l : l + 1]

    strip_v, wind, squares = strips(dirs, gy % 2 == 0, even, own, gya, gyb, ma, mb)
    for i, value in enumerate([strip_v] + wind):
        strip_o[2 * STRIP * i : 2 * STRIP * (i + 1)] = value
    for r in range(0, 2 * STRIP, 8):
        total = total + squares[r : r + 8]
    sum_o[...] = jnp.full(sum_o.shape, jnp.sum(total), jnp.float32)


def place(ref, strip):
    width = ref.shape[2]
    lane = iota((1, 1, LANES), 2)
    ref[:, :, :LANES] = jnp.where(lane < REACH, strip, ref[:, :, :LANES])
    ref[:, :, width - LANES :] = jnp.where(lane >= LANES - REACH, strip, ref[:, :, width - LANES :])


def stress_steps(
    total_x, total_y, dirs, cond, early, sides, stress, mob, blk, gxa, gxb, own, gya, gyb, ma, mb, strip,
    volts_o, stress_o, ext_c, ext_m, ext_v, ext_s,
):
    gx, gy = position()
    even = gx % 2 == 0
    width = early.shape[2]
    slot = slots_of(dirs)

    def near(right, row):
        a, b = gxa[pl.ds(row, 1), :], gxb[pl.ds(row, 1), :]
        return jnp.where(even, a, b) if right else jnp.where(even, b, a)

    for ref in (ext_c, ext_m, ext_v, ext_s):
        ref[0:8] = jnp.zeros((8, width), jnp.float32)
        ref[24:32] = jnp.zeros((8, width), jnp.float32)

    for l in range(LAYERS):

        @pl.when(dirs[l] == 0)
        def _(l=l):
            base, low = slot[l] * EDGE, slot[l] * 4
            for i in range(3):
                ext_v[7 - i : 8 - i] = sides[pl.ds(low + i, 1), :]
                ext_v[24 + i : 25 + i] = sides[pl.ds(low + ROWS + i, 1), :]
                for ref, first in ((ext_c, 0), (ext_m, 3), (ext_s, 6)):
                    ref[5 + i : 6 + i] = near(False, base + first + i)
                    ref[24 + i : 25 + i] = near(True, base + first + i)
            ext_v[8:24] = early[l]
            ext_v[8:9] = early[l, :1] + sides[pl.ds(low + 3, 1), :]
            ext_v[23:24] = early[l, ROWS - 1 :] + sides[pl.ds(low + ROWS + 3, 1), :]
            volts_o[l] = ext_v[8:24]
            ext_c[8:24] = cond[l]
            ext_m[8:24] = mob[l] * (1.0 - blk[l].astype(jnp.float32)) * inner_x(gx, total_x, (ROWS, width))
            ext_s[8:24] = stress[l]
            n = 32
            step = min(256, width)
            for start in range(0, width, step):
                lanes = slice(start, start + step)
                v, m, s = ext_v[:, lanes], ext_m[:, lanes], ext_s[:, lanes]
                wind = m * wind_factor * (ext_c[:, lanes] * (v - pltpu.roll(v, n - 1, 0)))
                for _ in range(STEPS):
                    flux = m * (pltpu.roll(s, n - 1, 0) - s) + wind
                    s = s + flux - pltpu.roll(flux, 1, 0)
                stress_o[l, :, lanes] = s[8:24]

        @pl.when(dirs[l] == 1)
        def _(l=l):
            for at in blocks(width, True):
                v, s = early[(l, *at)], stress[(l, *at)]
                volts_o[(l, *at)] = v
                inner = inner_y(gy, total_y, (8, width))
                m = mob[(l, *at)] * (1.0 - blk[(l, *at)].astype(jnp.float32)) * inner
                wind = m * wind_factor * (cond[(l, *at)] * (v - pltpu.roll(v, width - 1, 1)))
                for _ in range(STEPS):
                    flux = m * (pltpu.roll(s, width - 1, 1) - s) + wind
                    s = s + flux - pltpu.roll(flux, 1, 1)
                stress_o[(l, *at)] = s

    strip_v, *wind = (strip[2 * STRIP * i : 2 * STRIP * (i + 1)] for i in range(3))
    place(volts_o, turned(strip_v))
    place(stress_o, strip_stress(dirs, gy % 2 == 0, even, own, gya, gyb, ma, mb, wind))


def call(kernel, ins, outs, scratch=(), scalars=1, copies=0, cost=0):
    smem, vmem = pl.BlockSpec(memory_space=pltpu.SMEM), pl.BlockSpec(memory_space=pltpu.VMEM)
    held = pl.BlockSpec(memory_space=pltpu.HBM) if copies else vmem
    scratch = [pltpu.VMEM(*(s if isinstance(s[0], tuple) else (s, jnp.float32))) for s in scratch]
    return pl.pallas_call(
        kernel,
        out_shape=[jax.ShapeDtypeStruct(s, jnp.float32) for s in outs],
        in_specs=[smem] * scalars + [held] * (len(ins) - scalars),
        out_specs=[vmem] * len(outs),
        scratch_shapes=scratch + ([pltpu.SemaphoreType.DMA((copies,))] if copies else []),
        compiler_params=pltpu.CompilerParams(vmem_limit_bytes=(57 if copies else 16) * 2**20),
        cost_estimate=pl.CostEstimate(flops=cost, bytes_accessed=cost, transcendentals=0),
    )(*ins)


def swap(value, axes, first):
    count = lax.axis_size(axes)
    pairs = [(i, i + 1) for i in range(first, count - 1, 2)]
    return lax.ppermute(value, axes, pairs + [(b, a) for a, b in pairs])


def partial_sum(held, out):
    total = held[0]
    for i in range(1, held.shape[0]):
        total = total + held[i]
    for i in range(out.shape[0]):
        out[i] = total


def root_mean(count, held, out):
    total = jnp.sum(held[...][:, :1, :1])
    out[...] = jnp.sqrt(jnp.full((1, LANES), total / count, jnp.float32))


def rms_all(held, count):
    got = lax.all_to_all(held, NEAR, 0, 0)
    (held,) = call(partial_sum, (got,), [(lax.axis_size(FAR), 1, LANES)], scalars=0)
    got = lax.all_to_all(held, FAR, 0, 0)
    (out,) = call(functools.partial(root_mean, count), (got,), [(1, LANES)], scalars=0)
    return out[0, 0]


def body(volts_start, seg_cond, via_cond, via_mask, pad_mask, load_current, stress_start, mobility, blocked, layer_dirs):
    layers, rows, width = seg_cond.shape
    total_x, total_y = rows * lax.axis_size(X), width * lax.axis_size(Y)
    shape = (layers, rows, width)
    fields = (volts_start, seg_cond, via_cond, via_mask, pad_mask, load_current, stress_start, mobility, blocked)
    column = (FIELDS, REACH, LANES)
    own, gya, gyb = call(
        functools.partial(pack_columns, total_x, total_y, width),
        (layer_dirs, *fields),
        [(2, FIELDS, OWN, LANES), column, column],
        scratch=[(a.shape[:-1] + (LANES,), a.dtype) for a in fields for _ in range(2)],
        copies=18,
    )
    gyb, gya = swap(gyb, Y, 1), swap(gya, Y, 0)
    own, fields = lax.optimization_barrier((own, fields))
    gxa, gxb = call(
        functools.partial(pack_rows, total_x),
        (layer_dirs, *fields),
        [(SLOTS * EDGE, width)] * 2,
        cost=COST_ROWS,
    )
    sent_a, sent_b = gxa, gxb
    gxa, gxb = swap(gxa, X, 0), swap(gxb, X, 1)
    side = (FIELDS * STRIP, LANES)
    sa, sb = call(pack_strips, (own, gyb, gya), [side, side], scalars=0, cost=COST_STRIPS)
    message = (FIELDS * STRIP + ROWS * (width // LANES), LANES)
    cond, prior_y, via, diag_y, rate, first = call(
        functools.partial(conductances, total_x, total_y),
        (layer_dirs, sent_a, sent_b, *fields[:6]),
        [shape, shape, (layers - 1, rows, width), shape, shape, shape],
        cost=COST_SETUP,
    )
    prior_x, diag_x, early, edges, ma, mb = call(
        early_sweeps,
        (layer_dirs, cond, prior_y, via, diag_y, rate, first, fields[0], *fields[4:6], gxa, gxb, sa, sb),
        [shape, shape, shape, (2, layers, width), message, message],
        scratch=[shape, shape, shape, (2, SLOTS, width), (ROWS, width), (ROWS, width)],
        cost=COST_EARLY,
    )
    ma, mb = swap(ma, X, 0), swap(mb, X, 1)
    inner, ends = call(
        inner_residuals,
        (layer_dirs, cond, prior_x, prior_y, via, diag_x, diag_y, *fields[4:6], early),
        [(8, LANES), (12, layers, width)],
        cost=COST_SETUP,
    )
    held, sides, strip = call(
        last_sweep,
        (layer_dirs, inner, ends, edges, gxa, gxb, own, gya, gyb, ma, mb),
        [(lax.axis_size(NEAR), 1, LANES), (2 * ROWS, width), (6 * STRIP, LANES)],
        scratch=[(ROWS, width), (ROWS, width), (2, layers, width), (2, layers, width)],
    )
    volts, stress = call(
        functools.partial(stress_steps, total_x, total_y),
        (layer_dirs, cond, early, sides, *fields[6:], gxa, gxb, own, gya, gyb, ma, mb, strip),
        [shape, shape],
        scratch=[(32, width)] * 4,
        cost=12 * 2**20,
    )
    resid_rms = rms_all(held, layers * total_x * total_y)
    return volts, stress, resid_rms


def solution(mesh):
    gx, gy = mesh.shape["gx"], mesh.shape["gy"]
    fine = jax.sharding.Mesh(mesh.devices.reshape(gx // 4, 4, gy // 4, 2, 2), X + Y)
    cells, plane = P(None, X, Y), P(X, Y)
    in_specs = (cells, cells, cells, cells, plane, plane, cells, cells, cells, P())
    return jax.shard_map(body, mesh=fine, in_specs=in_specs, out_specs=(cells, cells, P()), check_vma=False)
```

```python
import functools

import jax
import jax.numpy as jnp
from jax import lax
from jax.experimental import pallas as pl
from jax.experimental.pallas import tpu as pltpu
from jax.sharding import PartitionSpec as P

SWEEPS = 3
STEPS = 3
LAYERS = 8
ROWS = 16
LANES = 128
REACH = 8
OWN = 16
STRIP = REACH + OWN
SLOTS = 4
EDGE = 12
FIELDS = 6

COST_ROWS = 2**20
COST_STRIPS = 4000 * 2**20
COST_EARLY = 1024
COST_SETUP = 4 * 2**20

damping = 0.8
pad_conductance = 4.0
supply_volts = 1.0
wind_factor = 4.0

X = ("z_lo", "x")
Y = ("y", "z_hi", "core")
NEAR = ("x", "y", "core")
FAR = ("z_hi", "z_lo")


def position():
    out = []
    for axes in (X, Y):
        at = lax.axis_index(axes[0])
        for a in axes[1:]:
            at = at * lax.axis_size(a) + lax.axis_index(a)
        out.append(at)
    return out


def iota(shape, dim):
    return lax.broadcasted_iota(jnp.int32, shape, dim)


def lane_dirs(dirs, shape):
    layer = iota(shape, len(shape) - 1) // ROWS
    found = jnp.zeros(shape, jnp.int32)
    for l in range(LAYERS):
        found = jnp.where(layer == l, dirs[l], found)
    return found == 1


def slots_of(dirs):
    slot, count = [], jnp.int32(0)
    for l in range(LAYERS):
        slot.append(count)
        count = count + (1 - dirs[l])
    return slot


def fetch(sources, targets, sems):
    copies = [pltpu.make_async_copy(a, b, sems.at[i]) for i, (a, b) in enumerate(zip(sources, targets))]
    for copy in copies:
        copy.start()
    return copies


def pack_columns(total_x, total_y, width, dirs, *refs):
    given, (own_ref, a_ref, b_ref), ins, sems = refs[:9], refs[9:12], refs[12:30], refs[30]
    parts = []
    for ref in given:
        for lanes in (slice(0, LANES), slice(width - LANES, width)):
            parts.append(ref.at[(slice(None),) * (len(ref.shape) - 1) + (lanes,)])
    copies = fetch(parts, ins, sems)
    gx, gy = position()
    col = iota((1, 1, LANES), 2)

    def pick(i):
        for copy in copies[2 * i : 2 * i + 2]:
            copy.wait()
        first, last = ins[2 * i][...], ins[2 * i + 1][...]
        return jnp.where(col.reshape((1,) * (first.ndim - 1) + (LANES,)) < LANES // 2, first, last)

    def field(f):
        if f < 2:
            return pick(f)
        if f == 2:
            return jnp.concatenate([pick(2) * pick(3).astype(jnp.float32), none], 0)
        if f == 3:
            top, load = pad_conductance * pick(4).astype(jnp.float32), pick(5)
            return jnp.concatenate([load[None]] + [none] * (LAYERS - 2) + [top[None]], 0)
        if f == 4:
            return pick(6)
        return pick(7) * (1.0 - pick(8).astype(jnp.float32))

    none = jnp.zeros((1, ROWS, LANES), jnp.float32)
    shape = (OWN, LANES)
    along_y = lane_dirs(dirs, shape)
    x = gx * ROWS + iota(shape, 1) % ROWS
    even = gy % 2 == 0
    for f in range(FIELDS):
        turned = field(f).reshape(LANES, LANES).T
        pieces = []
        for side, start in enumerate((0, LANES - OWN)):
            piece = turned[start : start + OWN]
            if f in (1, 5):
                y = gy * width + (0 if side == 0 else width - OWN) + iota(shape, 0)
                inner = jnp.where(along_y, y, x) < jnp.where(along_y, total_y - 1, total_x - 1)
                piece = jnp.where(inner, piece, 0.0)
            own_ref[side, f] = piece
            pieces.append(piece)
        left, right = pieces[0][:REACH], pieces[1][OWN - REACH :]
        a_ref[f] = jnp.where(even, right, left)
        b_ref[f] = jnp.where(even, left, right)


def inner_x(gx, total_x, shape):
    return (gx * ROWS + iota(shape, 0) < total_x - 1).astype(jnp.float32)


def inner_y(gy, total_y, shape):
    return (gy * shape[1] + iota(shape, 1) < total_y - 1).astype(jnp.float32)


def pack_rows(total_x, dirs, volts, seg, via_cond, via_mask, pad, load, stress, mob, blk, a_ref, b_ref):
    gx, _ = position()
    even = gx % 2 == 0
    width = volts.shape[2]
    inner = inner_x(gx, total_x, (ROWS, width))
    slot = slots_of(dirs)
    for l in range(LAYERS):

        @pl.when(dirs[l] == 0)
        def _(l=l):
            cond = seg[l] * inner
            mobile = mob[l] * (1.0 - blk[l].astype(jnp.float32)) * inner
            held, s = volts[l], stress[l]
            out = []
            for edge in (ROWS - 1, 0):
                here = slice(edge, edge + 1)
                num = jnp.zeros((1, width), jnp.float32)
                diag = cond[here]
                if edge:
                    num = cond[edge - 1 : edge] * held[edge - 1 : edge]
                    diag = diag + cond[edge - 1 : edge]
                else:
                    num = cond[here] * held[1:2]
                if l > 0:
                    below = via_cond[l - 1, here] * via_mask[l - 1, here].astype(jnp.float32)
                    num, diag = num + below * volts[l - 1, here], diag + below
                if l < LAYERS - 1:
                    above = via_cond[l, here] * via_mask[l, here].astype(jnp.float32)
                    num, diag = num + above * volts[l + 1, here], diag + above
                if l == LAYERS - 1:
                    top = pad_conductance * pad[here].astype(jnp.float32)
                    num, diag = num + top * supply_volts, diag + top
                if l == 0:
                    num = num - load[here]
                three = slice(ROWS - 3, ROWS) if edge else slice(0, 3)
                out.append([cond[three], mobile[three], s[three], held[here], num, diag])
            base = slot[l] * EDGE
            at = 0
            for right, left in zip(*out):
                for i in range(right.shape[0]):
                    row = slice(i, i + 1)
                    a_ref[pl.ds(base + at, 1), :] = jnp.where(even, right[row], left[row])
                    b_ref[pl.ds(base + at, 1), :] = jnp.where(even, left[row], right[row])
                    at += 1


def guarded(diag):
    return jnp.where(diag == 0.0, 1.0, diag)


def blocks(width, along_y):
    if along_y:
        return [(slice(r, r + 8), slice(0, width)) for r in range(0, ROWS, 8)]
    step = min(512, width)
    return [(slice(0, ROWS), slice(c, c + step)) for c in range(0, width, step)]


def rest_of(l, at, v, via, pad, load):
    total = None
    if l > 0:
        total = via[(l - 1, *at)] * v[(l - 1, *at)]
    if l < LAYERS - 1:
        above = via[(l, *at)] * v[(l + 1, *at)]
        total = above if total is None else total + above
    if l == LAYERS - 1:
        total = total + pad_conductance * supply_volts * pad[at].astype(jnp.float32)
    if l == 0:
        total = total - load[at]
    return total


def shifted(value, dim, before, after):
    n = value.shape[dim]
    prior, later = pltpu.roll(value, 1, dim), pltpu.roll(value, n - 1, dim)
    if dim == 0:
        row = iota(value.shape, 0)
        if before is not None:
            prior = jnp.where(row == 0, before, prior)
            later = jnp.where(row == n - 1, after, later)
    return prior, later


def strip_pair(recv_a, recv_b, even, own, f):
    from_right = jnp.where(even, recv_a[f], recv_b[f])
    from_left = jnp.where(even, recv_b[f], recv_a[f])
    return (
        jnp.concatenate([from_left, own[0, f]], 0),
        jnp.concatenate([own[1, f], from_right], 0),
    )


def conductances(
    total_x, total_y, dirs, after_a, after_b, volts, seg, via_cond, via_mask, pad, load,
    cond_o, prior_o, via_o, diag_o, rate_o, volts_o,
):
    gx, gy = position()
    width = seg.shape[2]
    for l in range(LAYERS):
        if l < LAYERS - 1:
            via_o[l] = via_cond[l] * via_mask[l].astype(jnp.float32)

        @pl.when(dirs[l] == 0)
        def _(l=l):
            cond = seg[l] * inner_x(gx, total_x, (ROWS, width))
            cond_o[l] = cond
            prior_o[l] = shifted(cond, 0, 0.0, 0.0)[0]

        @pl.when(dirs[l] == 1)
        def _(l=l):
            cond = seg[l] * inner_y(gy, total_y, (ROWS, width))
            cond_o[l] = cond
            prior_o[l] = pltpu.roll(cond, 1, 1)

    for l in range(LAYERS):
        diag = cond_o[l] + prior_o[l]
        if l > 0:
            diag = diag + via_o[l - 1]
        if l < LAYERS - 1:
            diag = diag + via_o[l]
        else:
            diag = diag + pad_conductance * pad[...].astype(jnp.float32)
        diag_o[l] = diag
        rate_o[l] = damping / guarded(diag)

    for l in range(LAYERS):
        for along_y in (False, True):

            @pl.when(dirs[l] == int(along_y))
            def _(l=l, along_y=along_y):
                for at in blocks(width, along_y):
                    v = volts[(l, *at)]
                    prior, later = shifted(v, int(along_y), 0.0, 0.0)
                    num = prior_o[(l, *at)] * prior + cond_o[(l, *at)] * later + rest_of(l, at, volts, via_o, pad, load)
                    volts_o[(l, *at)] = (1.0 - damping) * v + rate_o[(l, *at)] * num


def early_sweeps(
    dirs, cond_o, prior_i, via_o, diag_i, rate_i, first_v, volts, pad, load, gxa, gxb, strips_a, strips_b,
    prior_o, diag_o, volts_o, edges_o, a_ref, b_ref, rate_o, one, two, halo, to_right, to_left,
):
    gx, gy = position()
    even = gx % 2 == 0
    width = volts.shape[2]
    slot = slots_of(dirs)

    def near(right, row, lanes=slice(None)):
        a, b = gxa[pl.ds(row, 1), lanes], gxb[pl.ds(row, 1), lanes]
        return jnp.where(even, a, b) if right else jnp.where(even, b, a)

    for l in range(LAYERS):

        one[l] = first_v[l]

        @pl.when(dirs[l] == 0)
        def _(l=l):
            base = slot[l] * EDGE
            before, after, cond_left = near(False, base + 9), near(True, base + 9), near(False, base + 2)
            v, last = volts[l], cond_o[l, ROWS - 1 :]
            prior_o[l], diag_o[l], rate_o[l] = prior_i[l], diag_i[l], rate_i[l]
            prior_o[l, :1] = cond_left
            diag = diag_i[l, :1] + cond_left
            diag_o[l, :1] = diag
            rate = damping / guarded(diag)
            rate_o[l, :1] = rate
            end = (slice(0, 1), slice(None))
            num = cond_left * before + cond_o[l, :1] * v[1:2] + rest_of(l, end, volts, via_o, pad, load)
            one[l, :1] = (1.0 - damping) * v[:1] + rate * num
            one[l, ROWS - 1 :] = first_v[l, ROWS - 1 :] + rate_i[l, ROWS - 1 :] * last * after
            halo[0, pl.ds(slot[l], 1), :] = (1.0 - damping) * before + damping * (
                near(False, base + 10) + cond_left * v[:1]
            ) / guarded(near(False, base + 11))
            halo[1, pl.ds(slot[l], 1), :] = (1.0 - damping) * after + damping * (
                near(True, base + 10) + last * v[ROWS - 1 :]
            ) / guarded(near(True, base + 11) + last)

    for sweep, (old, new) in ((1, (one, two)), (2, (two, volts_o))):
        for l in range(LAYERS):

            @pl.when(dirs[l] == 0)
            def _(l=l):
                for at in blocks(width, False):
                    lanes = at[1]
                    v = old[(l, *at)]
                    if sweep == 1:
                        before, after = halo[0, pl.ds(slot[l], 1), lanes], halo[1, pl.ds(slot[l], 1), lanes]
                    else:
                        before = after = 0.0
                    prior, later = shifted(v, 0, before, after)
                    num = prior_o[(l, *at)] * prior + cond_o[(l, *at)] * later + rest_of(l, at, old, via_o, pad, load)
                    result = (1.0 - damping) * v + rate_o[(l, *at)] * num
                    new[(l, *at)] = result
                    if sweep == 2:
                        edges_o[0, l : l + 1, lanes] = v[:1]
                        edges_o[1, l : l + 1, lanes] = v[ROWS - 1 :]
                        send = slot[l] * 4
                        for ref, e, d in ((to_right, ROWS - 1, -1), (to_left, 0, 1)):
                            ref[pl.ds(send, 1), lanes] = v[e : e + 1]
                            ref[pl.ds(send + 1, 1), lanes] = num[e : e + 1]
                            ref[pl.ds(send + 2, 1), lanes] = result[e + d : e + d + 1]
                            ref[pl.ds(send + 3, 1), lanes] = result[e + 2 * d : e + 2 * d + 1]

            @pl.when(dirs[l] == 1)
            def _(l=l):
                for at in blocks(width, True):
                    v = old[(l, *at)]
                    prior, later = shifted(v, 1, None, None)
                    num = prior_i[(l, *at)] * prior + cond_o[(l, *at)] * later + rest_of(l, at, old, via_o, pad, load)
                    new[(l, *at)] = (1.0 - damping) * v + rate_i[(l, *at)] * num
                    if sweep == 2:
                        edges_o[:, l : l + 1, :] = jnp.zeros((2, 1, width), jnp.float32)

    a_ref[: SENT] = strips_a[...]
    b_ref[: SENT] = strips_b[...]
    for j in range(width // LANES):
        start = SENT + j * ROWS
        lanes = slice(j * LANES, (j + 1) * LANES)
        a_ref[start : start + ROWS] = jnp.where(even, to_right[:, lanes], to_left[:, lanes])
        b_ref[start : start + ROWS] = jnp.where(even, to_left[:, lanes], to_right[:, lanes])


def strip_rows(f):
    if f < 4:
        return slice(f * STRIP, (f + 1) * STRIP), slice(0, STRIP)
    start = 4 * STRIP + (f - 4) * REACH
    return slice(start, start + REACH), slice(REACH, 2 * REACH)


SENT = strip_rows(FIELDS - 1)[0].stop


def pack_strips(own, gyb, gya, a_ref, b_ref):
    gx, gy = position()
    even = gx % 2 == 0
    x = iota((STRIP, LANES), 1) % ROWS
    for f in range(FIELDS):
        left, right = strip_pair(gya, gyb, gy % 2 == 0, own, f)
        right_going = jnp.where(x >= 8, left, pltpu.roll(right, LANES - 8, 1))
        left_going = jnp.where(x < 8, left, pltpu.roll(right, 8, 1))
        to, rows = strip_rows(f)
        a_ref[to] = jnp.where(even, right_going, left_going)[rows]
        b_ref[to] = jnp.where(even, left_going, right_going)[rows]


def strip_field(f, even_y, even_x, own, gya, gyb, ma, mb):
    x = iota((STRIP, LANES), 1) % ROWS
    left, right = strip_pair(gya, gyb, even_y, own, f)
    at, rows = strip_rows(f)
    a, b = ma[at], mb[at]
    if rows.start:
        none = jnp.zeros((REACH, LANES), jnp.float32)
        a, b = jnp.concatenate([none, a, none], 0), jnp.concatenate([none, b, none], 0)
    from_right, from_left = jnp.where(even_x, a, b), jnp.where(even_x, b, a)
    far_left = jnp.where(x >= 8, from_left, from_right)
    far_right = jnp.where(x >= 8, pltpu.roll(from_left, 8, 1), pltpu.roll(from_right, LANES - 8, 1))
    return jnp.concatenate([left, right], 0), jnp.concatenate([far_left, far_right], 0)


def strip_shifts(dirs):
    tall = (2 * STRIP, LANES)
    along_y = lane_dirs(dirs, tall)
    x = iota(tall, 1) % ROWS

    def later(pair):
        o, h = pair
        out = []
        for this, other in ((o, h), (h, o)):
            across = jnp.where(x == ROWS - 1, pltpu.roll(other, ROWS - 1, 1), pltpu.roll(this, LANES - 1, 1))
            out.append(jnp.where(along_y, pltpu.roll(this, tall[0] - 1, 0), across))
        return out

    def prior(pair):
        o, h = pair
        out = []
        for this, other in ((o, h), (h, o)):
            across = jnp.where(x == 0, pltpu.roll(other, LANES - ROWS + 1, 1), pltpu.roll(this, 1, 1))
            out.append(jnp.where(along_y, pltpu.roll(this, 1, 0), across))
        return out

    return prior, later


def strips(dirs, even_y, even_x, own, gya, gyb, ma, mb):
    tall = (2 * STRIP, LANES)
    layer = iota(tall, 1) // ROWS
    prior, later = strip_shifts(dirs)
    volts, cond, via, ends, mobile = (
        strip_field(f, even_y, even_x, own, gya, gyb, ma, mb) for f in (0, 1, 2, 3, 5)
    )
    via_below = [pltpu.roll(a, ROWS, 1) for a in via]
    top = [jnp.where(layer == LAYERS - 1, a, 0.0) for a in ends]
    load = [jnp.where(layer == 0, a, 0.0) for a in ends]
    cond_prior = prior(cond)
    diag = [guarded(p + c + vb + va + t) for p, c, vb, va, t in zip(cond_prior, cond, via_below, via, top)]
    rate = [damping / d for d in diag]

    def inflow(v):
        before, after = prior(v), later(v)
        return [
            cond_prior[i] * before[i]
            + cond[i] * after[i]
            + via_below[i] * pltpu.roll(v[i], ROWS, 1)
            + via[i] * pltpu.roll(v[i], LANES - ROWS, 1)
            + top[i] * supply_volts
            - load[i]
            for i in range(2)
        ]

    for _ in range(SWEEPS):
        num = inflow(volts)
        volts = [(1.0 - damping) * v + r * n for v, r, n in zip(volts, rate, num)]
    resid = inflow(volts)[0] - diag[0] * volts[0]
    sub = iota(tall, 0)
    inside = ((sub >= REACH) & (sub < 2 * REACH)) | ((sub >= STRIP + REACH) & (sub < STRIP + 2 * REACH))
    squares = jnp.where(inside, resid * resid, 0.0)
    after = later(volts)
    wind = [mobile[i] * wind_factor * (cond[i] * (volts[i] - after[i])) for i in range(2)]
    return volts[0], wind, squares


def strip_stress(dirs, even_y, even_x, own, gya, gyb, ma, mb, wind):
    stress, mobile = (strip_field(f, even_y, even_x, own, gya, gyb, ma, mb) for f in (4, 5))
    prior, later = strip_shifts(dirs)
    for _ in range(STEPS):
        after = later(stress)
        flux = [mobile[i] * (after[i] - stress[i]) + wind[i] for i in range(2)]
        back = prior(flux)
        stress = [stress[i] + flux[i] - back[i] for i in range(2)]
    return turned(stress[0])


def turned(value):
    middle = jnp.zeros((LANES - 2 * OWN, LANES), jnp.float32)
    whole = jnp.concatenate([value[REACH:STRIP], middle, value[STRIP : STRIP + OWN]], 0)
    return whole.T.reshape(LAYERS, ROWS, LANES)


def inner_residuals(
    dirs, cond, prior_x, prior_y, via, diag_x, diag_y, pad, load, early, sum_o, ends_o,
):
    width = early.shape[2]
    sum_o[...] = jnp.zeros_like(sum_o)
    for l in range(LAYERS):

        def add(along_y, prior, diag, l=l):
            for at in blocks(width, along_y):
                v = early[(l, *at)]
                first, second = shifted(v, int(along_y), 0.0, 0.0)
                resid = (
                    prior[(l, *at)] * first
                    + cond[(l, *at)] * second
                    + rest_of(l, at, early, via, pad, load)
                    - diag[(l, *at)] * v
                )
                row, col = at[0].start + iota(v.shape, 0), at[1].start + iota(v.shape, 1)
                inside = (col >= REACH) & (col < width - REACH) & (row >= 2) & (row < ROWS - 2)
                squares = jnp.where(inside, resid * resid, 0.0)
                total = jnp.zeros((8, LANES), jnp.float32)
                for r in range(0, v.shape[0], 8):
                    for c in range(0, v.shape[1], LANES):
                        total = total + squares[r : r + 8, c : c + LANES]
                sum_o[...] += total
                for i, r in enumerate((0, 1, ROWS - 2, ROWS - 1)):
                    if at[0].start <= r < at[0].stop:
                        ends_o[i, l : l + 1, at[1]] = resid[r - at[0].start : r - at[0].start + 1]

        here = slice(l, l + 1)
        if l < LAYERS - 1:
            ends_o[10, here], ends_o[11, here] = via[l, :1], via[l, ROWS - 1 :]
        else:
            ends_o[10, here] = ends_o[11, here] = jnp.zeros((1, width), jnp.float32)

        @pl.when(dirs[l] == 0)
        def _(l=l, add=add, here=here):
            add(False, prior_x, diag_x)
            ends_o[4, here], ends_o[5, here] = diag_x[l, :1], diag_x[l, ROWS - 1 :]
            ends_o[6, here], ends_o[7, here] = prior_x[l, :1], cond[l, ROWS - 1 :]
            ends_o[8, here], ends_o[9, here] = cond[l, :1], cond[l, ROWS - 2 : ROWS - 1]

        @pl.when(dirs[l] == 1)
        def _(l=l, add=add, here=here):
            add(True, prior_y, diag_y)
            ends_o[4, here], ends_o[5, here] = diag_y[l, :1], diag_y[l, ROWS - 1 :]
            for i in range(6, 10):
                ends_o[i, here] = jnp.zeros((1, width), jnp.float32)


def last_sweep(
    dirs, inner, ends, edges, gxa, gxb, own, gya, gyb, ma, mb,
    sum_o, sides_o, near_left, near_right, second, third,
):
    gx, gy = position()
    even = gx % 2 == 0
    width = ends.shape[2]
    slot = slots_of(dirs)

    def near(right, row):
        a, b = gxa[pl.ds(row, 1), :], gxb[pl.ds(row, 1), :]
        return jnp.where(even, a, b) if right else jnp.where(even, b, a)

    for j in range(width // LANES):
        start = SENT + j * ROWS
        lanes = slice(j * LANES, (j + 1) * LANES)
        a, b = ma[start : start + ROWS], mb[start : start + ROWS]
        near_right[:, lanes] = jnp.where(even, a, b)
        near_left[:, lanes] = jnp.where(even, b, a)
    second[...] = jnp.zeros_like(second)
    third[...] = jnp.zeros_like(third)
    for l in range(LAYERS):

        @pl.when(dirs[l] == 0)
        def _(l=l):
            base, low = slot[l] * EDGE, slot[l] * 4
            for side, ref in enumerate((near_left, near_right)):
                here = slice(l, l + 1)
                v2 = ref[pl.ds(low, 1), :]
                cond = ends[6 + side, here]
                diag = near(bool(side), base + 11)
                if side:
                    diag = diag + cond
                v3 = (1.0 - damping) * v2 + damping * (
                    ref[pl.ds(low + 1, 1), :] + cond * edges[side, here]
                ) / guarded(diag)
                second[side, here] = v2
                third[side, here] = v3
                sides_o[pl.ds(low + ROWS * side, 1), :] = v3
                sides_o[pl.ds(low + ROWS * side + 1, 1), :] = ref[pl.ds(low + 2, 1), :]
                sides_o[pl.ds(low + ROWS * side + 2, 1), :] = ref[pl.ds(low + 3, 1), :]

    total = inner[...]
    col = iota((LAYERS, width), 1)
    inside = (col >= REACH) & (col < width - REACH)
    for side in range(2):
        diag, cond, via = ends[4 + side], ends[6 + side], ends[10 + side]
        change = damping * cond * second[side] / guarded(diag)
        second[side] = change
        outer = (
            ends[3 * side]
            - diag * change
            + cond * third[side]
            + pltpu.roll(via, 1, 0) * pltpu.roll(change, 1, 0)
            + via * pltpu.roll(change, LAYERS - 1, 0)
        )
        next_in = ends[1 + side] + ends[8 + side] * change
        squares = jnp.where(inside, outer * outer + next_in * next_in, 0.0)
        for c in range(0, width, LANES):
            total = total + squares[:, c : c + LANES]
    for l in range(LAYERS):

        @pl.when(dirs[l] == 0)
        def _(l=l):
            for side in range(2):
                sides_o[pl.ds(slot[l] * 4 + ROWS * side + 3, 1), :] = second[side, l : l + 1]

    _, _, squares = strips(dirs, gy % 2 == 0, even, own, gya, gyb, ma, mb)
    for r in range(0, 2 * STRIP, 8):
        total = total + squares[r : r + 8]
    sum_o[...] = jnp.full(sum_o.shape, jnp.sum(total), jnp.float32)


def place(ref, strip):
    width = ref.shape[2]
    lane = iota((1, 1, LANES), 2)
    ref[:, :, :LANES] = jnp.where(lane < REACH, strip, ref[:, :, :LANES])
    ref[:, :, width - LANES :] = jnp.where(lane >= LANES - REACH, strip, ref[:, :, width - LANES :])


def stress_steps(
    total_x, total_y, dirs, cond, early, sides, stress, mob, blk, gxa, gxb, own, gya, gyb, ma, mb,
    volts_o, stress_o, ext_c, ext_m, ext_v, ext_s,
):
    gx, gy = position()
    even = gx % 2 == 0
    width = early.shape[2]
    slot = slots_of(dirs)

    def near(right, row):
        a, b = gxa[pl.ds(row, 1), :], gxb[pl.ds(row, 1), :]
        return jnp.where(even, a, b) if right else jnp.where(even, b, a)

    for ref in (ext_c, ext_m, ext_v, ext_s):
        ref[0:8] = jnp.zeros((8, width), jnp.float32)
        ref[24:32] = jnp.zeros((8, width), jnp.float32)

    for l in range(LAYERS):

        @pl.when(dirs[l] == 0)
        def _(l=l):
            base, low = slot[l] * EDGE, slot[l] * 4
            for i in range(3):
                ext_v[7 - i : 8 - i] = sides[pl.ds(low + i, 1), :]
                ext_v[24 + i : 25 + i] = sides[pl.ds(low + ROWS + i, 1), :]
                for ref, first in ((ext_c, 0), (ext_m, 3), (ext_s, 6)):
                    ref[5 + i : 6 + i] = near(False, base + first + i)
                    ref[24 + i : 25 + i] = near(True, base + first + i)
            ext_v[8:24] = early[l]
            ext_v[8:9] = early[l, :1] + sides[pl.ds(low + 3, 1), :]
            ext_v[23:24] = early[l, ROWS - 1 :] + sides[pl.ds(low + ROWS + 3, 1), :]
            volts_o[l] = ext_v[8:24]
            ext_c[8:24] = cond[l]
            ext_m[8:24] = mob[l] * (1.0 - blk[l].astype(jnp.float32)) * inner_x(gx, total_x, (ROWS, width))
            ext_s[8:24] = stress[l]
            n = 32
            step = min(256, width)
            for start in range(0, width, step):
                lanes = slice(start, start + step)
                v, m, s = ext_v[:, lanes], ext_m[:, lanes], ext_s[:, lanes]
                wind = m * wind_factor * (ext_c[:, lanes] * (v - pltpu.roll(v, n - 1, 0)))
                for _ in range(STEPS):
                    flux = m * (pltpu.roll(s, n - 1, 0) - s) + wind
                    s = s + flux - pltpu.roll(flux, 1, 0)
                stress_o[l, :, lanes] = s[8:24]

        @pl.when(dirs[l] == 1)
        def _(l=l):
            for at in blocks(width, True):
                v, s = early[(l, *at)], stress[(l, *at)]
                volts_o[(l, *at)] = v
                inner = inner_y(gy, total_y, (8, width))
                m = mob[(l, *at)] * (1.0 - blk[(l, *at)].astype(jnp.float32)) * inner
                wind = m * wind_factor * (cond[(l, *at)] * (v - pltpu.roll(v, width - 1, 1)))
                for _ in range(STEPS):
                    flux = m * (pltpu.roll(s, width - 1, 1) - s) + wind
                    s = s + flux - pltpu.roll(flux, 1, 1)
                stress_o[(l, *at)] = s

    strip_v, wind, _ = strips(dirs, gy % 2 == 0, even, own, gya, gyb, ma, mb)
    place(volts_o, turned(strip_v))
    place(stress_o, strip_stress(dirs, gy % 2 == 0, even, own, gya, gyb, ma, mb, wind))


def call(kernel, ins, outs, scratch=(), scalars=1, copies=0, cost=0):
    smem, vmem = pl.BlockSpec(memory_space=pltpu.SMEM), pl.BlockSpec(memory_space=pltpu.VMEM)
    held = pl.BlockSpec(memory_space=pltpu.HBM) if copies else vmem
    scratch = [pltpu.VMEM(*(s if isinstance(s[0], tuple) else (s, jnp.float32))) for s in scratch]
    return pl.pallas_call(
        kernel,
        out_shape=[jax.ShapeDtypeStruct(s, jnp.float32) for s in outs],
        in_specs=[smem] * scalars + [held] * (len(ins) - scalars),
        out_specs=[vmem] * len(outs),
        scratch_shapes=scratch + ([pltpu.SemaphoreType.DMA((copies,))] if copies else []),
        compiler_params=pltpu.CompilerParams(vmem_limit_bytes=(57 if copies else 16) * 2**20),
        cost_estimate=pl.CostEstimate(flops=cost, bytes_accessed=cost, transcendentals=0),
    )(*ins)


def swap(value, axes, first):
    count = lax.axis_size(axes)
    pairs = [(i, i + 1) for i in range(first, count - 1, 2)]
    return lax.ppermute(value, axes, pairs + [(b, a) for a, b in pairs])


def partial_sum(held, out):
    total = held[0]
    for i in range(1, held.shape[0]):
        total = total + held[i]
    for i in range(out.shape[0]):
        out[i] = total


def root_mean(count, held, out):
    total = jnp.sum(held[...][:, :1, :1])
    out[...] = jnp.sqrt(jnp.full((1, LANES), total / count, jnp.float32))


def rms_all(held, count):
    got = lax.all_to_all(held, NEAR, 0, 0)
    (held,) = call(partial_sum, (got,), [(lax.axis_size(FAR), 1, LANES)], scalars=0)
    got = lax.all_to_all(held, FAR, 0, 0)
    (out,) = call(functools.partial(root_mean, count), (got,), [(1, LANES)], scalars=0)
    return out[0, 0]


def body(volts_start, seg_cond, via_cond, via_mask, pad_mask, load_current, stress_start, mobility, blocked, layer_dirs):
    layers, rows, width = seg_cond.shape
    total_x, total_y = rows * lax.axis_size(X), width * lax.axis_size(Y)
    shape = (layers, rows, width)
    fields = (volts_start, seg_cond, via_cond, via_mask, pad_mask, load_current, stress_start, mobility, blocked)
    column = (FIELDS, REACH, LANES)
    own, gya, gyb = call(
        functools.partial(pack_columns, total_x, total_y, width),
        (layer_dirs, *fields),
        [(2, FIELDS, OWN, LANES), column, column],
        scratch=[(a.shape[:-1] + (LANES,), a.dtype) for a in fields for _ in range(2)],
        copies=18,
    )
    gyb, gya = swap(gyb, Y, 1), swap(gya, Y, 0)
    own, fields = lax.optimization_barrier((own, fields))
    gxa, gxb = call(
        functools.partial(pack_rows, total_x),
        (layer_dirs, *fields),
        [(SLOTS * EDGE, width)] * 2,
        cost=COST_ROWS,
    )
    sent_a, sent_b = gxa, gxb
    gxa, gxb = swap(gxa, X, 0), swap(gxb, X, 1)
    side = (SENT, LANES)
    sa, sb = call(pack_strips, (own, gyb, gya), [side, side], scalars=0, cost=COST_STRIPS)
    message = (SENT + ROWS * (width // LANES), LANES)
    cond, prior_y, via, diag_y, rate, first = call(
        functools.partial(conductances, total_x, total_y),
        (layer_dirs, sent_a, sent_b, *fields[:6]),
        [shape, shape, (layers - 1, rows, width), shape, shape, shape],
        cost=COST_SETUP,
    )
    prior_x, diag_x, early, edges, ma, mb = call(
        early_sweeps,
        (layer_dirs, cond, prior_y, via, diag_y, rate, first, fields[0], *fields[4:6], gxa, gxb, sa, sb),
        [shape, shape, shape, (2, layers, width), message, message],
        scratch=[shape, shape, shape, (2, SLOTS, width), (ROWS, width), (ROWS, width)],
        cost=COST_EARLY,
    )
    ma, mb = swap(ma, X, 0), swap(mb, X, 1)
    inner, ends = call(
        inner_residuals,
        (layer_dirs, cond, prior_x, prior_y, via, diag_x, diag_y, *fields[4:6], early),
        [(8, LANES), (12, layers, width)],
        cost=COST_SETUP,
    )
    held, sides = call(
        last_sweep,
        (layer_dirs, inner, ends, edges, gxa, gxb, own, gya, gyb, ma, mb),
        [(lax.axis_size(NEAR), 1, LANES), (2 * ROWS, width)],
        scratch=[(ROWS, width), (ROWS, width), (2, layers, width), (2, layers, width)],
    )
    volts, stress = call(
        functools.partial(stress_steps, total_x, total_y),
        (layer_dirs, cond, early, sides, *fields[6:], gxa, gxb, own, gya, gyb, ma, mb),
        [shape, shape],
        scratch=[(32, width)] * 4,
        cost=12 * 2**20,
    )
    resid_rms = rms_all(held, layers * total_x * total_y)
    return volts, stress, resid_rms


def solution(mesh):
    gx, gy = mesh.shape["gx"], mesh.shape["gy"]
    fine = jax.sharding.Mesh(mesh.devices.reshape(gx // 4, 4, gy // 4, 2, 2), X + Y)
    cells, plane = P(None, X, Y), P(X, Y)
    in_specs = (cells, cells, cells, cells, plane, plane, cells, cells, cells, P())
    return jax.shard_map(body, mesh=fine, in_specs=in_specs, out_specs=(cells, cells, P()), check_vma=False)
```

```python
import functools

import jax
import jax.numpy as jnp
from jax import lax
from jax.experimental import pallas as pl
from jax.experimental.pallas import tpu as pltpu
from jax.sharding import PartitionSpec as P

SWEEPS = 3
STEPS = 3
LAYERS = 8
ROWS = 16
LANES = 128
REACH = 8
OWN = 16
STRIP = REACH + OWN
SLOTS = 4
EDGE = 12
FIELDS = 6

COST_ROWS = 2**20
COST_STRIPS = 4000 * 2**20
COST_EARLY = 1024
COST_SETUP = 4 * 2**20

damping = 0.8
pad_conductance = 4.0
supply_volts = 1.0
wind_factor = 4.0

X = ("z_lo", "x")
Y = ("y", "z_hi", "core")
NEAR = ("x", "y", "core")
FAR = ("z_hi", "z_lo")


def position():
    out = []
    for axes in (X, Y):
        at = lax.axis_index(axes[0])
        for a in axes[1:]:
            at = at * lax.axis_size(a) + lax.axis_index(a)
        out.append(at)
    return out


def iota(shape, dim):
    return lax.broadcasted_iota(jnp.int32, shape, dim)


def lane_dirs(dirs, shape):
    layer = iota(shape, len(shape) - 1) // ROWS
    found = jnp.zeros(shape, jnp.int32)
    for l in range(LAYERS):
        found = jnp.where(layer == l, dirs[l], found)
    return found == 1


def slots_of(dirs):
    slot, count = [], jnp.int32(0)
    for l in range(LAYERS):
        slot.append(count)
        count = count + (1 - dirs[l])
    return slot


def fetch(sources, targets, sems):
    copies = [pltpu.make_async_copy(a, b, sems.at[i]) for i, (a, b) in enumerate(zip(sources, targets))]
    for copy in copies:
        copy.start(priority=1)
    return copies


def pack_columns(total_x, total_y, width, dirs, *refs):
    given, (own_ref, a_ref, b_ref), ins, sems = refs[:9], refs[9:12], refs[12:30], refs[30]
    parts = []
    for ref in given:
        for lanes in (slice(0, LANES), slice(width - LANES, width)):
            parts.append(ref.at[(slice(None),) * (len(ref.shape) - 1) + (lanes,)])
    copies = fetch(parts, ins, sems)
    gx, gy = position()
    col = iota((1, 1, LANES), 2)

    def pick(i):
        for copy in copies[2 * i : 2 * i + 2]:
            copy.wait()
        first, last = ins[2 * i][...], ins[2 * i + 1][...]
        return jnp.where(col.reshape((1,) * (first.ndim - 1) + (LANES,)) < LANES // 2, first, last)

    def field(f):
        if f < 2:
            return pick(f)
        if f == 2:
            return jnp.concatenate([pick(2) * pick(3).astype(jnp.float32), none], 0)
        if f == 3:
            top, load = pad_conductance * pick(4).astype(jnp.float32), pick(5)
            return jnp.concatenate([load[None]] + [none] * (LAYERS - 2) + [top[None]], 0)
        if f == 4:
            return pick(6)
        return pick(7) * (1.0 - pick(8).astype(jnp.float32))

    none = jnp.zeros((1, ROWS, LANES), jnp.float32)
    shape = (OWN, LANES)
    along_y = lane_dirs(dirs, shape)
    x = gx * ROWS + iota(shape, 1) % ROWS
    even = gy % 2 == 0
    for f in range(FIELDS):
        turned = field(f).reshape(LANES, LANES).T
        pieces = []
        for side, start in enumerate((0, LANES - OWN)):
            piece = turned[start : start + OWN]
            if f in (1, 5):
                y = gy * width + (0 if side == 0 else width - OWN) + iota(shape, 0)
                inner = jnp.where(along_y, y, x) < jnp.where(along_y, total_y - 1, total_x - 1)
                piece = jnp.where(inner, piece, 0.0)
            own_ref[side, f] = piece
            pieces.append(piece)
        left, right = pieces[0][:REACH], pieces[1][OWN - REACH :]
        a_ref[f] = jnp.where(even, right, left)
        b_ref[f] = jnp.where(even, left, right)


def inner_x(gx, total_x, shape):
    return (gx * ROWS + iota(shape, 0) < total_x - 1).astype(jnp.float32)


def inner_y(gy, total_y, shape):
    return (gy * shape[1] + iota(shape, 1) < total_y - 1).astype(jnp.float32)


def pack_rows(total_x, dirs, volts, seg, via_cond, via_mask, pad, load, stress, mob, blk, a_ref, b_ref):
    gx, _ = position()
    even = gx % 2 == 0
    width = volts.shape[2]
    inner = inner_x(gx, total_x, (ROWS, width))
    slot = slots_of(dirs)
    for l in range(LAYERS):

        @pl.when(dirs[l] == 0)
        def _(l=l):
            cond = seg[l] * inner
            mobile = mob[l] * (1.0 - blk[l].astype(jnp.float32)) * inner
            held, s = volts[l], stress[l]
            out = []
            for edge in (ROWS - 1, 0):
                here = slice(edge, edge + 1)
                num = jnp.zeros((1, width), jnp.float32)
                diag = cond[here]
                if edge:
                    num = cond[edge - 1 : edge] * held[edge - 1 : edge]
                    diag = diag + cond[edge - 1 : edge]
                else:
                    num = cond[here] * held[1:2]
                if l > 0:
                    below = via_cond[l - 1, here] * via_mask[l - 1, here].astype(jnp.float32)
                    num, diag = num + below * volts[l - 1, here], diag + below
                if l < LAYERS - 1:
                    above = via_cond[l, here] * via_mask[l, here].astype(jnp.float32)
                    num, diag = num + above * volts[l + 1, here], diag + above
                if l == LAYERS - 1:
                    top = pad_conductance * pad[here].astype(jnp.float32)
                    num, diag = num + top * supply_volts, diag + top
                if l == 0:
                    num = num - load[here]
                three = slice(ROWS - 3, ROWS) if edge else slice(0, 3)
                out.append([cond[three], mobile[three], s[three], held[here], num, diag])
            base = slot[l] * EDGE
            at = 0
            for right, left in zip(*out):
                for i in range(right.shape[0]):
                    row = slice(i, i + 1)
                    a_ref[pl.ds(base + at, 1), :] = jnp.where(even, right[row], left[row])
                    b_ref[pl.ds(base + at, 1), :] = jnp.where(even, left[row], right[row])
                    at += 1


def guarded(diag):
    return jnp.where(diag == 0.0, 1.0, diag)


def blocks(width, along_y):
    if along_y:
        return [(slice(r, r + 8), slice(0, width)) for r in range(0, ROWS, 8)]
    step = min(512, width)
    return [(slice(0, ROWS), slice(c, c + step)) for c in range(0, width, step)]


def rest_of(l, at, v, via, pad, load):
    total = None
    if l > 0:
        total = via[(l - 1, *at)] * v[(l - 1, *at)]
    if l < LAYERS - 1:
        above = via[(l, *at)] * v[(l + 1, *at)]
        total = above if total is None else total + above
    if l == LAYERS - 1:
        total = total + pad_conductance * supply_volts * pad[at].astype(jnp.float32)
    if l == 0:
        total = total - load[at]
    return total


def shifted(value, dim, before, after):
    n = value.shape[dim]
    prior, later = pltpu.roll(value, 1, dim), pltpu.roll(value, n - 1, dim)
    if dim == 0:
        row = iota(value.shape, 0)
        if before is not None:
            prior = jnp.where(row == 0, before, prior)
            later = jnp.where(row == n - 1, after, later)
    return prior, later


def strip_pair(recv_a, recv_b, even, own, f):
    from_right = jnp.where(even, recv_a[f], recv_b[f])
    from_left = jnp.where(even, recv_b[f], recv_a[f])
    return (
        jnp.concatenate([from_left, own[0, f]], 0),
        jnp.concatenate([own[1, f], from_right], 0),
    )


def conductances(
    total_x, total_y, dirs, after_a, after_b, volts, seg, via_cond, via_mask, pad, load,
    cond_o, prior_o, via_o, diag_o, rate_o, volts_o,
):
    gx, gy = position()
    width = seg.shape[2]
    for l in range(LAYERS):
        if l < LAYERS - 1:
            via_o[l] = via_cond[l] * via_mask[l].astype(jnp.float32)

        @pl.when(dirs[l] == 0)
        def _(l=l):
            cond = seg[l] * inner_x(gx, total_x, (ROWS, width))
            cond_o[l] = cond
            prior_o[l] = shifted(cond, 0, 0.0, 0.0)[0]

        @pl.when(dirs[l] == 1)
        def _(l=l):
            cond = seg[l] * inner_y(gy, total_y, (ROWS, width))
            cond_o[l] = cond
            prior_o[l] = pltpu.roll(cond, 1, 1)

    for l in range(LAYERS):
        diag = cond_o[l] + prior_o[l]
        if l > 0:
            diag = diag + via_o[l - 1]
        if l < LAYERS - 1:
            diag = diag + via_o[l]
        else:
            diag = diag + pad_conductance * pad[...].astype(jnp.float32)
        diag_o[l] = diag
        rate_o[l] = damping / guarded(diag)

    for l in range(LAYERS):
        for along_y in (False, True):

            @pl.when(dirs[l] == int(along_y))
            def _(l=l, along_y=along_y):
                for at in blocks(width, along_y):
                    v = volts[(l, *at)]
                    prior, later = shifted(v, int(along_y), 0.0, 0.0)
                    num = prior_o[(l, *at)] * prior + cond_o[(l, *at)] * later + rest_of(l, at, volts, via_o, pad, load)
                    volts_o[(l, *at)] = (1.0 - damping) * v + rate_o[(l, *at)] * num


def early_sweeps(
    dirs, cond_o, prior_i, via_o, diag_i, rate_i, first_v, volts, pad, load, gxa, gxb, strips_a, strips_b,
    prior_o, diag_o, volts_o, edges_o, a_ref, b_ref, rate_o, one, two, halo, to_right, to_left,
):
    gx, gy = position()
    even = gx % 2 == 0
    width = volts.shape[2]
    slot = slots_of(dirs)

    def near(right, row, lanes=slice(None)):
        a, b = gxa[pl.ds(row, 1), lanes], gxb[pl.ds(row, 1), lanes]
        return jnp.where(even, a, b) if right else jnp.where(even, b, a)

    for l in range(LAYERS):

        one[l] = first_v[l]

        @pl.when(dirs[l] == 0)
        def _(l=l):
            base = slot[l] * EDGE
            before, after, cond_left = near(False, base + 9), near(True, base + 9), near(False, base + 2)
            v, last = volts[l], cond_o[l, ROWS - 1 :]
            prior_o[l], diag_o[l], rate_o[l] = prior_i[l], diag_i[l], rate_i[l]
            prior_o[l, :1] = cond_left
            diag = diag_i[l, :1] + cond_left
            diag_o[l, :1] = diag
            rate = damping / guarded(diag)
            rate_o[l, :1] = rate
            end = (slice(0, 1), slice(None))
            num = cond_left * before + cond_o[l, :1] * v[1:2] + rest_of(l, end, volts, via_o, pad, load)
            one[l, :1] = (1.0 - damping) * v[:1] + rate * num
            one[l, ROWS - 1 :] = first_v[l, ROWS - 1 :] + rate_i[l, ROWS - 1 :] * last * after
            halo[0, pl.ds(slot[l], 1), :] = (1.0 - damping) * before + damping * (
                near(False, base + 10) + cond_left * v[:1]
            ) / guarded(near(False, base + 11))
            halo[1, pl.ds(slot[l], 1), :] = (1.0 - damping) * after + damping * (
                near(True, base + 10) + last * v[ROWS - 1 :]
            ) / guarded(near(True, base + 11) + last)

    for sweep, (old, new) in ((1, (one, two)), (2, (two, volts_o))):
        for l in range(LAYERS):

            @pl.when(dirs[l] == 0)
            def _(l=l):
                for at in blocks(width, False):
                    lanes = at[1]
                    v = old[(l, *at)]
                    if sweep == 1:
                        before, after = halo[0, pl.ds(slot[l], 1), lanes], halo[1, pl.ds(slot[l], 1), lanes]
                    else:
                        before = after = 0.0
                    prior, later = shifted(v, 0, before, after)
                    num = prior_o[(l, *at)] * prior + cond_o[(l, *at)] * later + rest_of(l, at, old, via_o, pad, load)
                    result = (1.0 - damping) * v + rate_o[(l, *at)] * num
                    new[(l, *at)] = result
                    if sweep == 2:
                        edges_o[0, l : l + 1, lanes] = v[:1]
                        edges_o[1, l : l + 1, lanes] = v[ROWS - 1 :]
                        send = slot[l] * 4
                        for ref, e, d in ((to_right, ROWS - 1, -1), (to_left, 0, 1)):
                            ref[pl.ds(send, 1), lanes] = v[e : e + 1]
                            ref[pl.ds(send + 1, 1), lanes] = num[e : e + 1]
                            ref[pl.ds(send + 2, 1), lanes] = result[e + d : e + d + 1]
                            ref[pl.ds(send + 3, 1), lanes] = result[e + 2 * d : e + 2 * d + 1]

            @pl.when(dirs[l] == 1)
            def _(l=l):
                for at in blocks(width, True):
                    v = old[(l, *at)]
                    prior, later = shifted(v, 1, None, None)
                    num = prior_i[(l, *at)] * prior + cond_o[(l, *at)] * later + rest_of(l, at, old, via_o, pad, load)
                    new[(l, *at)] = (1.0 - damping) * v + rate_i[(l, *at)] * num
                    if sweep == 2:
                        edges_o[:, l : l + 1, :] = jnp.zeros((2, 1, width), jnp.float32)

    a_ref[: SENT] = strips_a[...]
    b_ref[: SENT] = strips_b[...]
    for j in range(width // LANES):
        start = SENT + j * ROWS
        lanes = slice(j * LANES, (j + 1) * LANES)
        a_ref[start : start + ROWS] = jnp.where(even, to_right[:, lanes], to_left[:, lanes])
        b_ref[start : start + ROWS] = jnp.where(even, to_left[:, lanes], to_right[:, lanes])


def strip_rows(f):
    if f < 4:
        return slice(f * STRIP, (f + 1) * STRIP), slice(0, STRIP)
    start = 4 * STRIP + (f - 4) * REACH
    return slice(start, start + REACH), slice(REACH, 2 * REACH)


SENT = strip_rows(FIELDS - 1)[0].stop


def pack_strips(own, gyb, gya, a_ref, b_ref):
    gx, gy = position()
    even = gx % 2 == 0
    x = iota((STRIP, LANES), 1) % ROWS
    for f in range(FIELDS):
        left, right = strip_pair(gya, gyb, gy % 2 == 0, own, f)
        right_going = jnp.where(x >= 8, left, pltpu.roll(right, LANES - 8, 1))
        left_going = jnp.where(x < 8, left, pltpu.roll(right, 8, 1))
        to, rows = strip_rows(f)
        a_ref[to] = jnp.where(even, right_going, left_going)[rows]
        b_ref[to] = jnp.where(even, left_going, right_going)[rows]


def strip_field(f, even_y, even_x, own, gya, gyb, ma, mb):
    x = iota((STRIP, LANES), 1) % ROWS
    left, right = strip_pair(gya, gyb, even_y, own, f)
    at, rows = strip_rows(f)
    a, b = ma[at], mb[at]
    if rows.start:
        none = jnp.zeros((REACH, LANES), jnp.float32)
        a, b = jnp.concatenate([none, a, none], 0), jnp.concatenate([none, b, none], 0)
    from_right, from_left = jnp.where(even_x, a, b), jnp.where(even_x, b, a)
    far_left = jnp.where(x >= 8, from_left, from_right)
    far_right = jnp.where(x >= 8, pltpu.roll(from_left, 8, 1), pltpu.roll(from_right, LANES - 8, 1))
    return jnp.concatenate([left, right], 0), jnp.concatenate([far_left, far_right], 0)


def strip_shifts(dirs):
    tall = (2 * STRIP, LANES)
    along_y = lane_dirs(dirs, tall)
    x = iota(tall, 1) % ROWS

    def later(pair):
        o, h = pair
        out = []
        for this, other in ((o, h), (h, o)):
            across = jnp.where(x == ROWS - 1, pltpu.roll(other, ROWS - 1, 1), pltpu.roll(this, LANES - 1, 1))
            out.append(jnp.where(along_y, pltpu.roll(this, tall[0] - 1, 0), across))
        return out

    def prior(pair):
        o, h = pair
        out = []
        for this, other in ((o, h), (h, o)):
            across = jnp.where(x == 0, pltpu.roll(other, LANES - ROWS + 1, 1), pltpu.roll(this, 1, 1))
            out.append(jnp.where(along_y, pltpu.roll(this, 1, 0), across))
        return out

    return prior, later


def strips(dirs, even_y, even_x, own, gya, gyb, ma, mb):
    tall = (2 * STRIP, LANES)
    layer = iota(tall, 1) // ROWS
    prior, later = strip_shifts(dirs)
    volts, cond, via, ends, mobile = (
        strip_field(f, even_y, even_x, own, gya, gyb, ma, mb) for f in (0, 1, 2, 3, 5)
    )
    via_below = [pltpu.roll(a, ROWS, 1) for a in via]
    top = [jnp.where(layer == LAYERS - 1, a, 0.0) for a in ends]
    load = [jnp.where(layer == 0, a, 0.0) for a in ends]
    cond_prior = prior(cond)
    diag = [guarded(p + c + vb + va + t) for p, c, vb, va, t in zip(cond_prior, cond, via_below, via, top)]
    rate = [damping / d for d in diag]

    def inflow(v):
        before, after = prior(v), later(v)
        return [
            cond_prior[i] * before[i]
            + cond[i] * after[i]
            + via_below[i] * pltpu.roll(v[i], ROWS, 1)
            + via[i] * pltpu.roll(v[i], LANES - ROWS, 1)
            + top[i] * supply_volts
            - load[i]
            for i in range(2)
        ]

    for _ in range(SWEEPS):
        num = inflow(volts)
        volts = [(1.0 - damping) * v + r * n for v, r, n in zip(volts, rate, num)]
    resid = inflow(volts)[0] - diag[0] * volts[0]
    sub = iota(tall, 0)
    inside = ((sub >= REACH) & (sub < 2 * REACH)) | ((sub >= STRIP + REACH) & (sub < STRIP + 2 * REACH))
    squares = jnp.where(inside, resid * resid, 0.0)
    after = later(volts)
    wind = [mobile[i] * wind_factor * (cond[i] * (volts[i] - after[i])) for i in range(2)]
    return volts[0], wind, squares


def strip_stress(dirs, even_y, even_x, own, gya, gyb, ma, mb, wind):
    stress, mobile = (strip_field(f, even_y, even_x, own, gya, gyb, ma, mb) for f in (4, 5))
    prior, later = strip_shifts(dirs)
    for _ in range(STEPS):
        after = later(stress)
        flux = [mobile[i] * (after[i] - stress[i]) + wind[i] for i in range(2)]
        back = prior(flux)
        stress = [stress[i] + flux[i] - back[i] for i in range(2)]
    return turned(stress[0])


def turned(value):
    middle = jnp.zeros((LANES - 2 * OWN, LANES), jnp.float32)
    whole = jnp.concatenate([value[REACH:STRIP], middle, value[STRIP : STRIP + OWN]], 0)
    return whole.T.reshape(LAYERS, ROWS, LANES)


def inner_residuals(
    dirs, cond, prior_x, prior_y, via, diag_x, diag_y, pad, load, early, sum_o, ends_o,
):
    width = early.shape[2]
    sum_o[...] = jnp.zeros_like(sum_o)
    for l in range(LAYERS):

        def add(along_y, prior, diag, l=l):
            for at in blocks(width, along_y):
                v = early[(l, *at)]
                first, second = shifted(v, int(along_y), 0.0, 0.0)
                resid = (
                    prior[(l, *at)] * first
                    + cond[(l, *at)] * second
                    + rest_of(l, at, early, via, pad, load)
                    - diag[(l, *at)] * v
                )
                row, col = at[0].start + iota(v.shape, 0), at[1].start + iota(v.shape, 1)
                inside = (col >= REACH) & (col < width - REACH) & (row >= 2) & (row < ROWS - 2)
                squares = jnp.where(inside, resid * resid, 0.0)
                total = jnp.zeros((8, LANES), jnp.float32)
                for r in range(0, v.shape[0], 8):
                    for c in range(0, v.shape[1], LANES):
                        total = total + squares[r : r + 8, c : c + LANES]
                sum_o[...] += total
                for i, r in enumerate((0, 1, ROWS - 2, ROWS - 1)):
                    if at[0].start <= r < at[0].stop:
                        ends_o[i, l : l + 1, at[1]] = resid[r - at[0].start : r - at[0].start + 1]

        here = slice(l, l + 1)
        if l < LAYERS - 1:
            ends_o[10, here], ends_o[11, here] = via[l, :1], via[l, ROWS - 1 :]
        else:
            ends_o[10, here] = ends_o[11, here] = jnp.zeros((1, width), jnp.float32)

        @pl.when(dirs[l] == 0)
        def _(l=l, add=add, here=here):
            add(False, prior_x, diag_x)
            ends_o[4, here], ends_o[5, here] = diag_x[l, :1], diag_x[l, ROWS - 1 :]
            ends_o[6, here], ends_o[7, here] = prior_x[l, :1], cond[l, ROWS - 1 :]
            ends_o[8, here], ends_o[9, here] = cond[l, :1], cond[l, ROWS - 2 : ROWS - 1]

        @pl.when(dirs[l] == 1)
        def _(l=l, add=add, here=here):
            add(True, prior_y, diag_y)
            ends_o[4, here], ends_o[5, here] = diag_y[l, :1], diag_y[l, ROWS - 1 :]
            for i in range(6, 10):
                ends_o[i, here] = jnp.zeros((1, width), jnp.float32)


def last_sweep(
    dirs, inner, ends, edges, gxa, gxb, own, gya, gyb, ma, mb,
    sum_o, sides_o, near_left, near_right, second, third,
):
    gx, gy = position()
    even = gx % 2 == 0
    width = ends.shape[2]
    slot = slots_of(dirs)

    def near(right, row):
        a, b = gxa[pl.ds(row, 1), :], gxb[pl.ds(row, 1), :]
        return jnp.where(even, a, b) if right else jnp.where(even, b, a)

    for j in range(width // LANES):
        start = SENT + j * ROWS
        lanes = slice(j * LANES, (j + 1) * LANES)
        a, b = ma[start : start + ROWS], mb[start : start + ROWS]
        near_right[:, lanes] = jnp.where(even, a, b)
        near_left[:, lanes] = jnp.where(even, b, a)
    second[...] = jnp.zeros_like(second)
    third[...] = jnp.zeros_like(third)
    for l in range(LAYERS):

        @pl.when(dirs[l] == 0)
        def _(l=l):
            base, low = slot[l] * EDGE, slot[l] * 4
            for side, ref in enumerate((near_left, near_right)):
                here = slice(l, l + 1)
                v2 = ref[pl.ds(low, 1), :]
                cond = ends[6 + side, here]
                diag = near(bool(side), base + 11)
                if side:
                    diag = diag + cond
                v3 = (1.0 - damping) * v2 + damping * (
                    ref[pl.ds(low + 1, 1), :] + cond * edges[side, here]
                ) / guarded(diag)
                second[side, here] = v2
                third[side, here] = v3
                sides_o[pl.ds(low + ROWS * side, 1), :] = v3
                sides_o[pl.ds(low + ROWS * side + 1, 1), :] = ref[pl.ds(low + 2, 1), :]
                sides_o[pl.ds(low + ROWS * side + 2, 1), :] = ref[pl.ds(low + 3, 1), :]

    total = inner[...]
    col = iota((LAYERS, width), 1)
    inside = (col >= REACH) & (col < width - REACH)
    for side in range(2):
        diag, cond, via = ends[4 + side], ends[6 + side], ends[10 + side]
        change = damping * cond * second[side] / guarded(diag)
        second[side] = change
        outer = (
            ends[3 * side]
            - diag * change
            + cond * third[side]
            + pltpu.roll(via, 1, 0) * pltpu.roll(change, 1, 0)
            + via * pltpu.roll(change, LAYERS - 1, 0)
        )
        next_in = ends[1 + side] + ends[8 + side] * change
        squares = jnp.where(inside, outer * outer + next_in * next_in, 0.0)
        for c in range(0, width, LANES):
            total = total + squares[:, c : c + LANES]
    for l in range(LAYERS):

        @pl.when(dirs[l] == 0)
        def _(l=l):
            for side in range(2):
                sides_o[pl.ds(slot[l] * 4 + ROWS * side + 3, 1), :] = second[side, l : l + 1]

    _, _, squares = strips(dirs, gy % 2 == 0, even, own, gya, gyb, ma, mb)
    for r in range(0, 2 * STRIP, 8):
        total = total + squares[r : r + 8]
    sum_o[...] = jnp.full(sum_o.shape, jnp.sum(total), jnp.float32)


def place(ref, strip):
    width = ref.shape[2]
    lane = iota((1, 1, LANES), 2)
    ref[:, :, :LANES] = jnp.where(lane < REACH, strip, ref[:, :, :LANES])
    ref[:, :, width - LANES :] = jnp.where(lane >= LANES - REACH, strip, ref[:, :, width - LANES :])


def stress_steps(
    total_x, total_y, dirs, cond, early, sides, stress, mob, blk, gxa, gxb, own, gya, gyb, ma, mb,
    volts_o, stress_o, ext_c, ext_m, ext_v, ext_s,
):
    gx, gy = position()
    even = gx % 2 == 0
    width = early.shape[2]
    slot = slots_of(dirs)

    def near(right, row):
        a, b = gxa[pl.ds(row, 1), :], gxb[pl.ds(row, 1), :]
        return jnp.where(even, a, b) if right else jnp.where(even, b, a)

    for ref in (ext_c, ext_m, ext_v, ext_s):
        ref[0:8] = jnp.zeros((8, width), jnp.float32)
        ref[24:32] = jnp.zeros((8, width), jnp.float32)

    for l in range(LAYERS):

        @pl.when(dirs[l] == 0)
        def _(l=l):
            base, low = slot[l] * EDGE, slot[l] * 4
            for i in range(3):
                ext_v[7 - i : 8 - i] = sides[pl.ds(low + i, 1), :]
                ext_v[24 + i : 25 + i] = sides[pl.ds(low + ROWS + i, 1), :]
                for ref, first in ((ext_c, 0), (ext_m, 3), (ext_s, 6)):
                    ref[5 + i : 6 + i] = near(False, base + first + i)
                    ref[24 + i : 25 + i] = near(True, base + first + i)
            ext_v[8:24] = early[l]
            ext_v[8:9] = early[l, :1] + sides[pl.ds(low + 3, 1), :]
            ext_v[23:24] = early[l, ROWS - 1 :] + sides[pl.ds(low + ROWS + 3, 1), :]
            volts_o[l] = ext_v[8:24]
            ext_c[8:24] = cond[l]
            ext_m[8:24] = mob[l] * (1.0 - blk[l].astype(jnp.float32)) * inner_x(gx, total_x, (ROWS, width))
            ext_s[8:24] = stress[l]
            n = 32
            step = min(256, width)
            for start in range(0, width, step):
                lanes = slice(start, start + step)
                v, m, s = ext_v[:, lanes], ext_m[:, lanes], ext_s[:, lanes]
                wind = m * wind_factor * (ext_c[:, lanes] * (v - pltpu.roll(v, n - 1, 0)))
                for _ in range(STEPS):
                    flux = m * (pltpu.roll(s, n - 1, 0) - s) + wind
                    s = s + flux - pltpu.roll(flux, 1, 0)
                stress_o[l, :, lanes] = s[8:24]

        @pl.when(dirs[l] == 1)
        def _(l=l):
            for at in blocks(width, True):
                v, s = early[(l, *at)], stress[(l, *at)]
                volts_o[(l, *at)] = v
                inner = inner_y(gy, total_y, (8, width))
                m = mob[(l, *at)] * (1.0 - blk[(l, *at)].astype(jnp.float32)) * inner
                wind = m * wind_factor * (cond[(l, *at)] * (v - pltpu.roll(v, width - 1, 1)))
                for _ in range(STEPS):
                    flux = m * (pltpu.roll(s, width - 1, 1) - s) + wind
                    s = s + flux - pltpu.roll(flux, 1, 1)
                stress_o[(l, *at)] = s

    strip_v, wind, _ = strips(dirs, gy % 2 == 0, even, own, gya, gyb, ma, mb)
    place(volts_o, turned(strip_v))
    place(stress_o, strip_stress(dirs, gy % 2 == 0, even, own, gya, gyb, ma, mb, wind))


def call(kernel, ins, outs, scratch=(), scalars=1, copies=0, cost=0):
    smem, vmem = pl.BlockSpec(memory_space=pltpu.SMEM), pl.BlockSpec(memory_space=pltpu.VMEM)
    held = pl.BlockSpec(memory_space=pltpu.HBM) if copies else vmem
    scratch = [pltpu.VMEM(*(s if isinstance(s[0], tuple) else (s, jnp.float32))) for s in scratch]
    return pl.pallas_call(
        kernel,
        out_shape=[jax.ShapeDtypeStruct(s, jnp.float32) for s in outs],
        in_specs=[smem] * scalars + [held] * (len(ins) - scalars),
        out_specs=[vmem] * len(outs),
        scratch_shapes=scratch + ([pltpu.SemaphoreType.DMA((copies,))] if copies else []),
        compiler_params=pltpu.CompilerParams(vmem_limit_bytes=(57 if copies else 16) * 2**20),
        cost_estimate=pl.CostEstimate(flops=cost, bytes_accessed=cost, transcendentals=0),
    )(*ins)


def swap(value, axes, first):
    count = lax.axis_size(axes)
    pairs = [(i, i + 1) for i in range(first, count - 1, 2)]
    return lax.ppermute(value, axes, pairs + [(b, a) for a, b in pairs])


def partial_sum(held, out):
    total = held[0]
    for i in range(1, held.shape[0]):
        total = total + held[i]
    for i in range(out.shape[0]):
        out[i] = total


def root_mean(count, held, out):
    total = jnp.sum(held[...][:, :1, :1])
    out[...] = jnp.sqrt(jnp.full((1, LANES), total / count, jnp.float32))


def rms_all(held, count):
    got = lax.all_to_all(held, NEAR, 0, 0)
    (held,) = call(partial_sum, (got,), [(lax.axis_size(FAR), 1, LANES)], scalars=0)
    got = lax.all_to_all(held, FAR, 0, 0)
    (out,) = call(functools.partial(root_mean, count), (got,), [(1, LANES)], scalars=0)
    return out[0, 0]


def body(volts_start, seg_cond, via_cond, via_mask, pad_mask, load_current, stress_start, mobility, blocked, layer_dirs):
    layers, rows, width = seg_cond.shape
    total_x, total_y = rows * lax.axis_size(X), width * lax.axis_size(Y)
    shape = (layers, rows, width)
    fields = (volts_start, seg_cond, via_cond, via_mask, pad_mask, load_current, stress_start, mobility, blocked)
    column = (FIELDS, REACH, LANES)
    own, gya, gyb = call(
        functools.partial(pack_columns, total_x, total_y, width),
        (layer_dirs, *fields),
        [(2, FIELDS, OWN, LANES), column, column],
        scratch=[(a.shape[:-1] + (LANES,), a.dtype) for a in fields for _ in range(2)],
        copies=18,
    )
    gyb, gya = swap(gyb, Y, 1), swap(gya, Y, 0)
    own, fields = lax.optimization_barrier((own, fields))
    gxa, gxb = call(
        functools.partial(pack_rows, total_x),
        (layer_dirs, *fields),
        [(SLOTS * EDGE, width)] * 2,
        cost=COST_ROWS,
    )
    sent_a, sent_b = gxa, gxb
    gxa, gxb = swap(gxa, X, 0), swap(gxb, X, 1)
    side = (SENT, LANES)
    sa, sb = call(pack_strips, (own, gyb, gya), [side, side], scalars=0, cost=COST_STRIPS)
    message = (SENT + ROWS * (width // LANES), LANES)
    cond, prior_y, via, diag_y, rate, first = call(
        functools.partial(conductances, total_x, total_y),
        (layer_dirs, sent_a, sent_b, *fields[:6]),
        [shape, shape, (layers - 1, rows, width), shape, shape, shape],
        cost=COST_SETUP,
    )
    prior_x, diag_x, early, edges, ma, mb = call(
        early_sweeps,
        (layer_dirs, cond, prior_y, via, diag_y, rate, first, fields[0], *fields[4:6], gxa, gxb, sa, sb),
        [shape, shape, shape, (2, layers, width), message, message],
        scratch=[shape, shape, shape, (2, SLOTS, width), (ROWS, width), (ROWS, width)],
        cost=COST_EARLY,
    )
    ma, mb = swap(ma, X, 0), swap(mb, X, 1)
    inner, ends = call(
        inner_residuals,
        (layer_dirs, cond, prior_x, prior_y, via, diag_x, diag_y, *fields[4:6], early),
        [(8, LANES), (12, layers, width)],
        cost=COST_SETUP,
    )
    held, sides = call(
        last_sweep,
        (layer_dirs, inner, ends, edges, gxa, gxb, own, gya, gyb, ma, mb),
        [(lax.axis_size(NEAR), 1, LANES), (2 * ROWS, width)],
        scratch=[(ROWS, width), (ROWS, width), (2, layers, width), (2, layers, width)],
    )
    volts, stress = call(
        functools.partial(stress_steps, total_x, total_y),
        (layer_dirs, cond, early, sides, *fields[6:], gxa, gxb, own, gya, gyb, ma, mb),
        [shape, shape],
        scratch=[(32, width)] * 4,
        cost=12 * 2**20,
    )
    resid_rms = rms_all(held, layers * total_x * total_y)
    return volts, stress, resid_rms


def solution(mesh):
    gx, gy = mesh.shape["gx"], mesh.shape["gy"]
    fine = jax.sharding.Mesh(mesh.devices.reshape(gx // 4, 4, gy // 4, 2, 2), X + Y)
    cells, plane = P(None, X, Y), P(X, Y)
    in_specs = (cells, cells, cells, cells, plane, plane, cells, cells, cells, P())
    return jax.shard_map(body, mesh=fine, in_specs=in_specs, out_specs=(cells, cells, P()), check_vma=False)
```

```python
import functools

import jax
import jax.numpy as jnp
from jax import lax
from jax.experimental import pallas as pl
from jax.experimental.pallas import tpu as pltpu
from jax.sharding import PartitionSpec as P

SWEEPS = 3
STEPS = 3
LAYERS = 8
ROWS = 16
LANES = 128
REACH = 8
OWN = 16
STRIP = REACH + OWN
SLOTS = 4
EDGE = 12
FIELDS = 6

COST_ROWS = 2**20
COST_STRIPS = 4000 * 2**20
COST_EARLY = 1024
COST_SETUP = 4 * 2**20

damping = 0.8
pad_conductance = 4.0
supply_volts = 1.0
wind_factor = 4.0

X = ("z_lo", "x")
Y = ("y", "z_hi", "core")
NEAR = ("x", "y", "core")
FAR = ("z_lo", "z_hi")


def position():
    out = []
    for axes in (X, Y):
        at = lax.axis_index(axes[0])
        for a in axes[1:]:
            at = at * lax.axis_size(a) + lax.axis_index(a)
        out.append(at)
    return out


def iota(shape, dim):
    return lax.broadcasted_iota(jnp.int32, shape, dim)


def lane_dirs(dirs, shape):
    layer = iota(shape, len(shape) - 1) // ROWS
    found = jnp.zeros(shape, jnp.int32)
    for l in range(LAYERS):
        found = jnp.where(layer == l, dirs[l], found)
    return found == 1


def slots_of(dirs):
    slot, count = [], jnp.int32(0)
    for l in range(LAYERS):
        slot.append(count)
        count = count + (1 - dirs[l])
    return slot


def fetch(sources, targets, sems):
    copies = [pltpu.make_async_copy(a, b, sems.at[i]) for i, (a, b) in enumerate(zip(sources, targets))]
    for copy in copies:
        copy.start(priority=1)
    return copies


def pack_columns(total_x, total_y, width, dirs, *refs):
    given, (own_ref, a_ref, b_ref), ins, sems = refs[:9], refs[9:12], refs[12:30], refs[30]
    parts = []
    for ref in given:
        for lanes in (slice(0, LANES), slice(width - LANES, width)):
            parts.append(ref.at[(slice(None),) * (len(ref.shape) - 1) + (lanes,)])
    copies = fetch(parts, ins, sems)
    gx, gy = position()
    col = iota((1, 1, LANES), 2)

    def pick(i):
        for copy in copies[2 * i : 2 * i + 2]:
            copy.wait()
        first, last = ins[2 * i][...], ins[2 * i + 1][...]
        return jnp.where(col.reshape((1,) * (first.ndim - 1) + (LANES,)) < LANES // 2, first, last)

    def field(f):
        if f < 2:
            return pick(f)
        if f == 2:
            return jnp.concatenate([pick(2) * pick(3).astype(jnp.float32), none], 0)
        if f == 3:
            top, load = pad_conductance * pick(4).astype(jnp.float32), pick(5)
            return jnp.concatenate([load[None]] + [none] * (LAYERS - 2) + [top[None]], 0)
        if f == 4:
            return pick(6)
        return pick(7) * (1.0 - pick(8).astype(jnp.float32))

    none = jnp.zeros((1, ROWS, LANES), jnp.float32)
    shape = (OWN, LANES)
    along_y = lane_dirs(dirs, shape)
    x = gx * ROWS + iota(shape, 1) % ROWS
    even = gy % 2 == 0
    for f in range(FIELDS):
        turned = field(f).reshape(LANES, LANES).T
        pieces = []
        for side, start in enumerate((0, LANES - OWN)):
            piece = turned[start : start + OWN]
            if f in (1, 5):
                y = gy * width + (0 if side == 0 else width - OWN) + iota(shape, 0)
                inner = jnp.where(along_y, y, x) < jnp.where(along_y, total_y - 1, total_x - 1)
                piece = jnp.where(inner, piece, 0.0)
            own_ref[side, f] = piece
            pieces.append(piece)
        left, right = pieces[0][:REACH], pieces[1][OWN - REACH :]
        a_ref[f] = jnp.where(even, right, left)
        b_ref[f] = jnp.where(even, left, right)


def inner_x(gx, total_x, shape):
    return (gx * ROWS + iota(shape, 0) < total_x - 1).astype(jnp.float32)


def inner_y(gy, total_y, shape):
    return (gy * shape[1] + iota(shape, 1) < total_y - 1).astype(jnp.float32)


def pack_rows(total_x, dirs, volts, seg, via_cond, via_mask, pad, load, stress, mob, blk, a_ref, b_ref):
    gx, _ = position()
    even = gx % 2 == 0
    width = volts.shape[2]
    inner = inner_x(gx, total_x, (ROWS, width))
    slot = slots_of(dirs)
    for l in range(LAYERS):

        @pl.when(dirs[l] == 0)
        def _(l=l):
            cond = seg[l] * inner
            mobile = mob[l] * (1.0 - blk[l].astype(jnp.float32)) * inner
            held, s = volts[l], stress[l]
            out = []
            for edge in (ROWS - 1, 0):
                here = slice(edge, edge + 1)
                num = jnp.zeros((1, width), jnp.float32)
                diag = cond[here]
                if edge:
                    num = cond[edge - 1 : edge] * held[edge - 1 : edge]
                    diag = diag + cond[edge - 1 : edge]
                else:
                    num = cond[here] * held[1:2]
                if l > 0:
                    below = via_cond[l - 1, here] * via_mask[l - 1, here].astype(jnp.float32)
                    num, diag = num + below * volts[l - 1, here], diag + below
                if l < LAYERS - 1:
                    above = via_cond[l, here] * via_mask[l, here].astype(jnp.float32)
                    num, diag = num + above * volts[l + 1, here], diag + above
                if l == LAYERS - 1:
                    top = pad_conductance * pad[here].astype(jnp.float32)
                    num, diag = num + top * supply_volts, diag + top
                if l == 0:
                    num = num - load[here]
                three = slice(ROWS - 3, ROWS) if edge else slice(0, 3)
                out.append([cond[three], mobile[three], s[three], held[here], num, diag])
            base = slot[l] * EDGE
            at = 0
            for right, left in zip(*out):
                for i in range(right.shape[0]):
                    row = slice(i, i + 1)
                    a_ref[pl.ds(base + at, 1), :] = jnp.where(even, right[row], left[row])
                    b_ref[pl.ds(base + at, 1), :] = jnp.where(even, left[row], right[row])
                    at += 1


def guarded(diag):
    return jnp.where(diag == 0.0, 1.0, diag)


def blocks(width, along_y):
    if along_y:
        return [(slice(r, r + 8), slice(0, width)) for r in range(0, ROWS, 8)]
    step = min(512, width)
    return [(slice(0, ROWS), slice(c, c + step)) for c in range(0, width, step)]


def rest_of(l, at, v, via, pad, load):
    total = None
    if l > 0:
        total = via[(l - 1, *at)] * v[(l - 1, *at)]
    if l < LAYERS - 1:
        above = via[(l, *at)] * v[(l + 1, *at)]
        total = above if total is None else total + above
    if l == LAYERS - 1:
        total = total + pad_conductance * supply_volts * pad[at].astype(jnp.float32)
    if l == 0:
        total = total - load[at]
    return total


def shifted(value, dim, before, after):
    n = value.shape[dim]
    prior, later = pltpu.roll(value, 1, dim), pltpu.roll(value, n - 1, dim)
    if dim == 0:
        row = iota(value.shape, 0)
        if before is not None:
            prior = jnp.where(row == 0, before, prior)
            later = jnp.where(row == n - 1, after, later)
    return prior, later


def strip_pair(recv_a, recv_b, even, own, f):
    from_right = jnp.where(even, recv_a[f], recv_b[f])
    from_left = jnp.where(even, recv_b[f], recv_a[f])
    return (
        jnp.concatenate([from_left, own[0, f]], 0),
        jnp.concatenate([own[1, f], from_right], 0),
    )


def conductances(
    total_x, total_y, dirs, after_a, after_b, volts, seg, via_cond, via_mask, pad, load,
    cond_o, prior_o, via_o, diag_o, rate_o, volts_o,
):
    gx, gy = position()
    width = seg.shape[2]
    for l in range(LAYERS):
        if l < LAYERS - 1:
            via_o[l] = via_cond[l] * via_mask[l].astype(jnp.float32)

        @pl.when(dirs[l] == 0)
        def _(l=l):
            cond = seg[l] * inner_x(gx, total_x, (ROWS, width))
            cond_o[l] = cond
            prior_o[l] = shifted(cond, 0, 0.0, 0.0)[0]

        @pl.when(dirs[l] == 1)
        def _(l=l):
            cond = seg[l] * inner_y(gy, total_y, (ROWS, width))
            cond_o[l] = cond
            prior_o[l] = pltpu.roll(cond, 1, 1)

    for l in range(LAYERS):
        diag = cond_o[l] + prior_o[l]
        if l > 0:
            diag = diag + via_o[l - 1]
        if l < LAYERS - 1:
            diag = diag + via_o[l]
        else:
            diag = diag + pad_conductance * pad[...].astype(jnp.float32)
        diag_o[l] = diag
        rate_o[l] = damping / guarded(diag)

    for l in range(LAYERS):
        for along_y in (False, True):

            @pl.when(dirs[l] == int(along_y))
            def _(l=l, along_y=along_y):
                for at in blocks(width, along_y):
                    v = volts[(l, *at)]
                    prior, later = shifted(v, int(along_y), 0.0, 0.0)
                    num = prior_o[(l, *at)] * prior + cond_o[(l, *at)] * later + rest_of(l, at, volts, via_o, pad, load)
                    volts_o[(l, *at)] = (1.0 - damping) * v + rate_o[(l, *at)] * num


def early_sweeps(
    dirs, cond_o, prior_i, via_o, diag_i, rate_i, first_v, volts, pad, load, gxa, gxb, strips_a, strips_b,
    prior_o, diag_o, volts_o, edges_o, a_ref, b_ref, rate_o, one, two, halo, to_right, to_left,
):
    gx, gy = position()
    even = gx % 2 == 0
    width = volts.shape[2]
    slot = slots_of(dirs)

    def near(right, row, lanes=slice(None)):
        a, b = gxa[pl.ds(row, 1), lanes], gxb[pl.ds(row, 1), lanes]
        return jnp.where(even, a, b) if right else jnp.where(even, b, a)

    for l in range(LAYERS):

        one[l] = first_v[l]

        @pl.when(dirs[l] == 0)
        def _(l=l):
            base = slot[l] * EDGE
            before, after, cond_left = near(False, base + 9), near(True, base + 9), near(False, base + 2)
            v, last = volts[l], cond_o[l, ROWS - 1 :]
            prior_o[l], diag_o[l], rate_o[l] = prior_i[l], diag_i[l], rate_i[l]
            prior_o[l, :1] = cond_left
            diag = diag_i[l, :1] + cond_left
            diag_o[l, :1] = diag
            rate = damping / guarded(diag)
            rate_o[l, :1] = rate
            end = (slice(0, 1), slice(None))
            num = cond_left * before + cond_o[l, :1] * v[1:2] + rest_of(l, end, volts, via_o, pad, load)
            one[l, :1] = (1.0 - damping) * v[:1] + rate * num
            one[l, ROWS - 1 :] = first_v[l, ROWS - 1 :] + rate_i[l, ROWS - 1 :] * last * after
            halo[0, pl.ds(slot[l], 1), :] = (1.0 - damping) * before + damping * (
                near(False, base + 10) + cond_left * v[:1]
            ) / guarded(near(False, base + 11))
            halo[1, pl.ds(slot[l], 1), :] = (1.0 - damping) * after + damping * (
                near(True, base + 10) + last * v[ROWS - 1 :]
            ) / guarded(near(True, base + 11) + last)

    for sweep, (old, new) in ((1, (one, two)), (2, (two, volts_o))):
        for l in range(LAYERS):

            @pl.when(dirs[l] == 0)
            def _(l=l):
                for at in blocks(width, False):
                    lanes = at[1]
                    v = old[(l, *at)]
                    if sweep == 1:
                        before, after = halo[0, pl.ds(slot[l], 1), lanes], halo[1, pl.ds(slot[l], 1), lanes]
                    else:
                        before = after = 0.0
                    prior, later = shifted(v, 0, before, after)
                    num = prior_o[(l, *at)] * prior + cond_o[(l, *at)] * later + rest_of(l, at, old, via_o, pad, load)
                    result = (1.0 - damping) * v + rate_o[(l, *at)] * num
                    new[(l, *at)] = result
                    if sweep == 2:
                        edges_o[0, l : l + 1, lanes] = v[:1]
                        edges_o[1, l : l + 1, lanes] = v[ROWS - 1 :]
                        send = slot[l] * 4
                        for ref, e, d in ((to_right, ROWS - 1, -1), (to_left, 0, 1)):
                            ref[pl.ds(send, 1), lanes] = v[e : e + 1]
                            ref[pl.ds(send + 1, 1), lanes] = num[e : e + 1]
                            ref[pl.ds(send + 2, 1), lanes] = result[e + d : e + d + 1]
                            ref[pl.ds(send + 3, 1), lanes] = result[e + 2 * d : e + 2 * d + 1]

            @pl.when(dirs[l] == 1)
            def _(l=l):
                for at in blocks(width, True):
                    v = old[(l, *at)]
                    prior, later = shifted(v, 1, None, None)
                    num = prior_i[(l, *at)] * prior + cond_o[(l, *at)] * later + rest_of(l, at, old, via_o, pad, load)
                    new[(l, *at)] = (1.0 - damping) * v + rate_i[(l, *at)] * num
                    if sweep == 2:
                        edges_o[:, l : l + 1, :] = jnp.zeros((2, 1, width), jnp.float32)

    a_ref[: SENT] = strips_a[...]
    b_ref[: SENT] = strips_b[...]
    for j in range(width // LANES):
        start = SENT + j * ROWS
        lanes = slice(j * LANES, (j + 1) * LANES)
        a_ref[start : start + ROWS] = jnp.where(even, to_right[:, lanes], to_left[:, lanes])
        b_ref[start : start + ROWS] = jnp.where(even, to_left[:, lanes], to_right[:, lanes])


def strip_rows(f):
    if f < 4:
        return slice(f * STRIP, (f + 1) * STRIP), slice(0, STRIP)
    start = 4 * STRIP + (f - 4) * REACH
    return slice(start, start + REACH), slice(REACH, 2 * REACH)


SENT = strip_rows(FIELDS - 1)[0].stop


def pack_strips(own, gyb, gya, a_ref, b_ref):
    gx, gy = position()
    even = gx % 2 == 0
    x = iota((STRIP, LANES), 1) % ROWS
    for f in range(FIELDS):
        left, right = strip_pair(gya, gyb, gy % 2 == 0, own, f)
        right_going = jnp.where(x >= 8, left, pltpu.roll(right, LANES - 8, 1))
        left_going = jnp.where(x < 8, left, pltpu.roll(right, 8, 1))
        to, rows = strip_rows(f)
        a_ref[to] = jnp.where(even, right_going, left_going)[rows]
        b_ref[to] = jnp.where(even, left_going, right_going)[rows]


def strip_field(f, even_y, even_x, own, gya, gyb, ma, mb):
    x = iota((STRIP, LANES), 1) % ROWS
    left, right = strip_pair(gya, gyb, even_y, own, f)
    at, rows = strip_rows(f)
    a, b = ma[at], mb[at]
    if rows.start:
        none = jnp.zeros((REACH, LANES), jnp.float32)
        a, b = jnp.concatenate([none, a, none], 0), jnp.concatenate([none, b, none], 0)
    from_right, from_left = jnp.where(even_x, a, b), jnp.where(even_x, b, a)
    far_left = jnp.where(x >= 8, from_left, from_right)
    far_right = jnp.where(x >= 8, pltpu.roll(from_left, 8, 1), pltpu.roll(from_right, LANES - 8, 1))
    return jnp.concatenate([left, right], 0), jnp.concatenate([far_left, far_right], 0)


def strip_shifts(dirs):
    tall = (2 * STRIP, LANES)
    along_y = lane_dirs(dirs, tall)
    x = iota(tall, 1) % ROWS

    def later(pair):
        o, h = pair
        out = []
        for this, other in ((o, h), (h, o)):
            across = jnp.where(x == ROWS - 1, pltpu.roll(other, ROWS - 1, 1), pltpu.roll(this, LANES - 1, 1))
            out.append(jnp.where(along_y, pltpu.roll(this, tall[0] - 1, 0), across))
        return out

    def prior(pair):
        o, h = pair
        out = []
        for this, other in ((o, h), (h, o)):
            across = jnp.where(x == 0, pltpu.roll(other, LANES - ROWS + 1, 1), pltpu.roll(this, 1, 1))
            out.append(jnp.where(along_y, pltpu.roll(this, 1, 0), across))
        return out

    return prior, later


def strips(dirs, even_y, even_x, own, gya, gyb, ma, mb):
    tall = (2 * STRIP, LANES)
    layer = iota(tall, 1) // ROWS
    prior, later = strip_shifts(dirs)
    volts, cond, via, ends, mobile = (
        strip_field(f, even_y, even_x, own, gya, gyb, ma, mb) for f in (0, 1, 2, 3, 5)
    )
    via_below = [pltpu.roll(a, ROWS, 1) for a in via]
    top = [jnp.where(layer == LAYERS - 1, a, 0.0) for a in ends]
    load = [jnp.where(layer == 0, a, 0.0) for a in ends]
    cond_prior = prior(cond)
    diag = [guarded(p + c + vb + va + t) for p, c, vb, va, t in zip(cond_prior, cond, via_below, via, top)]
    rate = [damping / d for d in diag]

    def inflow(v):
        before, after = prior(v), later(v)
        return [
            cond_prior[i] * before[i]
            + cond[i] * after[i]
            + via_below[i] * pltpu.roll(v[i], ROWS, 1)
            + via[i] * pltpu.roll(v[i], LANES - ROWS, 1)
            + top[i] * supply_volts
            - load[i]
            for i in range(2)
        ]

    for _ in range(SWEEPS):
        num = inflow(volts)
        volts = [(1.0 - damping) * v + r * n for v, r, n in zip(volts, rate, num)]
    resid = inflow(volts)[0] - diag[0] * volts[0]
    sub = iota(tall, 0)
    inside = ((sub >= REACH) & (sub < 2 * REACH)) | ((sub >= STRIP + REACH) & (sub < STRIP + 2 * REACH))
    squares = jnp.where(inside, resid * resid, 0.0)
    after = later(volts)
    wind = [mobile[i] * wind_factor * (cond[i] * (volts[i] - after[i])) for i in range(2)]
    return volts[0], wind, squares


def strip_stress(dirs, even_y, even_x, own, gya, gyb, ma, mb, wind):
    stress, mobile = (strip_field(f, even_y, even_x, own, gya, gyb, ma, mb) for f in (4, 5))
    prior, later = strip_shifts(dirs)
    for _ in range(STEPS):
        after = later(stress)
        flux = [mobile[i] * (after[i] - stress[i]) + wind[i] for i in range(2)]
        back = prior(flux)
        stress = [stress[i] + flux[i] - back[i] for i in range(2)]
    return turned(stress[0])


def turned(value):
    middle = jnp.zeros((LANES - 2 * OWN, LANES), jnp.float32)
    whole = jnp.concatenate([value[REACH:STRIP], middle, value[STRIP : STRIP + OWN]], 0)
    return whole.T.reshape(LAYERS, ROWS, LANES)


def inner_residuals(
    dirs, cond, prior_x, prior_y, via, diag_x, diag_y, pad, load, early, sum_o, ends_o,
):
    width = early.shape[2]
    sum_o[...] = jnp.zeros_like(sum_o)
    for l in range(LAYERS):

        def add(along_y, prior, diag, l=l):
            for at in blocks(width, along_y):
                v = early[(l, *at)]
                first, second = shifted(v, int(along_y), 0.0, 0.0)
                resid = (
                    prior[(l, *at)] * first
                    + cond[(l, *at)] * second
                    + rest_of(l, at, early, via, pad, load)
                    - diag[(l, *at)] * v
                )
                row, col = at[0].start + iota(v.shape, 0), at[1].start + iota(v.shape, 1)
                inside = (col >= REACH) & (col < width - REACH) & (row >= 2) & (row < ROWS - 2)
                squares = jnp.where(inside, resid * resid, 0.0)
                total = jnp.zeros((8, LANES), jnp.float32)
                for r in range(0, v.shape[0], 8):
                    for c in range(0, v.shape[1], LANES):
                        total = total + squares[r : r + 8, c : c + LANES]
                sum_o[...] += total
                for i, r in enumerate((0, 1, ROWS - 2, ROWS - 1)):
                    if at[0].start <= r < at[0].stop:
                        ends_o[i, l : l + 1, at[1]] = resid[r - at[0].start : r - at[0].start + 1]

        here = slice(l, l + 1)
        if l < LAYERS - 1:
            ends_o[10, here], ends_o[11, here] = via[l, :1], via[l, ROWS - 1 :]
        else:
            ends_o[10, here] = ends_o[11, here] = jnp.zeros((1, width), jnp.float32)

        @pl.when(dirs[l] == 0)
        def _(l=l, add=add, here=here):
            add(False, prior_x, diag_x)
            ends_o[4, here], ends_o[5, here] = diag_x[l, :1], diag_x[l, ROWS - 1 :]
            ends_o[6, here], ends_o[7, here] = prior_x[l, :1], cond[l, ROWS - 1 :]
            ends_o[8, here], ends_o[9, here] = cond[l, :1], cond[l, ROWS - 2 : ROWS - 1]

        @pl.when(dirs[l] == 1)
        def _(l=l, add=add, here=here):
            add(True, prior_y, diag_y)
            ends_o[4, here], ends_o[5, here] = diag_y[l, :1], diag_y[l, ROWS - 1 :]
            for i in range(6, 10):
                ends_o[i, here] = jnp.zeros((1, width), jnp.float32)


def last_sweep(
    dirs, inner, ends, edges, gxa, gxb, own, gya, gyb, ma, mb,
    sum_o, sides_o, near_left, near_right, second, third,
):
    gx, gy = position()
    even = gx % 2 == 0
    width = ends.shape[2]
    slot = slots_of(dirs)

    def near(right, row):
        a, b = gxa[pl.ds(row, 1), :], gxb[pl.ds(row, 1), :]
        return jnp.where(even, a, b) if right else jnp.where(even, b, a)

    for j in range(width // LANES):
        start = SENT + j * ROWS
        lanes = slice(j * LANES, (j + 1) * LANES)
        a, b = ma[start : start + ROWS], mb[start : start + ROWS]
        near_right[:, lanes] = jnp.where(even, a, b)
        near_left[:, lanes] = jnp.where(even, b, a)
    second[...] = jnp.zeros_like(second)
    third[...] = jnp.zeros_like(third)
    for l in range(LAYERS):

        @pl.when(dirs[l] == 0)
        def _(l=l):
            base, low = slot[l] * EDGE, slot[l] * 4
            for side, ref in enumerate((near_left, near_right)):
                here = slice(l, l + 1)
                v2 = ref[pl.ds(low, 1), :]
                cond = ends[6 + side, here]
                diag = near(bool(side), base + 11)
                if side:
                    diag = diag + cond
                v3 = (1.0 - damping) * v2 + damping * (
                    ref[pl.ds(low + 1, 1), :] + cond * edges[side, here]
                ) / guarded(diag)
                second[side, here] = v2
                third[side, here] = v3
                sides_o[pl.ds(low + ROWS * side, 1), :] = v3
                sides_o[pl.ds(low + ROWS * side + 1, 1), :] = ref[pl.ds(low + 2, 1), :]
                sides_o[pl.ds(low + ROWS * side + 2, 1), :] = ref[pl.ds(low + 3, 1), :]

    total = inner[...]
    col = iota((LAYERS, width), 1)
    inside = (col >= REACH) & (col < width - REACH)
    for side in range(2):
        diag, cond, via = ends[4 + side], ends[6 + side], ends[10 + side]
        change = damping * cond * second[side] / guarded(diag)
        second[side] = change
        outer = (
            ends[3 * side]
            - diag * change
            + cond * third[side]
            + pltpu.roll(via, 1, 0) * pltpu.roll(change, 1, 0)
            + via * pltpu.roll(change, LAYERS - 1, 0)
        )
        next_in = ends[1 + side] + ends[8 + side] * change
        squares = jnp.where(inside, outer * outer + next_in * next_in, 0.0)
        for c in range(0, width, LANES):
            total = total + squares[:, c : c + LANES]
    for l in range(LAYERS):

        @pl.when(dirs[l] == 0)
        def _(l=l):
            for side in range(2):
                sides_o[pl.ds(slot[l] * 4 + ROWS * side + 3, 1), :] = second[side, l : l + 1]

    _, _, squares = strips(dirs, gy % 2 == 0, even, own, gya, gyb, ma, mb)
    for r in range(0, 2 * STRIP, 8):
        total = total + squares[r : r + 8]
    sum_o[...] = jnp.full(sum_o.shape, jnp.sum(total), jnp.float32)


def place(ref, strip):
    width = ref.shape[2]
    lane = iota((1, 1, LANES), 2)
    ref[:, :, :LANES] = jnp.where(lane < REACH, strip, ref[:, :, :LANES])
    ref[:, :, width - LANES :] = jnp.where(lane >= LANES - REACH, strip, ref[:, :, width - LANES :])


def stress_steps(
    total_x, total_y, dirs, cond, early, sides, stress, mob, blk, gxa, gxb, own, gya, gyb, ma, mb,
    volts_o, stress_o, ext_c, ext_m, ext_v, ext_s,
):
    gx, gy = position()
    even = gx % 2 == 0
    width = early.shape[2]
    slot = slots_of(dirs)

    def near(right, row):
        a, b = gxa[pl.ds(row, 1), :], gxb[pl.ds(row, 1), :]
        return jnp.where(even, a, b) if right else jnp.where(even, b, a)

    for ref in (ext_c, ext_m, ext_v, ext_s):
        ref[0:8] = jnp.zeros((8, width), jnp.float32)
        ref[24:32] = jnp.zeros((8, width), jnp.float32)

    for l in range(LAYERS):

        @pl.when(dirs[l] == 0)
        def _(l=l):
            base, low = slot[l] * EDGE, slot[l] * 4
            for i in range(3):
                ext_v[7 - i : 8 - i] = sides[pl.ds(low + i, 1), :]
                ext_v[24 + i : 25 + i] = sides[pl.ds(low + ROWS + i, 1), :]
                for ref, first in ((ext_c, 0), (ext_m, 3), (ext_s, 6)):
                    ref[5 + i : 6 + i] = near(False, base + first + i)
                    ref[24 + i : 25 + i] = near(True, base + first + i)
            ext_v[8:24] = early[l]
            ext_v[8:9] = early[l, :1] + sides[pl.ds(low + 3, 1), :]
            ext_v[23:24] = early[l, ROWS - 1 :] + sides[pl.ds(low + ROWS + 3, 1), :]
            volts_o[l] = ext_v[8:24]
            ext_c[8:24] = cond[l]
            ext_m[8:24] = mob[l] * (1.0 - blk[l].astype(jnp.float32)) * inner_x(gx, total_x, (ROWS, width))
            ext_s[8:24] = stress[l]
            n = 32
            step = min(256, width)
            for start in range(0, width, step):
                lanes = slice(start, start + step)
                v, m, s = ext_v[:, lanes], ext_m[:, lanes], ext_s[:, lanes]
                wind = m * wind_factor * (ext_c[:, lanes] * (v - pltpu.roll(v, n - 1, 0)))
                for _ in range(STEPS):
                    flux = m * (pltpu.roll(s, n - 1, 0) - s) + wind
                    s = s + flux - pltpu.roll(flux, 1, 0)
                stress_o[l, :, lanes] = s[8:24]

        @pl.when(dirs[l] == 1)
        def _(l=l):
            for at in blocks(width, True):
                v, s = early[(l, *at)], stress[(l, *at)]
                volts_o[(l, *at)] = v
                inner = inner_y(gy, total_y, (8, width))
                m = mob[(l, *at)] * (1.0 - blk[(l, *at)].astype(jnp.float32)) * inner
                wind = m * wind_factor * (cond[(l, *at)] * (v - pltpu.roll(v, width - 1, 1)))
                for _ in range(STEPS):
                    flux = m * (pltpu.roll(s, width - 1, 1) - s) + wind
                    s = s + flux - pltpu.roll(flux, 1, 1)
                stress_o[(l, *at)] = s

    strip_v, wind, _ = strips(dirs, gy % 2 == 0, even, own, gya, gyb, ma, mb)
    place(volts_o, turned(strip_v))
    place(stress_o, strip_stress(dirs, gy % 2 == 0, even, own, gya, gyb, ma, mb, wind))


def call(kernel, ins, outs, scratch=(), scalars=1, copies=0, cost=0):
    smem, vmem = pl.BlockSpec(memory_space=pltpu.SMEM), pl.BlockSpec(memory_space=pltpu.VMEM)
    held = pl.BlockSpec(memory_space=pltpu.HBM) if copies else vmem
    scratch = [pltpu.VMEM(*(s if isinstance(s[0], tuple) else (s, jnp.float32))) for s in scratch]
    return pl.pallas_call(
        kernel,
        out_shape=[jax.ShapeDtypeStruct(s, jnp.float32) for s in outs],
        in_specs=[smem] * scalars + [held] * (len(ins) - scalars),
        out_specs=[vmem] * len(outs),
        scratch_shapes=scratch + ([pltpu.SemaphoreType.DMA((copies,))] if copies else []),
        compiler_params=pltpu.CompilerParams(vmem_limit_bytes=(57 if copies else 16) * 2**20),
        cost_estimate=pl.CostEstimate(flops=cost, bytes_accessed=cost, transcendentals=0),
    )(*ins)


def swap(value, axes, first):
    count = lax.axis_size(axes)
    pairs = [(i, i + 1) for i in range(first, count - 1, 2)]
    return lax.ppermute(value, axes, pairs + [(b, a) for a, b in pairs])


def partial_sum(held, out):
    total = held[0]
    for i in range(1, held.shape[0]):
        total = total + held[i]
    for i in range(out.shape[0]):
        out[i] = total


def root_mean(count, held, out):
    total = jnp.sum(held[...][:, :1, :1])
    out[...] = jnp.sqrt(jnp.full((1, LANES), total / count, jnp.float32))


def rms_all(held, count):
    got = lax.all_to_all(held, NEAR, 0, 0)
    (held,) = call(partial_sum, (got,), [(lax.axis_size(FAR), 1, LANES)], scalars=0)
    got = lax.all_to_all(held, FAR, 0, 0)
    (out,) = call(functools.partial(root_mean, count), (got,), [(1, LANES)], scalars=0)
    return out[0, 0]


def body(volts_start, seg_cond, via_cond, via_mask, pad_mask, load_current, stress_start, mobility, blocked, layer_dirs):
    layers, rows, width = seg_cond.shape
    total_x, total_y = rows * lax.axis_size(X), width * lax.axis_size(Y)
    shape = (layers, rows, width)
    fields = (volts_start, seg_cond, via_cond, via_mask, pad_mask, load_current, stress_start, mobility, blocked)
    column = (FIELDS, REACH, LANES)
    own, gya, gyb = call(
        functools.partial(pack_columns, total_x, total_y, width),
        (layer_dirs, *fields),
        [(2, FIELDS, OWN, LANES), column, column],
        scratch=[(a.shape[:-1] + (LANES,), a.dtype) for a in fields for _ in range(2)],
        copies=18,
    )
    gyb, gya = swap(gyb, Y, 1), swap(gya, Y, 0)
    own, fields = lax.optimization_barrier((own, fields))
    gxa, gxb = call(
        functools.partial(pack_rows, total_x),
        (layer_dirs, *fields),
        [(SLOTS * EDGE, width)] * 2,
        cost=COST_ROWS,
    )
    sent_a, sent_b = gxa, gxb
    gxa, gxb = swap(gxa, X, 0), swap(gxb, X, 1)
    side = (SENT, LANES)
    sa, sb = call(pack_strips, (own, gyb, gya), [side, side], scalars=0, cost=COST_STRIPS)
    message = (SENT + ROWS * (width // LANES), LANES)
    cond, prior_y, via, diag_y, rate, first = call(
        functools.partial(conductances, total_x, total_y),
        (layer_dirs, sent_a, sent_b, *fields[:6]),
        [shape, shape, (layers - 1, rows, width), shape, shape, shape],
        cost=COST_SETUP,
    )
    prior_x, diag_x, early, edges, ma, mb = call(
        early_sweeps,
        (layer_dirs, cond, prior_y, via, diag_y, rate, first, fields[0], *fields[4:6], gxa, gxb, sa, sb),
        [shape, shape, shape, (2, layers, width), message, message],
        scratch=[shape, shape, shape, (2, SLOTS, width), (ROWS, width), (ROWS, width)],
        cost=COST_EARLY,
    )
    ma, mb = swap(ma, X, 0), swap(mb, X, 1)
    inner, ends = call(
        inner_residuals,
        (layer_dirs, cond, prior_x, prior_y, via, diag_x, diag_y, *fields[4:6], early),
        [(8, LANES), (12, layers, width)],
        cost=COST_SETUP,
    )
    held, sides = call(
        last_sweep,
        (layer_dirs, inner, ends, edges, gxa, gxb, own, gya, gyb, ma, mb),
        [(lax.axis_size(NEAR), 1, LANES), (2 * ROWS, width)],
        scratch=[(ROWS, width), (ROWS, width), (2, layers, width), (2, layers, width)],
    )
    volts, stress = call(
        functools.partial(stress_steps, total_x, total_y),
        (layer_dirs, cond, early, sides, *fields[6:], gxa, gxb, own, gya, gyb, ma, mb),
        [shape, shape],
        scratch=[(32, width)] * 4,
        cost=12 * 2**20,
    )
    resid_rms = rms_all(held, layers * total_x * total_y)
    return volts, stress, resid_rms


def solution(mesh):
    gx, gy = mesh.shape["gx"], mesh.shape["gy"]
    fine = jax.sharding.Mesh(mesh.devices.reshape(gx // 4, 4, gy // 4, 2, 2), X + Y)
    cells, plane = P(None, X, Y), P(X, Y)
    in_specs = (cells, cells, cells, cells, plane, plane, cells, cells, cells, P())
    return jax.shard_map(body, mesh=fine, in_specs=in_specs, out_specs=(cells, cells, P()), check_vma=False)
```
